256 devices in a mesh: ctx: 16 (over z, x_lo), tp: 16 (over x_hi, y, core).
Axes of the slice: x: 4 (x_hi: 2, x_lo: 2; x = x_hi * 2 + x_lo), y: 4, z: 8, core: 2. Of those that a mesh axis runs over, the one named last changes fastest.
Arguments:
- residual: bfloat16 [2048, 8192], P('ctx', 'tp'), may hold values from -17 to 17
- features: bfloat16 [2048, 3, 8192], P('ctx', None, 'tp'), may hold values from -5 to 5
- filters: float32 [2048, 8192], P('ctx', 'tp'), may hold values from -1.5 to 1.5
- skip_gain: float32 [8192], P('tp'), may hold values from 0.3 to 1.5
- w_out: bfloat16 [8192, 8192], P(None, 'tp'), may hold values from -0.0625 to 0.0625
- norm_gain: float32 [8192], P('tp'), may hold values from 0.25 to 1.75
- w_gate: bfloat16 [8192, 21888], P('tp', 'ctx'), may hold values from -0.0625 to 0.0625
- w_up: bfloat16 [8192, 21888], P('tp', 'ctx'), may hold values from -0.0625 to 0.0625
Outputs:
- stream: bfloat16 [2048, 8192], P('ctx', 'tp')
- hidden: bfloat16 [2048, 21888], P('tp', 'ctx')
The draws below stay inside these ranges and needn't reach their ends.
All inputs are finite; a program needn't handle non-finite values.
Results may differ from the reference program's by a relative error of at most 0.034.
Values may be sent and summed in bfloat16 or wider, within the bound.
No kernel may reach another device: no remote copies, remote signals or barrier semaphores. Data moves between devices by JAX's collectives and lax.ppermute only.
A program may use at most 128 MiB of HBM per device.

```python
import math
import jax
import jax.numpy as jnp
from jax import lax

D = 8192
FF = 21888
TOKENS = 2048
N_TP = 16


def draw_residual(key, part):
    key = jax.random.fold_in(key, 5)
    value_key, rough_key = jax.random.split(key)
    spread_log = math.log(3.0)
    position = jnp.arange(D, dtype=jnp.float32) / D
    rough = jax.random.uniform(rough_key, (D,), jnp.float32, 0.7, 1.4)
    column_scale = jnp.exp(spread_log * (position - 0.5)) * rough
    values = jax.random.truncated_normal(value_key, -4.0, 4.0, (TOKENS, D), jnp.float32)
    return (values * column_scale).astype(jnp.bfloat16)


def draw_filters(key, part):
    key = jax.random.fold_in(key, 11)
    rate_key, value_key = jax.random.split(key)
    lower_log = math.log(0.5 / TOKENS)
    upper_log = math.log(1.0 / 30.0)
    rates = jnp.exp(jax.random.uniform(rate_key, (D,), jnp.float32, lower_log, upper_log))
    lags = jnp.arange(TOKENS, dtype=jnp.float32)[:, None]
    norming = jnp.sqrt(2.0 * rates / (1.0 - jnp.exp(-2.0 * rates * TOKENS)))
    values = jax.random.truncated_normal(value_key, -4.0, 4.0, (TOKENS, D), jnp.float32)
    return values * jnp.exp(-rates * lags) * norming


def block_scale(rng, shape, shards, least, top_value):
    level = 1.0
    for axis_at, blocks in shards:
        draws = jax.random.uniform(jax.random.fold_in(jax.random.fold_in(rng, 6), axis_at), (blocks,), jnp.float32, least / len(shards), top_value / len(shards))
        level = level * jnp.repeat(jnp.exp(draws), shape[axis_at] // blocks).reshape((-1,) + (1,) * (len(shape) - 1 - axis_at))
    return level


def gaussian(own_key, extent, scale, most, pieces=(), held_as=jnp.bfloat16):
    entries = jax.random.normal(own_key, extent, jnp.float32) * scale
    if len(pieces) > 0:
        entries = block_scale(own_key, extent, pieces, -0.22, 0.18) * entries
    return jnp.clip(entries, min=-most, max=most).astype(held_as)


def setup_inputs(seed: int = 0) -> dict:
    arg_keys = jax.random.split(jax.random.key(seed), 9)
    return {
        "residual": draw_residual(jax.random.fold_in(arg_keys[8], 71), 0),
        "features": gaussian(arg_keys[1], (TOKENS, 3, D), 1.0, 5.0, ((0, 16), (2, 16))),
        "filters": draw_filters(jax.random.fold_in(arg_keys[8], 71), 0),
        "skip_gain": jnp.clip(0.3 + 1.2 * jax.random.uniform(arg_keys[3], (D,), jnp.float32) ** block_scale(arg_keys[3], (D,), ((0, 16),), -0.2, 0.2), 0.3, 1.5),
        "w_out": gaussian(arg_keys[4], (D, D), D ** -0.5, 0.0625, ((1, 16),)),
        "norm_gain": jnp.clip(1.0 + 0.15 * jax.random.normal(arg_keys[5], (D,), jnp.float32), 0.25, 1.75),
        "w_gate": gaussian(arg_keys[6], (D, FF), D ** -0.5, 0.0625, ((0, 16), (1, 16))),
        "w_up": gaussian(arg_keys[7], (D, FF), D ** -0.5, 0.0625, ((0, 16), (1, 16))),
    }


def block_partials(scaled, weight):
    width = D // N_TP

    def step(total, index):
        start = (index * width).astype(jnp.int32)
        rows = lax.dynamic_slice_in_dim(scaled, start, width, 1)
        cols = lax.dynamic_slice_in_dim(weight, start, width, 0)
        part = jnp.dot(rows, cols, preferred_element_type=jnp.float32).astype(jnp.bfloat16)
        return (total + part.astype(jnp.float32), None)
    start_total = jnp.zeros((scaled.shape[0], weight.shape[1]), jnp.float32)
    total, _ = lax.scan(step, start_total, jnp.arange(N_TP, dtype=jnp.int32))
    return total

def reference(residual, features, filters, skip_gain, w_out, norm_gain, w_gate, w_up):
    outer_gate = features[:, 0, :].astype(jnp.float32)
    product_kv = features[:, 1, :].astype(jnp.float32) * features[:, 2, :].astype(jnp.float32)
    length = 2 * TOKENS
    spectra = jnp.fft.rfft(product_kv, n=length, axis=0) * jnp.fft.rfft(filters, n=length, axis=0)
    long_conv = jnp.fft.irfft(spectra, n=length, axis=0)[:TOKENS].astype(jnp.float32)
    mixed = (outer_gate * (long_conv + skip_gain * product_kv)).astype(jnp.bfloat16)
    stream = (residual.astype(jnp.float32) + jnp.dot(mixed, w_out, preferred_element_type=jnp.float32)).astype(jnp.bfloat16)
    stream_f = stream.astype(jnp.float32)
    mean_sq = lax.optimization_barrier(jnp.mean(stream_f * stream_f, axis=1, keepdims=True))
    scaled = (stream_f * norm_gain).astype(jnp.bfloat16)
    row_scale = jax.lax.rsqrt(mean_sq + 1e-06)
    gate_vals = block_partials(scaled, w_gate) * row_scale
    up_vals = block_partials(scaled, w_up) * row_scale
    hidden = (jax.nn.silu(gate_vals) * up_vals).astype(jnp.bfloat16)
    return (stream, hidden)
```

```python
import math

import jax
import jax.numpy as jnp
import numpy as np
from jax import lax
from jax.experimental import pallas as pl
from jax.experimental.pallas import tpu as pltpu
from jax.sharding import PartitionSpec as P

F32 = jnp.float32
BF16 = jnp.bfloat16
AXES = ("ctx", "tp")
N_CTX = 16
N_TP = 16
ROWS = 128
CH = 512
SUB = 32
FF_LOC = 1368
FF_PAD = 1376
EPS = 1e-06
PLANE_GROUPS = [[xh * 8 + y * 2 + k for xh in range(2) for y in range(4)] for k in range(2)]


def split_index(i):
    c, t = divmod(i, N_TP)
    z, x_lo = divmod(c, 2)
    x_hi, r = divmod(t, 8)
    y, k = divmod(r, 2)
    return z, x_hi * 2 + x_lo, y, k


def join_index(z, x, y, k):
    x = x % 4
    return ((z % 8) * 2 + x % 2) * N_TP + (x // 2) * 8 + (y % 4) * 2 + k % 2


def shift(arr, z=0, x=0, y=0, k=0):
    pairs = []
    for i in range(N_CTX * N_TP):
        az, ax, ay, ak = split_index(i)
        pairs.append((i, join_index(az + z, ax + x, ay + y, ak + k)))
    return lax.ppermute(arr, AXES, pairs)


def split_bf16(table):
    high = np.asarray(table, np.float32).astype(jnp.bfloat16)
    low = (np.asarray(table, np.float32) - high.astype(np.float32)).astype(jnp.bfloat16)
    return high, low


def dft_tables():
    size = 2 * ROWS
    pos = np.arange(ROWS)
    freq = np.arange(ROWS)
    phase = (pos[:, None] * freq[None, :]) % size
    angle = 2.0 * math.pi / size * phase
    cos, sin = np.cos(angle), np.sin(angle)
    sign = np.where(pos % 2 == 0, 1.0, -1.0)
    fwd_im = -sin
    fwd_im[:, 0] = sign
    forward = np.concatenate([cos, fwd_im], axis=1)
    weight = np.where(freq == 0, 1.0, 2.0)[:, None] / size
    inv_re = cos.T * weight
    inv_im = -sin.T * weight
    inv_im[0, :] = sign / size
    inverse = np.concatenate([inv_re, inv_im], axis=0)
    return split_bf16(forward) + split_bf16(inverse)


def dot(a, b):
    return jnp.dot(a, b, preferred_element_type=F32)


def dot_nt(a, b):
    return lax.dot_general(a, b, (((1,), (1,)), ((), ())), preferred_element_type=F32)


def prep_kernel(feat_ref, filt_ref, out_ref):
    prod = feat_ref[1].astype(F32) * feat_ref[2].astype(F32)
    filt = filt_ref[...]
    for j in range(CH // 128):
        cols = slice(128 * j, 128 * j + 128)
        out_ref[4 * j : 4 * j + 4, 0:SUB, :] = prod[:, cols].T.astype(BF16).reshape(4, SUB, 128)
        out_ref[4 * j : 4 * j + 4, SUB : 2 * SUB, :] = (
            filt[:, cols].T.astype(BF16).reshape(4, SUB, 128)
        )


def conv_kernel(x_ref, fh_ref, fl_ref, gh_ref, gl_ref, out_ref, spec, filt, outs):
    x = x_ref[...].reshape(N_CTX * 2 * SUB, ROWS)
    spec[...] = (dot(x, fh_ref[...]) + dot(x, fl_ref[...])).reshape(N_CTX, 2 * SUB, 256)
    lane = lax.broadcasted_iota(jnp.int32, (SUB, 128), 1)
    sign = jnp.where(lane % 2 == 0, 1.0, -1.0).astype(F32)
    first = lane == 0
    for d in range(N_CTX):
        re = spec[d, SUB:, 0:128]
        im = spec[d, SUB:, 128:256]
        if d > 0:
            re = re + sign * spec[d - 1, SUB:, 0:128]
            im = im + sign * spec[d - 1, SUB:, 128:256]
        filt[d, 0] = re
        filt[d, 1] = jnp.where(first, 0.0, im)
        filt[d, 2] = jnp.where(first, im, re)
    for m in range(N_CTX):
        acc_re = jnp.zeros((SUB, 128), F32)
        acc_im = jnp.zeros((SUB, 128), F32)
        for n in range(m + 1):
            pr = spec[n, 0:SUB, 0:128]
            pi = spec[n, 0:SUB, 128:256]
            hr, hz, hq = filt[m - n, 0], filt[m - n, 1], filt[m - n, 2]
            acc_re = acc_re + (pr * hr - pi * hz)
            acc_im = acc_im + (pr * hz + pi * hq)
        outs[m, :, 0:128] = acc_re
        outs[m, :, 128:256] = acc_im
    total = outs[...].reshape(N_CTX * SUB, 256)
    high = total.astype(BF16)
    low = (total - high.astype(F32)).astype(BF16)
    y = dot(high, gh_ref[...]) + dot(high, gl_ref[...]) + dot(low, gh_ref[...])
    out_ref[...] = y.astype(BF16).reshape(N_CTX, SUB, ROWS)


def mix_kernel(conv_ref, feat_ref, skip_ref, out_ref):
    conv = conv_ref[...].reshape(CH, ROWS).astype(F32)
    for j in range(CH // 128):
        cols = slice(128 * j, 128 * j + 128)
        prod = feat_ref[1, :, cols].astype(F32) * feat_ref[2, :, cols].astype(F32)
        long = conv[cols, :].T
        gate = feat_ref[0, :, cols].astype(F32)
        out_ref[:, cols] = (gate * (long + skip_ref[:, cols] * prod)).astype(BF16)


def out_proj_kernel(mixed_ref, w_ref, res_ref, out_ref, acc):
    t = pl.program_id(0)

    @pl.when(t == 0)
    def _():
        acc[...] = res_ref[...].astype(F32)

    acc[...] += dot(mixed_ref[0], w_ref[...])

    @pl.when(t == pl.num_programs(0) - 1)
    def _():
        out_ref[...] = acc[...].astype(BF16)


def mlp_kernel(own_ref, oth_ref, gain_ref, wo_ref, wx_ref, out_ref, so, sx, aux):
    part = pl.program_id(1)

    @pl.when(part == 0)
    def _():
        own = own_ref[0].astype(F32)
        oth = oth_ref[0].astype(F32)
        so[...] = (own * gain_ref[0:1, :]).astype(BF16)
        sx[...] = (oth * gain_ref[1:2, :]).astype(BF16)
        ones = jnp.ones((8, CH), BF16)
        sq = own * own
        hi = sq.astype(BF16)
        total = dot_nt(ones, hi) + dot_nt(ones, (sq - hi.astype(F32)).astype(BF16))
        sq = oth * oth
        hi = sq.astype(BF16)
        total += dot_nt(ones, hi) + dot_nt(ones, (sq - hi.astype(F32)).astype(BF16))
        hi = total.astype(BF16).astype(F32)
        row = lax.broadcasted_iota(jnp.int32, (8, ROWS), 0)
        aux[...] = jnp.where(row == 0, hi, jnp.where(row == 1, total - hi, 0.0))

    res = dot_nt(wo_ref[0], so[...]) + dot_nt(wx_ref[0], sx[...])
    tail = jnp.where(part == 0, aux[...], jnp.zeros_like(aux))
    res = jnp.concatenate([res[:FF_LOC], res[FF_LOC:] + tail], axis=0)
    out_ref[0] = res.astype(BF16)


def finish_kernel(part_ref, out_ref):
    gate = part_ref[0:FF_PAD].astype(F32)
    up = part_ref[FF_PAD:].astype(F32)
    sums = gate[FF_LOC : FF_LOC + 1] + gate[FF_LOC + 1 : FF_LOC + 2]
    scale = lax.rsqrt(sums * (1.0 / (N_TP * CH)) + EPS)
    g = gate[:FF_LOC] * scale
    u = up[:FF_LOC] * scale
    out_ref[...] = (g / (1.0 + jnp.exp(-g)) * u).astype(BF16)


def params(mib):
    return pltpu.CompilerParams(vmem_limit_bytes=mib * 1024 * 1024)


def whole(shape):
    zeros = (0,) * len(shape)
    return pl.BlockSpec(shape, lambda *_: zeros)


def shards(residual, features, filters, skip_gain, w_out, norm_gain, w_gate, w_up):
    core = lax.axis_index("tp") % 2
    x_lo = lax.axis_index("ctx") % 2
    feat = features.transpose(1, 0, 2)

    pad = jnp.zeros((FF_PAD - FF_LOC, CH), BF16)
    w_own = jnp.concatenate([w_gate.T, pad, w_up.T, pad], axis=0)

    sent = pl.pallas_call(
        prep_kernel,
        out_shape=jax.ShapeDtypeStruct((N_CTX, 2 * SUB, ROWS), BF16),
        name="prep",
    )(feat, filters)
    recv = lax.all_to_all(sent, "ctx", 0, 0, tiled=True)
    w_oth = shift(w_own, k=1)
    tables = [jnp.asarray(t) for t in dft_tables()]
    conv = pl.pallas_call(
        conv_kernel,
        out_shape=jax.ShapeDtypeStruct((N_CTX, SUB, ROWS), BF16),
        scratch_shapes=[
            pltpu.VMEM((N_CTX, 2 * SUB, 256), F32),
            pltpu.VMEM((N_CTX, 3, SUB, 128), F32),
            pltpu.VMEM((N_CTX, SUB, 256), F32),
        ],
        compiler_params=params(32),
        name="conv",
    )(recv, *tables)
    conv_rows = lax.all_to_all(conv, "ctx", 0, 0, tiled=True)
    mixed = pl.pallas_call(
        mix_kernel,
        out_shape=jax.ShapeDtypeStruct((ROWS, CH), BF16),
        name="mix",
    )(conv_rows, feat, skip_gain[None, :])

    mixed_all = lax.all_gather(mixed, "tp")
    stream = pl.pallas_call(
        out_proj_kernel,
        out_shape=jax.ShapeDtypeStruct((ROWS, CH), BF16),
        grid=(N_TP,),
        in_specs=[
            pl.BlockSpec((1, ROWS, CH), lambda t: (t, 0, 0)),
            pl.BlockSpec((CH, CH), lambda t: (t, 0)),
            whole((ROWS, CH)),
        ],
        out_specs=whole((ROWS, CH)),
        scratch_shapes=[pltpu.VMEM((ROWS, CH), F32)],
        compiler_params=params(32),
        name="out_proj",
    )(mixed_all, w_out, residual)

    gain_oth = shift(norm_gain[None, :], k=1)
    gains = jnp.concatenate([norm_gain[None, :], gain_oth], axis=0)
    stream_oth = shift(stream, k=1)
    both = jnp.stack([stream, stream_oth])
    across = shift(both, x=0) if False else lax.ppermute(
        both,
        AXES,
        [
            (i, join_index(z, x ^ 1, y, k))
            for i in range(N_CTX * N_TP)
            for z, x, y, k in [split_index(i)]
        ],
    )
    held = jnp.where(x_lo == core, both, across)
    z_groups = [[z * 2 + xl for z in range(8)] for xl in range(2)]
    gathered = lax.all_gather(held, "ctx", axis_index_groups=z_groups)

    partial = pl.pallas_call(
        mlp_kernel,
        out_shape=jax.ShapeDtypeStruct((8, 2 * FF_PAD, ROWS), BF16),
        grid=(8, 2),
        in_specs=[
            pl.BlockSpec((None, 1, ROWS, CH), lambda b, p: (b, 0, 0, 0)),
            pl.BlockSpec((None, 1, ROWS, CH), lambda b, p: (b, 1, 0, 0)),
            whole((2, CH)),
            pl.BlockSpec((1, FF_PAD, CH), lambda b, p: (p, 0, 0)),
            pl.BlockSpec((1, FF_PAD, CH), lambda b, p: (p, 0, 0)),
        ],
        out_specs=pl.BlockSpec((1, FF_PAD, ROWS), lambda b, p: (b, p, 0)),
        scratch_shapes=[
            pltpu.VMEM((ROWS, CH), BF16),
            pltpu.VMEM((ROWS, CH), BF16),
            pltpu.VMEM((8, ROWS), F32),
        ],
        compiler_params=params(48),
        name="mlp",
    )(
        gathered,
        gathered,
        gains,
        w_own.reshape(2, FF_PAD, CH),
        w_oth.reshape(2, FF_PAD, CH),
    )
    reduced = lax.psum_scatter(
        partial, "tp", scatter_dimension=0, axis_index_groups=PLANE_GROUPS, tiled=True
    )[0]
    hidden_t = pl.pallas_call(
        finish_kernel,
        out_shape=jax.ShapeDtypeStruct((FF_LOC, ROWS), BF16),
        compiler_params=params(32),
        name="finish",
    )(reduced)
    return stream, hidden_t.T


def solution(mesh):
    placed = (
        P("ctx", "tp"),
        P("ctx", None, "tp"),
        P("ctx", "tp"),
        P("tp"),
        P(None, "tp"),
        P("tp"),
        P("tp", "ctx"),
        P("tp", "ctx"),
    )
    return jax.shard_map(
        shards,
        mesh=mesh,
        in_specs=placed,
        out_specs=(P("ctx", "tp"), P("tp", "ctx")),
        check_vma=False,
    )
```

```python
import math

import jax
import jax.numpy as jnp
import numpy as np
from jax import lax
from jax.experimental import pallas as pl
from jax.experimental.pallas import tpu as pltpu
from jax.sharding import PartitionSpec as P

F32 = jnp.float32
BF16 = jnp.bfloat16
AXES = ("ctx", "tp")
N_CTX = 16
N_TP = 16
ROWS = 128
CH = 512
SUB = 32
FF_LOC = 1368
FF_PAD = 1376
EPS = 1e-06
PLANE_GROUPS = [[xh * 8 + y * 2 + k for xh in range(2) for y in range(4)] for k in range(2)]
Z_GROUPS = [[z * 2 + x_lo for z in range(8)] for x_lo in range(2)]


def split_index(i):
    c, t = divmod(i, N_TP)
    z, x_lo = divmod(c, 2)
    x_hi, r = divmod(t, 8)
    y, k = divmod(r, 2)
    return z, x_hi * 2 + x_lo, y, k


def join_index(z, x, y, k):
    x = x % 4
    return ((z % 8) * 2 + x % 2) * N_TP + (x // 2) * 8 + (y % 4) * 2 + k % 2


def shift(arr, z=0, x=0, y=0, k=0):
    pairs = []
    for i in range(N_CTX * N_TP):
        az, ax, ay, ak = split_index(i)
        pairs.append((i, join_index(az + z, ax + x, ay + y, ak + k)))
    return lax.ppermute(arr, AXES, pairs)


def split_bf16(table):
    high = np.asarray(table, np.float32).astype(jnp.bfloat16)
    low = (np.asarray(table, np.float32) - high.astype(np.float32)).astype(jnp.bfloat16)
    return high, low


def dft_tables():
    size = 2 * ROWS
    pos = np.arange(ROWS)
    freq = np.arange(ROWS)
    phase = (pos[:, None] * freq[None, :]) % size
    angle = 2.0 * math.pi / size * phase
    cos, sin = np.cos(angle), np.sin(angle)
    sign = np.where(pos % 2 == 0, 1.0, -1.0)
    fwd_im = -sin
    fwd_im[:, 0] = sign
    forward = np.concatenate([cos, fwd_im], axis=1)
    weight = np.where(freq == 0, 1.0, 2.0)[:, None] / size
    inv_re = cos.T * weight
    inv_im = -sin.T * weight
    inv_im[0, :] = sign / size
    inverse = np.concatenate([inv_re, inv_im], axis=0)
    return np.concatenate(split_bf16(forward) + split_bf16(inverse.T), axis=1)


def dot(a, b):
    return jnp.dot(a, b, preferred_element_type=F32)


def dot_nt(a, b):
    return lax.dot_general(a, b, (((1,), (1,)), ((), ())), preferred_element_type=F32)


def prep_kernel(feat_ref, filt_ref, out_ref):
    prod = feat_ref[1].astype(F32) * feat_ref[2].astype(F32)
    filt = filt_ref[...]
    for j in range(CH // 128):
        cols = slice(128 * j, 128 * j + 128)
        out_ref[4 * j : 4 * j + 4, 0:SUB, :] = prod[:, cols].T.astype(BF16).reshape(4, SUB, 128)
        out_ref[4 * j : 4 * j + 4, SUB : 2 * SUB, :] = (
            filt[:, cols].T.astype(BF16).reshape(4, SUB, 128)
        )


def conv_kernel(x_ref, tab_ref, out_ref, spec, filt, outs):
    x = x_ref[...].reshape(N_CTX * 2 * SUB, ROWS)
    spec[...] = (dot(x, tab_ref[:, 0:256]) + dot(x, tab_ref[:, 256:512])).reshape(N_CTX, 2 * SUB, 256)
    lane = lax.broadcasted_iota(jnp.int32, (SUB, 128), 1)
    sign = jnp.where(lane % 2 == 0, 1.0, -1.0).astype(F32)
    first = lane == 0
    for d in range(N_CTX):
        re = spec[d, SUB:, 0:128]
        im = spec[d, SUB:, 128:256]
        if d > 0:
            re = re + sign * spec[d - 1, SUB:, 0:128]
            im = im + sign * spec[d - 1, SUB:, 128:256]
        filt[d, 0] = re
        filt[d, 1] = jnp.where(first, 0.0, im)
        filt[d, 2] = jnp.where(first, im, re)
    for m in range(N_CTX):
        acc_re = jnp.zeros((SUB, 128), F32)
        acc_im = jnp.zeros((SUB, 128), F32)
        for n in range(m + 1):
            pr = spec[n, 0:SUB, 0:128]
            pi = spec[n, 0:SUB, 128:256]
            hr, hz, hq = filt[m - n, 0], filt[m - n, 1], filt[m - n, 2]
            acc_re = acc_re + (pr * hr - pi * hz)
            acc_im = acc_im + (pr * hz + pi * hq)
        outs[m, :, 0:128] = acc_re
        outs[m, :, 128:256] = acc_im
    total = outs[...].reshape(N_CTX * SUB, 256)
    high = total.astype(BF16)
    low = (total - high.astype(F32)).astype(BF16)
    inv_high, inv_low = tab_ref[:, 512:768], tab_ref[:, 768:1024]
    y = dot_nt(high, inv_high) + dot_nt(high, inv_low) + dot_nt(low, inv_high)
    out_ref[...] = y.astype(BF16).reshape(N_CTX, SUB, ROWS)


def mix_kernel(conv_ref, feat_ref, skip_ref, out_ref):
    conv = conv_ref[...].reshape(CH, ROWS).astype(F32)
    for j in range(CH // 128):
        cols = slice(128 * j, 128 * j + 128)
        prod = feat_ref[1, :, cols].astype(F32) * feat_ref[2, :, cols].astype(F32)
        long = conv[cols, :].T
        gate = feat_ref[0, :, cols].astype(F32)
        mixed = (gate * (long + skip_ref[:, cols] * prod)).astype(BF16)
        for copy in range(8):
            out_ref[copy, :, cols] = mixed


def out_proj_first_kernel(core_ref, mixed_ref, w_ref, res_ref, out_ref):
    del core_ref
    j = pl.program_id(0)

    @pl.when(j == 0)
    def _():
        out_ref[...] = res_ref[...].astype(F32)

    out_ref[...] += dot(mixed_ref[0], w_ref[...])


def out_proj_second_kernel(core_ref, mixed_ref, w_ref, sum_ref, out_ref, acc):
    del core_ref
    j = pl.program_id(0)

    @pl.when(j == 0)
    def _():
        acc[...] = sum_ref[...]

    acc[...] += dot(mixed_ref[0], w_ref[...])

    @pl.when(j == pl.num_programs(0) - 1)
    def _():
        out_ref[...] = acc[...].astype(BF16)


def square_sums(values):
    ones = jnp.ones((8, CH), BF16)
    sq = values * values
    high = sq.astype(BF16)
    return dot_nt(ones, high) + dot_nt(ones, (sq - high.astype(F32)).astype(BF16))


def two_rows(total):
    high = total.astype(BF16).astype(F32)
    row = lax.broadcasted_iota(jnp.int32, total.shape, 0)
    return jnp.where(row == 0, high, jnp.where(row == 1, total - high, 0.0))


def with_tail(rows, tail):
    return jnp.concatenate([rows, tail], axis=0).astype(BF16)


def mlp_kernel(
    idx_ref, own0_ref, oth0_ref, own1_ref, oth1_ref, gain_ref, gain_oth_ref,
    wg_ref, wgx_ref, wu_ref, wux_ref, g0_ref, g1_ref, *rest
):
    del idx_ref
    up_refs, (so, sx, aux) = rest[:4], rest[4:]
    b = pl.program_id(0)
    for a, (own_ref, oth_ref) in enumerate(((own0_ref, oth0_ref), (own1_ref, oth1_ref))):
        own = own_ref[...].astype(F32)
        oth = oth_ref[...].astype(F32)
        rows = slice(a * ROWS, a * ROWS + ROWS)
        so[rows, :] = (own * gain_ref[...]).astype(BF16)
        sx[rows, :] = (oth * gain_oth_ref[...]).astype(BF16)
        aux[:, rows] = two_rows(square_sums(own) + square_sums(oth))
    zeros = jnp.zeros((FF_PAD - FF_LOC, ROWS), F32)
    gate = dot_nt(wg_ref[...], so[...]) + dot_nt(wgx_ref[...], sx[...])
    g0_ref[0] = with_tail(gate[:, :ROWS], zeros)
    g1_ref[0] = with_tail(gate[:, ROWS:], zeros)
    up = dot_nt(wu_ref[...], so[...]) + dot_nt(wux_ref[...], sx[...])
    for step, up_ref in enumerate(up_refs):

        @pl.when(b == step)
        def _():
            up_ref[0] = with_tail(up[:, :ROWS], aux[:, :ROWS])
            up_ref[1] = with_tail(up[:, ROWS:], aux[:, ROWS:])


def gate_mid_kernel(own_ref, recv_ref, *out_refs):
    for b, out_ref in enumerate(out_refs):
        out_ref[...] = (own_ref[b].astype(F32) + recv_ref[b].astype(F32)).astype(BF16)


def up_mid_kernel(own_ref, r1_ref, r2_ref, r3_ref, keep_ref, send_ref):
    for a, out_ref in enumerate((keep_ref, send_ref)):
        total = own_ref[a].astype(F32) + r1_ref[a].astype(F32)
        total = total + (r2_ref[a].astype(F32) + r3_ref[a].astype(F32))
        tail = total[FF_LOC:]
        out_ref[...] = with_tail(total[:FF_LOC], two_rows(tail[0:1] + tail[1:2] + jnp.zeros_like(tail)))


def finish_kernel(g0_ref, g1_ref, g2_ref, g3_ref, u0_ref, u1_ref, out_ref):
    gate = (g0_ref[...].astype(F32) + g1_ref[...].astype(F32)) + (
        g2_ref[...].astype(F32) + g3_ref[...].astype(F32)
    )
    up = u0_ref[...].astype(F32) + u1_ref[...].astype(F32)
    sums = up[FF_LOC : FF_LOC + 1] + up[FF_LOC + 1 : FF_LOC + 2]
    scale = lax.rsqrt(sums * (1.0 / (N_TP * CH)) + EPS)
    g = gate[:FF_LOC] * scale
    u = up[:FF_LOC] * scale
    out_ref[...] = (g / (1.0 + jnp.exp(-g)) * u).astype(BF16)


def params(mib):
    return pltpu.CompilerParams(vmem_limit_bytes=mib * 1024 * 1024)


def whole(shape):
    zeros = (0,) * len(shape)
    return pl.BlockSpec(shape, lambda *_: zeros)


def pairs_of(rule):
    pairs = []
    for i in range(N_CTX * N_TP):
        target = rule(*split_index(i))
        if target is not None:
            pairs.append((i, join_index(*target)))
    return pairs


def to_row_owner_first(z, x, y, k):
    return (z, x ^ 1, y, k) if k == x % 2 else (z, x, y, k ^ 1)


def to_row_owner_second(z, x, y, k):
    return None if k == x % 2 else (z, x ^ 1, y, k ^ 1)


def out_proj(kernel, offset, core, mixed, w_out, start, dtype, scratch):
    return pl.pallas_call(
        kernel,
        out_shape=jax.ShapeDtypeStruct((ROWS, CH), dtype),
        grid_spec=pltpu.PrefetchScalarGridSpec(
            num_scalar_prefetch=1,
            grid=(N_TP // 2,),
            in_specs=[
                pl.BlockSpec((1, ROWS, CH), lambda j, c: (j, 0, 0)),
                pl.BlockSpec((CH, CH), lambda j, c: (2 * j + jnp.bitwise_xor(c[0], offset), 0)),
                whole((ROWS, CH)),
            ],
            out_specs=whole((ROWS, CH)),
            scratch_shapes=scratch,
        ),
        compiler_params=params(56),
        name="out_proj",
    )(core, mixed, w_out, start)


def shards(residual, features, filters, skip_gain, w_out, norm_gain, w_gate, w_up):
    ctx = lax.axis_index("ctx")
    tp = lax.axis_index("tp")
    core, x_lo = tp % 2, ctx % 2
    x_hi, y = tp // 8, (tp // 2) % 4
    feat = features.transpose(1, 0, 2)
    wg, wu = w_gate.T, w_up.T
    gain = norm_gain[None, :]
    wg_oth, wu_oth, gain_oth = shift(wg, k=1), shift(wu, k=1), shift(gain, k=1)

    sent = pl.pallas_call(
        prep_kernel,
        out_shape=jax.ShapeDtypeStruct((N_CTX, 2 * SUB, ROWS), BF16),
        compiler_params=params(56),
        name="prep",
    )(feat, filters)
    recv = lax.all_to_all(sent, "ctx", 0, 0, tiled=True)
    conv = pl.pallas_call(
        conv_kernel,
        out_shape=jax.ShapeDtypeStruct((N_CTX, SUB, ROWS), BF16),
        scratch_shapes=[
            pltpu.VMEM((N_CTX, 2 * SUB, 256), F32),
            pltpu.VMEM((N_CTX, 3, SUB, 128), F32),
            pltpu.VMEM((N_CTX, SUB, 256), F32),
        ],
        compiler_params=params(56),
        name="conv",
    )(recv, jnp.asarray(dft_tables()))
    conv_rows = lax.all_to_all(conv, "ctx", 0, 0, tiled=True)
    copies = pl.pallas_call(
        mix_kernel,
        out_shape=jax.ShapeDtypeStruct((8, ROWS, CH), BF16),
        compiler_params=params(56),
        name="mix",
    )(conv_rows, feat, skip_gain[None, :])

    mixed = lax.all_to_all(
        copies, "tp", 0, 0, axis_index_groups=PLANE_GROUPS, tiled=True
    )
    mixed_oth = shift(mixed, k=1)
    core_arr = core.astype(jnp.int32)[None]
    half = out_proj(out_proj_first_kernel, 0, core_arr, mixed, w_out, residual, F32, [])
    stream = out_proj(
        out_proj_second_kernel, 1, core_arr, mixed_oth, w_out, half, BF16,
        [pltpu.VMEM((ROWS, CH), F32)],
    )

    first = lax.ppermute(stream, AXES, pairs_of(to_row_owner_first))
    second = lax.ppermute(stream, AXES, pairs_of(to_row_owner_second))
    here = x_lo == core
    held = jnp.stack([jnp.where(here, stream, first), jnp.where(here, first, second)])
    gathered = lax.all_gather(held, "ctx", axis_index_groups=Z_GROUPS)

    order = [4 * ((x_hi + a) % 2) + (y + b) % 4 for b in range(4) for a in range(2)]
    idx = jnp.stack(order).astype(jnp.int32)

    def rows_spec(a, part):
        return pl.BlockSpec((None, None, ROWS, CH), lambda b, i: (i[2 * b + a], part, 0, 0))

    part_shape = (FF_PAD, ROWS)
    outs = pl.pallas_call(
        mlp_kernel,
        out_shape=[jax.ShapeDtypeStruct((4,) + part_shape, BF16)] * 2
        + [jax.ShapeDtypeStruct((2,) + part_shape, BF16)] * 4,
        grid_spec=pltpu.PrefetchScalarGridSpec(
            num_scalar_prefetch=1,
            grid=(4,),
            in_specs=[rows_spec(0, 0), rows_spec(0, 1), rows_spec(1, 0), rows_spec(1, 1)]
            + [whole((1, CH))] * 2
            + [whole((FF_LOC, CH))] * 4,
            out_specs=[pl.BlockSpec((1,) + part_shape, lambda b, i: (b, 0, 0))] * 2
            + [whole((2,) + part_shape)] * 4,
            scratch_shapes=[
                pltpu.VMEM((2 * ROWS, CH), BF16),
                pltpu.VMEM((2 * ROWS, CH), BF16),
                pltpu.VMEM((8, 2 * ROWS), F32),
            ],
        ),
        compiler_params=params(56),
        name="mlp",
    )(idx, gathered, gathered, gathered, gathered, gain, gain_oth, wg, wg_oth, wu, wu_oth)
    g_keep, g_send, u_parts = outs[0], outs[1], outs[2:]

    g_recv = shift(g_send, x=2)
    u_recv = [shift(u_parts[b], y=b) for b in (2, 1, 3)]
    g_mid = pl.pallas_call(
        gate_mid_kernel,
        out_shape=[jax.ShapeDtypeStruct(part_shape, BF16)] * 4,
        compiler_params=params(56),
        name="gate_mid",
    )(g_keep, g_recv)
    u_keep, u_send = pl.pallas_call(
        up_mid_kernel,
        out_shape=[jax.ShapeDtypeStruct(part_shape, BF16)] * 2,
        compiler_params=params(56),
        name="up_mid",
    )(u_parts[0], *u_recv)
    u_last = shift(u_send, x=2)
    g_last = [shift(g_mid[b], y=b) for b in (2, 1, 3)]
    hidden_t = pl.pallas_call(
        finish_kernel,
        out_shape=jax.ShapeDtypeStruct((FF_LOC, ROWS), BF16),
        compiler_params=params(56),
        name="finish",
    )(g_mid[0], *g_last, u_keep, u_last)
    return stream, hidden_t.T


def solution(mesh):
    placed = (
        P("ctx", "tp"),
        P("ctx", None, "tp"),
        P("ctx", "tp"),
        P("tp"),
        P(None, "tp"),
        P("tp"),
        P("tp", "ctx"),
        P("tp", "ctx"),
    )
    return jax.shard_map(
        shards,
        mesh=mesh,
        in_specs=placed,
        out_specs=(P("ctx", "tp"), P("tp", "ctx")),
        check_vma=False,
    )
```

```python
import functools
import math

import jax
import jax.numpy as jnp
import numpy as np
from jax import lax
from jax.experimental import pallas as pl
from jax.experimental.pallas import tpu as pltpu
from jax.sharding import PartitionSpec as P

F32 = jnp.float32
BF16 = jnp.bfloat16
AXES = ("ctx", "tp")
N_CTX = 16
N_TP = 16
ROWS = 128
CH = 512
SUB = 32
FF_LOC = 1368
FF_PAD = 1376
EPS = 1e-06
PLANE_GROUPS = [[xh * 8 + y * 2 + k for xh in range(2) for y in range(4)] for k in range(2)]


def split_index(i):
    c, t = divmod(i, N_TP)
    z, x_lo = divmod(c, 2)
    x_hi, r = divmod(t, 8)
    y, k = divmod(r, 2)
    return z, x_hi * 2 + x_lo, y, k


def join_index(z, x, y, k):
    x = x % 4
    return ((z % 8) * 2 + x % 2) * N_TP + (x // 2) * 8 + (y % 4) * 2 + k % 2


def shift(arr, z=0, x=0, y=0, k=0):
    pairs = []
    for i in range(N_CTX * N_TP):
        az, ax, ay, ak = split_index(i)
        pairs.append((i, join_index(az + z, ax + x, ay + y, ak + k)))
    return lax.ppermute(arr, AXES, pairs)


def split_bf16(table):
    high = np.asarray(table, np.float32).astype(jnp.bfloat16)
    low = (np.asarray(table, np.float32) - high.astype(np.float32)).astype(jnp.bfloat16)
    return high, low


def dft_tables():
    size = 2 * ROWS
    pos = np.arange(ROWS)
    freq = np.arange(ROWS)
    phase = (pos[:, None] * freq[None, :]) % size
    angle = 2.0 * math.pi / size * phase
    cos, sin = np.cos(angle), np.sin(angle)
    sign = np.where(pos % 2 == 0, 1.0, -1.0)
    fwd_im = -sin
    fwd_im[:, 0] = sign
    forward = np.concatenate([cos, fwd_im], axis=1)
    weight = np.where(freq == 0, 1.0, 2.0)[:, None] / size
    inv_re = cos.T * weight
    inv_im = -sin.T * weight
    inv_im[0, :] = sign / size
    inverse = np.concatenate([inv_re, inv_im], axis=0)
    return np.concatenate(split_bf16(forward) + split_bf16(inverse.T), axis=1)


def dot(a, b):
    return jnp.dot(a, b, preferred_element_type=F32)


def dot_nt(a, b):
    return lax.dot_general(a, b, (((1,), (1,)), ((), ())), preferred_element_type=F32)


def prep_kernel(feat_ref, filt_ref, out_ref):
    prod = feat_ref[1].astype(F32) * feat_ref[2].astype(F32)
    filt = filt_ref[...]
    for j in range(CH // 128):
        cols = slice(128 * j, 128 * j + 128)
        out_ref[4 * j : 4 * j + 4, 0:SUB, :] = prod[:, cols].T.astype(BF16).reshape(4, SUB, 128)
        out_ref[4 * j : 4 * j + 4, SUB : 2 * SUB, :] = (
            filt[:, cols].T.astype(BF16).reshape(4, SUB, 128)
        )


def conv_kernel(x_ref, tab_ref, out_ref, spec, filt, outs):
    x = x_ref[...].reshape(N_CTX * 2 * SUB, ROWS)
    spec[...] = (dot(x, tab_ref[:, 0:256]) + dot(x, tab_ref[:, 256:512])).reshape(N_CTX, 2 * SUB, 256)
    lane = lax.broadcasted_iota(jnp.int32, (SUB, 128), 1)
    sign = jnp.where(lane % 2 == 0, 1.0, -1.0).astype(F32)
    first = lane == 0
    for d in range(N_CTX):
        re = spec[d, SUB:, 0:128]
        im = spec[d, SUB:, 128:256]
        if d > 0:
            re = re + sign * spec[d - 1, SUB:, 0:128]
            im = im + sign * spec[d - 1, SUB:, 128:256]
        filt[d, 0] = re
        filt[d, 1] = jnp.where(first, 0.0, im)
        filt[d, 2] = jnp.where(first, im, re)
    for m in range(N_CTX):
        acc_re = jnp.zeros((SUB, 128), F32)
        acc_im = jnp.zeros((SUB, 128), F32)
        for n in range(m + 1):
            pr = spec[n, 0:SUB, 0:128]
            pi = spec[n, 0:SUB, 128:256]
            hr, hz, hq = filt[m - n, 0], filt[m - n, 1], filt[m - n, 2]
            acc_re = acc_re + (pr * hr - pi * hz)
            acc_im = acc_im + (pr * hz + pi * hq)
        outs[m, :, 0:128] = acc_re
        outs[m, :, 128:256] = acc_im
    total = outs[...].reshape(N_CTX * SUB, 256)
    high = total.astype(BF16)
    low = (total - high.astype(F32)).astype(BF16)
    inv_high, inv_low = tab_ref[:, 512:768], tab_ref[:, 768:1024]
    y = dot_nt(high, inv_high) + dot_nt(high, inv_low) + dot_nt(low, inv_high)
    out_ref[...] = y.astype(BF16).reshape(N_CTX, SUB, ROWS)


def mix_kernel(conv_ref, feat_ref, skip_ref, out_ref):
    conv = conv_ref[...].reshape(CH, ROWS).astype(F32)
    for j in range(CH // 128):
        cols = slice(128 * j, 128 * j + 128)
        prod = feat_ref[1, :, cols].astype(F32) * feat_ref[2, :, cols].astype(F32)
        long = conv[cols, :].T
        gate = feat_ref[0, :, cols].astype(F32)
        mixed = (gate * (long + skip_ref[:, cols] * prod)).astype(BF16)
        for copy in range(8):
            out_ref[copy, :, cols] = mixed


def out_proj_kernel(offset, core_ref, mixed_hbm, w_hbm, start_ref, out_ref, mixed, w_buf, sem):
    first = jnp.bitwise_xor(core_ref[0], offset)
    copies = []
    for j in range(N_TP // 2):
        rows = pl.ds(pl.multiple_of((2 * j + first) * CH, CH), CH)
        copies.append(
            (
                pltpu.make_async_copy(mixed_hbm.at[j], mixed.at[j], sem.at[0, j]),
                pltpu.make_async_copy(w_hbm.at[rows], w_buf.at[j], sem.at[1, j]),
            )
        )
    for pair in copies:
        for copy in pair:
            copy.start()
    acc = start_ref[...].astype(F32)
    for j, pair in enumerate(copies):
        for copy in pair:
            copy.wait()
        acc = acc + dot(mixed[j], w_buf[j])
    out_ref[...] = acc.astype(out_ref.dtype)


def square_sums(values):
    ones = jnp.ones((8, CH), BF16)
    sq = values * values
    high = sq.astype(BF16)
    return dot_nt(ones, high) + dot_nt(ones, (sq - high.astype(F32)).astype(BF16))


def two_rows(total):
    high = total.astype(BF16).astype(F32)
    row = lax.broadcasted_iota(jnp.int32, total.shape, 0)
    return jnp.where(row == 0, high, jnp.where(row == 1, total - high, 0.0))


def with_tail(rows, tail):
    return jnp.concatenate([rows, tail], axis=0).astype(BF16)


def mlp_kernel(slots, with_squares, idx_ref, *refs):
    blocks, (gain_ref, gain_oth_ref, w_ref, wx_ref) = refs[:9], refs[9:13]
    n = len(slots)
    out_ref, rows_in, so, sx, row_sem = refs[13:]

    def halves(d):
        if d == 4:
            return blocks[4], blocks[5]
        whole_block = blocks[d if d < 4 else d + 1]
        return whole_block.at[0], whole_block.at[1]

    def row_copy(d, at, part):
        return pltpu.make_async_copy(halves(d)[part], rows_in.at[at, part], row_sem.at[at, part])

    for at, slot in enumerate(slots):
        which = idx_ref[slot]
        for d in range(8):

            @pl.when(which == d)
            def _():
                row_copy(d, at, 0).start()
                row_copy(d, at, 1).start()
    tails = []
    for at in range(n):
        row_copy(0, at, 0).wait()
        row_copy(0, at, 1).wait()
        own = rows_in[at, 0].astype(F32)
        oth = rows_in[at, 1].astype(F32)
        span = slice(at * ROWS, at * ROWS + ROWS)
        so[span, :] = (own * gain_ref[...]).astype(BF16)
        sx[span, :] = (oth * gain_oth_ref[...]).astype(BF16)
        if with_squares:
            tails.append(two_rows(square_sums(own) + square_sums(oth)))
        else:
            tails.append(jnp.zeros((FF_PAD - FF_LOC, ROWS), F32))
    for at in range(0, n, 2):
        span = slice(at * ROWS, at * ROWS + 2 * ROWS)
        res = dot_nt(w_ref[...], so[span, :]) + dot_nt(wx_ref[...], sx[span, :])
        out_ref[at] = with_tail(res[:, :ROWS], tails[at])
        out_ref[at + 1] = with_tail(res[:, ROWS:], tails[at + 1])


def params(mib):
    return pltpu.CompilerParams(vmem_limit_bytes=mib * 1024 * 1024)


def pairs_of(rule):
    pairs = []
    for i in range(N_CTX * N_TP):
        target = rule(*split_index(i))
        if target is not None:
            pairs.append((i, join_index(*target)))
    return pairs


def to_row_owner_first(z, x, y, k):
    return (z, x ^ 1, y, k) if k == x % 2 else (z, x, y, k ^ 1)


def to_row_owner_second(z, x, y, k):
    return None if k == x % 2 else (z, x ^ 1, y, k ^ 1)


def in_smem():
    return pl.BlockSpec(memory_space=pltpu.SMEM)


def anywhere():
    return pl.BlockSpec(memory_space=pl.ANY)


def out_proj(offset, core, mixed, w_out, start, dtype):
    return pl.pallas_call(
        functools.partial(out_proj_kernel, offset),
        out_shape=jax.ShapeDtypeStruct((ROWS, CH), dtype),
        in_specs=[
            in_smem(),
            anywhere(),
            pl.BlockSpec(memory_space=pltpu.HBM),
            pl.BlockSpec(memory_space=pltpu.VMEM),
        ],
        scratch_shapes=[
            pltpu.VMEM((N_TP // 2, ROWS, CH), BF16),
            pltpu.VMEM((N_TP // 2, CH, CH), BF16),
            pltpu.SemaphoreType.DMA((2, N_TP // 2)),
        ],
        compiler_params=params(51),
        cost_estimate=pl.CostEstimate(
            flops=2 * ROWS * CH * N_TP // 2 * CH, bytes_accessed=5 << 20, transcendentals=0
        ),
        name="out_proj",
    )(core, mixed, w_out, start)


def mlp_part(slots, with_squares, idx, blocks, gains, weights):
    n = len(slots)
    vmem = pl.BlockSpec(memory_space=pltpu.VMEM)
    return pl.pallas_call(
        functools.partial(mlp_kernel, tuple(slots), with_squares),
        out_shape=jax.ShapeDtypeStruct((n, FF_PAD, ROWS), BF16),
        in_specs=[in_smem()] + [anywhere()] * 9 + [vmem] * 4,
        scratch_shapes=[
            pltpu.VMEM((n, 2, ROWS, CH), BF16),
            pltpu.VMEM((n * ROWS, CH), BF16),
            pltpu.VMEM((n * ROWS, CH), BF16),
            pltpu.SemaphoreType.DMA((n, 2)),
        ],
        compiler_params=params(24),
        cost_estimate=pl.CostEstimate(
            flops=4 * n * ROWS * CH * FF_LOC, bytes_accessed=5 << 20, transcendentals=0
        ),
        name="mlp",
    )(idx, *blocks, *gains, *weights)


def shards(residual, features, filters, skip_gain, w_out, norm_gain, w_gate, w_up):
    ctx = lax.axis_index("ctx")
    tp = lax.axis_index("tp")
    core, x_lo = tp % 2, ctx % 2
    x_hi, y = tp // 8, (tp // 2) % 4
    feat = features.transpose(1, 0, 2)
    wg, wu = w_gate.T, w_up.T
    gain = norm_gain[None, :]
    wg_oth, wu_oth, gain_oth = shift(wg, k=1), shift(wu, k=1), shift(gain, k=1)

    sent = pl.pallas_call(
        prep_kernel,
        out_shape=jax.ShapeDtypeStruct((N_CTX, 2 * SUB, ROWS), BF16),
        compiler_params=params(56),
        name="prep",
    )(feat, filters)
    recv = lax.all_to_all(sent, "ctx", 0, 0, tiled=True)
    recv, wg_oth, wu_oth, gain_oth = lax.optimization_barrier((recv, wg_oth, wu_oth, gain_oth))
    conv = pl.pallas_call(
        conv_kernel,
        out_shape=jax.ShapeDtypeStruct((N_CTX, SUB, ROWS), BF16),
        scratch_shapes=[
            pltpu.VMEM((N_CTX, 2 * SUB, 256), F32),
            pltpu.VMEM((N_CTX, 3, SUB, 128), F32),
            pltpu.VMEM((N_CTX, SUB, 256), F32),
        ],
        compiler_params=params(56),
        name="conv",
    )(recv, jnp.asarray(dft_tables()))
    conv_rows = lax.all_to_all(conv, "ctx", 0, 0, tiled=True)
    copies = pl.pallas_call(
        mix_kernel,
        out_shape=jax.ShapeDtypeStruct((8, ROWS, CH), BF16),
        compiler_params=params(56),
        name="mix",
    )(conv_rows, feat, skip_gain[None, :])

    mixed = lax.all_to_all(
        copies, "tp", 0, 0, axis_index_groups=PLANE_GROUPS, tiled=True
    )
    mixed_oth = shift(mixed, k=1)
    core_arr = core.astype(jnp.int32)[None]
    half = out_proj(0, core_arr, mixed, w_out, residual, F32)
    stream = out_proj(1, core_arr, mixed_oth, w_out, half, BF16)

    first = lax.ppermute(stream, AXES, pairs_of(to_row_owner_first))
    second = lax.ppermute(stream, AXES, pairs_of(to_row_owner_second))
    here = x_lo == core
    held = jnp.stack([jnp.where(here, stream, first), jnp.where(here, first, second)])
    below, above = [held], [held]
    for step in (1, 2):
        below.append(shift(held, z=step))
        above.append(shift(held, z=-step))
    below.append(shift(below[2], z=1))
    above.append(shift(above[2], z=-1))
    opposite = (shift(below[2][0], z=2), shift(above[2][1], z=-2))
    blocks = above + list(opposite) + [below[3], below[2], below[1]]

    z = ctx // 2
    idx = jnp.stack(
        [
            (4 * ((x_hi + a) % 2) + (y + b) % 4 - z) % 8
            for b in range(4)
            for a in range(2)
        ]
    ).astype(jnp.int32)
    part = functools.partial(
        mlp_part, idx=idx, blocks=blocks, gains=(gain, gain_oth)
    )
    gate_w, up_w = (wg, wg_oth), (wu, wu_oth)

    g_send_a = part((5, 3), False, weights=gate_w)
    idx_up, g_send_a = lax.optimization_barrier((idx, g_send_a))
    g_recv_a = shift(g_send_a, x=2)
    part_up = functools.partial(part, idx=idx_up)
    u_sends = {b: part_up((2 * b, 2 * b + 1), True, weights=up_w) for b in (2, 1, 3)}
    u_recv = {b: shift(u_sends[b], y=b) for b in (2, 1, 3)}
    g_send_b = part((7, 1), False, weights=gate_w)
    g_recv_b = shift(g_send_b, x=2)
    g_keep_a = part((4, 2), False, weights=gate_w)
    g_keep_b = part((6, 0), False, weights=gate_w)
    u_keep = part((0, 1), True, weights=up_w)

    def add(*terms):
        total = terms[0].astype(F32)
        for term in terms[1:]:
            total = total + term.astype(F32)
        return total

    g_last = [
        shift(add(g_keep_a[0], g_recv_a[0]).astype(BF16), y=2),
        shift(add(g_keep_a[1], g_recv_a[1]).astype(BF16), y=1),
        shift(add(g_keep_b[0], g_recv_b[0]).astype(BF16), y=3),
    ]
    g_own = add(g_keep_b[1], g_recv_b[1])
    u_send = add(u_keep[1], *(u_recv[b][1] for b in (2, 1, 3))).astype(BF16)
    u_last = shift(u_send, x=2)
    u_own = add(u_keep[0], *(u_recv[b][0] for b in (2, 1, 3)))
    gate = add(g_own, *g_last)
    up = add(u_own, u_last)
    sums = up[FF_LOC : FF_LOC + 1] + up[FF_LOC + 1 : FF_LOC + 2]
    scale = lax.rsqrt(sums * (1.0 / (N_TP * CH)) + EPS)
    gate_vals = gate[:FF_LOC] * scale
    up_vals = up[:FF_LOC] * scale
    hidden_t = (jax.nn.silu(gate_vals) * up_vals).astype(BF16)
    return stream, hidden_t.T


def solution(mesh):
    placed = (
        P("ctx", "tp"),
        P("ctx", None, "tp"),
        P("ctx", "tp"),
        P("tp"),
        P(None, "tp"),
        P("tp"),
        P("tp", "ctx"),
        P("tp", "ctx"),
    )
    return jax.shard_map(
        shards,
        mesh=mesh,
        in_specs=placed,
        out_specs=(P("ctx", "tp"), P("tp", "ctx")),
        check_vma=False,
    )
```

```python
import functools
import math

import jax
import jax.numpy as jnp
import numpy as np
from jax import lax
from jax.experimental import pallas as pl
from jax.experimental.pallas import tpu as pltpu
from jax.sharding import PartitionSpec as P

F32 = jnp.float32
BF16 = jnp.bfloat16
AXES = ("ctx", "tp")
N_CTX = 16
N_TP = 16
ROWS = 128
CH = 512
SUB = 32
FF_LOC = 1368
FF_PAD = 1376
EPS = 1e-06
NEAR = 5
PLANE_GROUPS = [[xh * 8 + y * 2 + k for xh in range(2) for y in range(4)] for k in range(2)]


def split_index(i):
    c, t = divmod(i, N_TP)
    z, x_lo = divmod(c, 2)
    x_hi, r = divmod(t, 8)
    y, k = divmod(r, 2)
    return z, x_hi * 2 + x_lo, y, k


def join_index(z, x, y, k):
    x = x % 4
    return ((z % 8) * 2 + x % 2) * N_TP + (x // 2) * 8 + (y % 4) * 2 + k % 2


def shift(arr, z=0, x=0, y=0, k=0):
    pairs = []
    for i in range(N_CTX * N_TP):
        az, ax, ay, ak = split_index(i)
        pairs.append((i, join_index(az + z, ax + x, ay + y, ak + k)))
    return lax.ppermute(arr, AXES, pairs)


def split_bf16(table):
    high = np.asarray(table, np.float32).astype(jnp.bfloat16)
    low = (np.asarray(table, np.float32) - high.astype(np.float32)).astype(jnp.bfloat16)
    return high, low


def dft_tables():
    size = 2 * ROWS
    pos = np.arange(ROWS)
    freq = np.arange(ROWS)
    phase = (pos[:, None] * freq[None, :]) % size
    angle = 2.0 * math.pi / size * phase
    cos, sin = np.cos(angle), np.sin(angle)
    sign = np.where(pos % 2 == 0, 1.0, -1.0)
    fwd_im = -sin
    fwd_im[:, 0] = sign
    forward = np.concatenate([cos, fwd_im], axis=1)
    weight = np.where(freq == 0, 1.0, 2.0)[:, None] / size
    inv_re = cos.T * weight
    inv_im = -sin.T * weight
    inv_im[0, :] = sign / size
    inverse = np.concatenate([inv_re, inv_im], axis=0)
    return np.concatenate(split_bf16(forward) + split_bf16(inverse.T), axis=1)


def dot(a, b):
    return jnp.dot(a, b, preferred_element_type=F32)


def dot_nt(a, b):
    return lax.dot_general(a, b, (((1,), (1,)), ((), ())), preferred_element_type=F32)


def prep_kernel(feat_ref, filt_ref, out_ref):
    prod = feat_ref[1].astype(F32) * feat_ref[2].astype(F32)
    filt = filt_ref[...]
    for j in range(CH // 128):
        cols = slice(128 * j, 128 * j + 128)
        out_ref[4 * j : 4 * j + 4, 0:SUB, :] = prod[:, cols].T.astype(BF16).reshape(4, SUB, 128)
        out_ref[4 * j : 4 * j + 4, SUB : 2 * SUB, :] = (
            filt[:, cols].T.astype(BF16).reshape(4, SUB, 128)
        )


def conv_kernel(x_ref, tab_ref, out_ref, spec, filt, outs):
    x = x_ref[...].reshape(N_CTX * 2 * SUB, ROWS)
    spec[...] = (dot(x, tab_ref[:, 0:256]) + dot(x, tab_ref[:, 256:512])).reshape(N_CTX, 2 * SUB, 256)
    lane = lax.broadcasted_iota(jnp.int32, (SUB, 128), 1)
    sign = jnp.where(lane % 2 == 0, 1.0, -1.0).astype(F32)
    first = lane == 0
    for d in range(N_CTX):
        re = spec[d, SUB:, 0:128]
        im = spec[d, SUB:, 128:256]
        if d > 0:
            re = re + sign * spec[d - 1, SUB:, 0:128]
            im = im + sign * spec[d - 1, SUB:, 128:256]
        filt[d, 0] = re
        filt[d, 1] = jnp.where(first, 0.0, im)
        filt[d, 2] = jnp.where(first, im, re)
    for m in range(N_CTX):
        acc_re = jnp.zeros((SUB, 128), F32)
        acc_im = jnp.zeros((SUB, 128), F32)
        for n in range(m + 1):
            pr = spec[n, 0:SUB, 0:128]
            pi = spec[n, 0:SUB, 128:256]
            hr, hz, hq = filt[m - n, 0], filt[m - n, 1], filt[m - n, 2]
            acc_re = acc_re + (pr * hr - pi * hz)
            acc_im = acc_im + (pr * hz + pi * hq)
        outs[m, :, 0:128] = acc_re
        outs[m, :, 128:256] = acc_im
    total = outs[...].reshape(N_CTX * SUB, 256)
    high = total.astype(BF16)
    low = (total - high.astype(F32)).astype(BF16)
    inv_high, inv_low = tab_ref[:, 512:768], tab_ref[:, 768:1024]
    y = dot_nt(high, inv_high) + dot_nt(high, inv_low) + dot_nt(low, inv_high)
    out_ref[...] = y.astype(BF16).reshape(N_CTX, SUB, ROWS)


def mix_kernel(conv_ref, feat_ref, skip_ref, out_ref):
    conv = conv_ref[...].reshape(CH, ROWS).astype(F32)
    for j in range(CH // 128):
        cols = slice(128 * j, 128 * j + 128)
        prod = feat_ref[1, :, cols].astype(F32) * feat_ref[2, :, cols].astype(F32)
        long = conv[cols, :].T
        gate = feat_ref[0, :, cols].astype(F32)
        mixed = (gate * (long + skip_ref[:, cols] * prod)).astype(BF16)
        for copy in range(8):
            out_ref[copy, :, cols] = mixed


def out_proj_kernel(offset, core_ref, mixed_hbm, w_hbm, start_ref, out_ref, mixed, w_buf, sem):
    first = jnp.bitwise_xor(core_ref[0], offset)
    copies = []
    for j in range(N_TP // 2):
        rows = pl.ds(pl.multiple_of((2 * j + first) * CH, CH), CH)
        copies.append(
            (
                pltpu.make_async_copy(mixed_hbm.at[j], mixed.at[j], sem.at[0, j]),
                pltpu.make_async_copy(w_hbm.at[rows], w_buf.at[j], sem.at[1, j]),
            )
        )
    for pair in copies:
        for copy in pair:
            copy.start()
    acc = start_ref[...].astype(F32)
    for j, pair in enumerate(copies):
        for copy in pair:
            copy.wait()
        acc = acc + dot(mixed[j], w_buf[j])
    out_ref[...] = acc.astype(out_ref.dtype)


def square_sums(values):
    ones = jnp.ones((8, CH), BF16)
    sq = values * values
    high = sq.astype(BF16)
    return dot_nt(ones, high) + dot_nt(ones, (sq - high.astype(F32)).astype(BF16))


def two_rows(total):
    high = total.astype(BF16).astype(F32)
    row = lax.broadcasted_iota(jnp.int32, total.shape, 0)
    return jnp.where(row == 0, high, jnp.where(row == 1, total - high, 0.0))


def with_tail(rows, tail):
    return jnp.concatenate([rows, tail], axis=0).astype(BF16)


def scale_kernel(n, *refs):
    blocks, (gain_ref, gain_oth_ref, out_ref, tail_ref) = refs[:-4], refs[-4:]
    halves = []
    for ref in blocks:
        halves += [ref.at[0], ref.at[1]] if len(ref.shape) == 3 else [ref]
    for i in range(n):
        own = halves[2 * i][...].astype(F32)
        oth = halves[2 * i + 1][...].astype(F32)
        out_ref[i, 0] = (own * gain_ref[...]).astype(BF16)
        out_ref[i, 1] = (oth * gain_oth_ref[...]).astype(BF16)
        tail_ref[i] = two_rows(square_sums(own) + square_sums(oth))


def mlp_kernel(groups, with_squares, idx_ref, near_ref, far_ref, near_tail_ref, far_tail_ref, *refs):
    w_ref, wx_ref = refs[:2]
    out_refs = refs[2:-3]
    so, sx, tail = refs[-3:]
    slots = [slot for group in groups for slot in group]
    for at, slot in enumerate(slots):
        which = idx_ref[slot]
        span = slice(at * ROWS, at * ROWS + ROWS)

        @pl.when(which < NEAR)
        def _():
            so[span, :] = near_ref[which, 0]
            sx[span, :] = near_ref[which, 1]
            tail[at] = near_tail_ref[which]

        @pl.when(which >= NEAR)
        def _():
            so[span, :] = far_ref[which - NEAR, 0]
            sx[span, :] = far_ref[which - NEAR, 1]
            tail[at] = far_tail_ref[which - NEAR]

    res = dot_nt(w_ref[...], so[...]) + dot_nt(wx_ref[...], sx[...])
    at = 0
    for group, out_ref in zip(groups, out_refs):
        for i in range(len(group)):
            end = tail[at] if with_squares else jnp.zeros((FF_PAD - FF_LOC, ROWS), F32)
            out_ref[i] = with_tail(res[:, at * ROWS : at * ROWS + ROWS], end)
            at += 1


def params(mib):
    return pltpu.CompilerParams(vmem_limit_bytes=mib * 1024 * 1024)


def pairs_of(rule):
    pairs = []
    for i in range(N_CTX * N_TP):
        target = rule(*split_index(i))
        if target is not None:
            pairs.append((i, join_index(*target)))
    return pairs


def to_row_owner_first(z, x, y, k):
    return (z, x ^ 1, y, k) if k == x % 2 else (z, x, y, k ^ 1)


def to_row_owner_second(z, x, y, k):
    return None if k == x % 2 else (z, x ^ 1, y, k ^ 1)


def in_smem():
    return pl.BlockSpec(memory_space=pltpu.SMEM)


def anywhere():
    return pl.BlockSpec(memory_space=pl.ANY)


def out_proj(offset, core, mixed, w_out, start, dtype):
    return pl.pallas_call(
        functools.partial(out_proj_kernel, offset),
        out_shape=jax.ShapeDtypeStruct((ROWS, CH), dtype),
        in_specs=[
            in_smem(),
            anywhere(),
            pl.BlockSpec(memory_space=pltpu.HBM),
            pl.BlockSpec(memory_space=pltpu.VMEM),
        ],
        scratch_shapes=[
            pltpu.VMEM((N_TP // 2, ROWS, CH), BF16),
            pltpu.VMEM((N_TP // 2, CH, CH), BF16),
            pltpu.SemaphoreType.DMA((2, N_TP // 2)),
        ],
        compiler_params=params(51),
        cost_estimate=pl.CostEstimate(
            flops=2 * ROWS * CH * N_TP // 2 * CH, bytes_accessed=5 << 20, transcendentals=0
        ),
        name="out_proj",
    )(core, mixed, w_out, start)


def scale(blocks, gains, n):
    return pl.pallas_call(
        functools.partial(scale_kernel, n),
        out_shape=[
            jax.ShapeDtypeStruct((n, 2, ROWS, CH), BF16),
            jax.ShapeDtypeStruct((n, 8, ROWS), F32),
        ],
        compiler_params=params(24),
        cost_estimate=pl.CostEstimate(
            flops=8 * n * ROWS * CH * 8, bytes_accessed=n << 19, transcendentals=0
        ),
        name="scale",
    )(*blocks, *gains)


def mlp_part(groups, with_squares, idx, rows, weights):
    n = sum(len(group) for group in groups)
    vmem = pl.BlockSpec(memory_space=pltpu.VMEM)
    return pl.pallas_call(
        functools.partial(mlp_kernel, groups, with_squares),
        out_shape=[jax.ShapeDtypeStruct((len(g), FF_PAD, ROWS), BF16) for g in groups],
        in_specs=[in_smem()] + [vmem] * 6,
        scratch_shapes=[
            pltpu.VMEM((n * ROWS, CH), BF16),
            pltpu.VMEM((n * ROWS, CH), BF16),
            pltpu.VMEM((n, 8, ROWS), F32),
        ],
        compiler_params=params(24),
        cost_estimate=pl.CostEstimate(
            flops=4 * n * ROWS * CH * FF_LOC, bytes_accessed=5 << 20, transcendentals=0
        ),
        name="mlp",
    )(idx, *rows, *weights)


def shards(residual, features, filters, skip_gain, w_out, norm_gain, w_gate, w_up):
    ctx = lax.axis_index("ctx")
    tp = lax.axis_index("tp")
    core, x_lo = tp % 2, ctx % 2
    x_hi, y = tp // 8, (tp // 2) % 4
    feat = features.transpose(1, 0, 2)
    wg, wu = w_gate.T, w_up.T
    gain = norm_gain[None, :]
    wg_oth, wu_oth, gain_oth = shift(wg, k=1), shift(wu, k=1), shift(gain, k=1)

    sent = pl.pallas_call(
        prep_kernel,
        out_shape=jax.ShapeDtypeStruct((N_CTX, 2 * SUB, ROWS), BF16),
        compiler_params=params(56),
        name="prep",
    )(feat, filters)
    recv = lax.all_to_all(sent, "ctx", 0, 0, tiled=True)
    recv, wg_oth, wu_oth, gain_oth = lax.optimization_barrier((recv, wg_oth, wu_oth, gain_oth))
    conv = pl.pallas_call(
        conv_kernel,
        out_shape=jax.ShapeDtypeStruct((N_CTX, SUB, ROWS), BF16),
        scratch_shapes=[
            pltpu.VMEM((N_CTX, 2 * SUB, 256), F32),
            pltpu.VMEM((N_CTX, 3, SUB, 128), F32),
            pltpu.VMEM((N_CTX, SUB, 256), F32),
        ],
        compiler_params=params(56),
        name="conv",
    )(recv, jnp.asarray(dft_tables()))
    conv_rows = lax.all_to_all(conv, "ctx", 0, 0, tiled=True)
    copies = pl.pallas_call(
        mix_kernel,
        out_shape=jax.ShapeDtypeStruct((8, ROWS, CH), BF16),
        compiler_params=params(56),
        name="mix",
    )(conv_rows, feat, skip_gain[None, :])

    mixed = lax.all_to_all(
        copies, "tp", 0, 0, axis_index_groups=PLANE_GROUPS, tiled=True
    )
    mixed_oth = shift(mixed, k=1)
    core_arr = core.astype(jnp.int32)[None]
    half = out_proj(0, core_arr, mixed, w_out, residual, F32)
    stream = out_proj(1, core_arr, mixed_oth, w_out, half, BF16)

    first = lax.ppermute(stream, AXES, pairs_of(to_row_owner_first))
    second = lax.ppermute(stream, AXES, pairs_of(to_row_owner_second))
    here = x_lo == core
    held = jnp.stack([jnp.where(here, stream, first), jnp.where(here, first, second)])
    below, above = [held], [held]
    for step in (2, 1):
        below.insert(1, shift(held, z=step))
        above.insert(1, shift(held, z=-step))
    below.append(shift(below[2], z=1))
    above.append(shift(above[2], z=-1))
    opposite = (shift(below[2][0], z=2), shift(above[2][1], z=-2))
    gains = (gain, gain_oth)
    near, near_tail = scale([held, above[1], above[2], below[2], below[1]], gains, NEAR)
    far, far_tail = scale([above[3], *opposite, below[3]], gains, 8 - NEAR)
    rows = (near, far, near_tail, far_tail)

    z = ctx // 2
    order = []
    for b in range(4):
        for a in range(2):
            d = (4 * ((x_hi + a) % 2) + (y + b) % 4 - z) % 8
            order.append(jnp.where(d <= 2, d, jnp.where(d >= 6, d - 3, d + 2)))
    idx = jnp.stack(order).astype(jnp.int32)
    gate_w, up_w = (wg, wg_oth), (wu, wu_oth)

    def gate_part(*groups):
        return mlp_part(groups, False, idx, rows, gate_w)

    def up_part(*groups):
        return mlp_part(groups, True, idx, rows, up_w)

    def add(*terms):
        total = terms[0].astype(F32)
        for term in terms[1:]:
            total = total + term.astype(F32)
        return total

    (u_plus,) = up_part((4, 3))
    u_plus = shift(u_plus, y=1)
    (u_minus,) = up_part((5, 6))
    u_minus = shift(u_minus, y=-1)
    (g_send_a,) = gate_part((5, 1))
    g_recv_a = shift(g_send_a, x=2)
    (g_send_b,) = gate_part((3, 7))
    g_recv_b = shift(g_send_b, x=2)
    (u_pair,) = up_part((2, 7))
    (g_keep_a,) = gate_part((4, 0))
    (g_keep_b,) = gate_part((2, 6))
    (u_keep,) = up_part((0, 1))
    u_plus_2 = shift(add(u_pair[0], u_plus[0]).astype(BF16), y=1)
    u_minus_2 = shift(add(u_pair[1], u_minus[0]).astype(BF16), y=-1)
    g_last_2 = shift(add(g_keep_a[0], g_recv_a[0]).astype(BF16), y=2)
    g_last_1 = shift(add(g_keep_b[0], g_recv_b[0]).astype(BF16), y=1)
    g_last_3 = shift(add(g_keep_b[1], g_recv_b[1]).astype(BF16), y=-1)
    u_last = shift(add(u_keep[1], u_plus[1], u_minus_2).astype(BF16), x=2)
    up = add(u_keep[0], u_plus_2, u_minus[1], u_last)
    gate = add(g_keep_a[1], g_recv_a[1], g_last_1, g_last_2, g_last_3)
    sums = up[FF_LOC : FF_LOC + 1] + up[FF_LOC + 1 : FF_LOC + 2]
    row_scale = lax.rsqrt(sums * (1.0 / (N_TP * CH)) + EPS)
    gate_vals = gate[:FF_LOC] * row_scale
    up_vals = up[:FF_LOC] * row_scale
    hidden_t = (jax.nn.silu(gate_vals) * up_vals).astype(BF16)
    return stream, hidden_t.T


def solution(mesh):
    placed = (
        P("ctx", "tp"),
        P("ctx", None, "tp"),
        P("ctx", "tp"),
        P("tp"),
        P(None, "tp"),
        P("tp"),
        P("tp", "ctx"),
        P("tp", "ctx"),
    )
    return jax.shard_map(
        shards,
        mesh=mesh,
        in_specs=placed,
        out_specs=(P("ctx", "tp"), P("tp", "ctx")),
        check_vma=False,
    )
```

```python
import functools
import math

import jax
import jax.numpy as jnp
import numpy as np
from jax import lax
from jax.experimental import pallas as pl
from jax.experimental.pallas import tpu as pltpu
from jax.sharding import PartitionSpec as P

F32 = jnp.float32
BF16 = jnp.bfloat16
AXES = ("ctx", "tp")
N_CTX = 16
N_TP = 16
ROWS = 128
CH = 512
SUB = 32
FF_LOC = 1368
FF_PAD = 1376
EPS = 1e-06
NEAR = 5
PLANE_GROUPS = [[xh * 8 + y * 2 + k for xh in range(2) for y in range(4)] for k in range(2)]


def split_index(i):
    c, t = divmod(i, N_TP)
    z, x_lo = divmod(c, 2)
    x_hi, r = divmod(t, 8)
    y, k = divmod(r, 2)
    return z, x_hi * 2 + x_lo, y, k


def join_index(z, x, y, k):
    x = x % 4
    return ((z % 8) * 2 + x % 2) * N_TP + (x // 2) * 8 + (y % 4) * 2 + k % 2


def shift(arr, z=0, x=0, y=0, k=0):
    pairs = []
    for i in range(N_CTX * N_TP):
        az, ax, ay, ak = split_index(i)
        pairs.append((i, join_index(az + z, ax + x, ay + y, ak + k)))
    return lax.ppermute(arr, AXES, pairs)


def split_bf16(table):
    high = np.asarray(table, np.float32).astype(jnp.bfloat16)
    low = (np.asarray(table, np.float32) - high.astype(np.float32)).astype(jnp.bfloat16)
    return high, low


def dft_tables():
    size = 2 * ROWS
    pos = np.arange(ROWS)
    freq = np.arange(ROWS)
    phase = (pos[:, None] * freq[None, :]) % size
    angle = 2.0 * math.pi / size * phase
    cos, sin = np.cos(angle), np.sin(angle)
    sign = np.where(pos % 2 == 0, 1.0, -1.0)
    fwd_im = -sin
    fwd_im[:, 0] = sign
    forward = np.concatenate([cos, fwd_im], axis=1)
    weight = np.where(freq == 0, 1.0, 2.0)[:, None] / size
    inv_re = cos.T * weight
    inv_im = -sin.T * weight
    inv_im[0, :] = sign / size
    inverse = np.concatenate([inv_re, inv_im], axis=0)
    return np.concatenate(split_bf16(forward) + split_bf16(inverse.T), axis=1)


def dot(a, b):
    return jnp.dot(a, b, preferred_element_type=F32)


def dot_nt(a, b):
    return lax.dot_general(a, b, (((1,), (1,)), ((), ())), preferred_element_type=F32)


def prep_kernel(feat_ref, filt_ref, out_ref):
    prod = feat_ref[1].astype(F32) * feat_ref[2].astype(F32)
    filt = filt_ref[...]
    for j in range(CH // 128):
        cols = slice(128 * j, 128 * j + 128)
        out_ref[4 * j : 4 * j + 4, 0:SUB, :] = prod[:, cols].T.astype(BF16).reshape(4, SUB, 128)
        out_ref[4 * j : 4 * j + 4, SUB : 2 * SUB, :] = (
            filt[:, cols].T.astype(BF16).reshape(4, SUB, 128)
        )


def conv_kernel(x_ref, tab_ref, out_ref, spec, filt, outs):
    x = x_ref[...].reshape(N_CTX * 2 * SUB, ROWS)
    spec[...] = (dot(x, tab_ref[:, 0:256]) + dot(x, tab_ref[:, 256:512])).reshape(N_CTX, 2 * SUB, 256)
    lane = lax.broadcasted_iota(jnp.int32, (SUB, 128), 1)
    sign = jnp.where(lane % 2 == 0, 1.0, -1.0).astype(F32)
    first = lane == 0
    for d in range(N_CTX):
        re = spec[d, SUB:, 0:128]
        im = spec[d, SUB:, 128:256]
        if d > 0:
            re = re + sign * spec[d - 1, SUB:, 0:128]
            im = im + sign * spec[d - 1, SUB:, 128:256]
        filt[d, 0] = re
        filt[d, 1] = jnp.where(first, 0.0, im)
        filt[d, 2] = jnp.where(first, im, re)
    for m in range(N_CTX):
        acc_re = jnp.zeros((SUB, 128), F32)
        acc_im = jnp.zeros((SUB, 128), F32)
        for n in range(m + 1):
            pr = spec[n, 0:SUB, 0:128]
            pi = spec[n, 0:SUB, 128:256]
            hr, hz, hq = filt[m - n, 0], filt[m - n, 1], filt[m - n, 2]
            acc_re = acc_re + (pr * hr - pi * hz)
            acc_im = acc_im + (pr * hz + pi * hq)
        outs[m, :, 0:128] = acc_re
        outs[m, :, 128:256] = acc_im
    total = outs[...].reshape(N_CTX * SUB, 256)
    high = total.astype(BF16)
    low = (total - high.astype(F32)).astype(BF16)
    inv_high, inv_low = tab_ref[:, 512:768], tab_ref[:, 768:1024]
    y = dot_nt(high, inv_high) + dot_nt(high, inv_low) + dot_nt(low, inv_high)
    out_ref[...] = y.astype(BF16).reshape(N_CTX, SUB, ROWS)


def mix_kernel(conv_ref, feat_ref, skip_ref, out_ref):
    conv = conv_ref[...].reshape(CH, ROWS).astype(F32)
    for j in range(CH // 128):
        cols = slice(128 * j, 128 * j + 128)
        prod = feat_ref[1, :, cols].astype(F32) * feat_ref[2, :, cols].astype(F32)
        long = conv[cols, :].T
        gate = feat_ref[0, :, cols].astype(F32)
        mixed = (gate * (long + skip_ref[:, cols] * prod)).astype(BF16)
        for copy in range(8):
            out_ref[copy, :, cols] = mixed


def out_proj_kernel(offset, core_ref, mixed_hbm, w_hbm, start_ref, out_ref, mixed, w_buf, sem):
    first = jnp.bitwise_xor(core_ref[0], offset)
    copies = []
    for j in range(N_TP // 2):
        rows = pl.ds(pl.multiple_of((2 * j + first) * CH, CH), CH)
        copies.append(
            (
                pltpu.make_async_copy(mixed_hbm.at[j], mixed.at[j], sem.at[0, j]),
                pltpu.make_async_copy(w_hbm.at[rows], w_buf.at[j], sem.at[1, j]),
            )
        )
    for pair in copies:
        for copy in pair:
            copy.start()
    acc = start_ref[...].astype(F32)
    for j, pair in enumerate(copies):
        for copy in pair:
            copy.wait()
        acc = acc + dot(mixed[j], w_buf[j])
    out_ref[...] = acc.astype(out_ref.dtype)


def square_sums(values):
    ones = jnp.ones((8, CH), BF16)
    sq = values * values
    high = sq.astype(BF16)
    return dot_nt(ones, high) + dot_nt(ones, (sq - high.astype(F32)).astype(BF16))


def two_rows(total):
    high = total.astype(BF16).astype(F32)
    row = lax.broadcasted_iota(jnp.int32, total.shape, 0)
    return jnp.where(row == 0, high, jnp.where(row == 1, total - high, 0.0))


def with_tail(rows, tail):
    return jnp.concatenate([rows, tail], axis=0).astype(BF16)


def scale_kernel(*refs):
    blocks, (gain_ref, gain_oth_ref, out_ref, tail_ref) = refs[:-4], refs[-4:]
    for i, block in enumerate(blocks):
        own = block[0].astype(F32)
        oth = block[1].astype(F32)
        out_ref[i, 0] = (own * gain_ref[...]).astype(BF16)
        out_ref[i, 1] = (oth * gain_oth_ref[...]).astype(BF16)
        tail_ref[i] = two_rows(square_sums(own) + square_sums(oth))


def mlp_kernel(groups, with_squares, idx_ref, near_ref, far_ref, near_tail_ref, far_tail_ref, *refs):
    w_ref, wx_ref = refs[:2]
    out_refs, order_ref = refs[2:-4], refs[-4]
    so, sx, tail = refs[-3:]
    for slot in range(8):
        order_ref[slot] = idx_ref[slot]
    slots = [slot for group in groups for slot in group]
    for at, slot in enumerate(slots):
        which = idx_ref[slot]
        span = slice(at * ROWS, at * ROWS + ROWS)

        @pl.when(which < NEAR)
        def _():
            so[span, :] = near_ref[which, 0]
            sx[span, :] = near_ref[which, 1]
            tail[at] = near_tail_ref[which]

        @pl.when(which >= NEAR)
        def _():
            so[span, :] = far_ref[which - NEAR, 0]
            sx[span, :] = far_ref[which - NEAR, 1]
            tail[at] = far_tail_ref[which - NEAR]

    res = dot_nt(w_ref[...], so[...]) + dot_nt(wx_ref[...], sx[...])
    at = 0
    for group, out_ref in zip(groups, out_refs):
        for i in range(len(group)):
            end = tail[at] if with_squares else jnp.zeros((FF_PAD - FF_LOC, ROWS), F32)
            out_ref[i] = with_tail(res[:, at * ROWS : at * ROWS + ROWS], end)
            at += 1


def params(mib):
    return pltpu.CompilerParams(vmem_limit_bytes=mib * 1024 * 1024)


def pairs_of(rule):
    pairs = []
    for i in range(N_CTX * N_TP):
        target = rule(*split_index(i))
        if target is not None:
            pairs.append((i, join_index(*target)))
    return pairs


def to_row_owner_first(z, x, y, k):
    return (z, x ^ 1, y, k) if k == x % 2 else (z, x, y, k ^ 1)


def to_row_owner_second(z, x, y, k):
    return None if k == x % 2 else (z, x ^ 1, y, k ^ 1)


def in_smem():
    return pl.BlockSpec(memory_space=pltpu.SMEM)


def anywhere():
    return pl.BlockSpec(memory_space=pl.ANY)


def to_opposite(z, x, y, k):
    return (z + 2, x, y, k) if z % 2 == 0 else (z - 2, x, y, k)


def out_proj(offset, core, mixed, w_out, start, dtype):
    return pl.pallas_call(
        functools.partial(out_proj_kernel, offset),
        out_shape=jax.ShapeDtypeStruct((ROWS, CH), dtype),
        in_specs=[
            in_smem(),
            anywhere(),
            pl.BlockSpec(memory_space=pltpu.HBM),
            pl.BlockSpec(memory_space=pltpu.VMEM),
        ],
        scratch_shapes=[
            pltpu.VMEM((N_TP // 2, ROWS, CH), BF16),
            pltpu.VMEM((N_TP // 2, CH, CH), BF16),
            pltpu.SemaphoreType.DMA((2, N_TP // 2)),
        ],
        compiler_params=params(51),
        cost_estimate=pl.CostEstimate(
            flops=2 * ROWS * CH * N_TP // 2 * CH, bytes_accessed=5 << 20, transcendentals=0
        ),
        name="out_proj",
    )(core, mixed, w_out, start)


def scale(blocks, gains):
    n = len(blocks)
    return pl.pallas_call(
        scale_kernel,
        out_shape=[
            jax.ShapeDtypeStruct((n, 2, ROWS, CH), BF16),
            jax.ShapeDtypeStruct((n, 8, ROWS), F32),
        ],
        compiler_params=params(14),
        cost_estimate=pl.CostEstimate(
            flops=8 * n * ROWS * CH * 8, bytes_accessed=n << 19, transcendentals=0
        ),
        name="scale",
    )(*blocks, *gains)


def mlp_part(groups, with_squares, idx, rows, weights):
    n = sum(len(group) for group in groups)
    vmem = pl.BlockSpec(memory_space=pltpu.VMEM)
    return pl.pallas_call(
        functools.partial(mlp_kernel, groups, with_squares),
        out_shape=[jax.ShapeDtypeStruct((len(g), FF_PAD, ROWS), BF16) for g in groups]
        + [jax.ShapeDtypeStruct((8,), jnp.int32)],
        in_specs=[in_smem()] + [vmem] * 6,
        out_specs=[vmem] * len(groups) + [in_smem()],
        scratch_shapes=[
            pltpu.VMEM((n * ROWS, CH), BF16),
            pltpu.VMEM((n * ROWS, CH), BF16),
            pltpu.VMEM((n, 8, ROWS), F32),
        ],
        compiler_params=params(18),
        cost_estimate=pl.CostEstimate(
            flops=10**8, bytes_accessed=1 << 19, transcendentals=0
        ),
        name="mlp",
    )(idx, *rows, *weights)


def shards(residual, features, filters, skip_gain, w_out, norm_gain, w_gate, w_up):
    ctx = lax.axis_index("ctx")
    tp = lax.axis_index("tp")
    core, x_lo = tp % 2, ctx % 2
    x_hi, y = tp // 8, (tp // 2) % 4
    feat = features.transpose(1, 0, 2)
    wg, wu = w_gate.T, w_up.T
    gain = norm_gain[None, :]
    wg_oth, wu_oth, gain_oth = shift(wg, k=1), shift(wu, k=1), shift(gain, k=1)

    sent = pl.pallas_call(
        prep_kernel,
        out_shape=jax.ShapeDtypeStruct((N_CTX, 2 * SUB, ROWS), BF16),
        compiler_params=params(56),
        name="prep",
    )(feat, filters)
    recv = lax.all_to_all(sent, "ctx", 0, 0, tiled=True)
    recv, wg_oth, wu_oth, gain_oth = lax.optimization_barrier((recv, wg_oth, wu_oth, gain_oth))
    conv = pl.pallas_call(
        conv_kernel,
        out_shape=jax.ShapeDtypeStruct((N_CTX, SUB, ROWS), BF16),
        scratch_shapes=[
            pltpu.VMEM((N_CTX, 2 * SUB, 256), F32),
            pltpu.VMEM((N_CTX, 3, SUB, 128), F32),
            pltpu.VMEM((N_CTX, SUB, 256), F32),
        ],
        compiler_params=params(14),
        name="conv",
    )(recv, jnp.asarray(dft_tables()))
    conv_rows = lax.all_to_all(conv, "ctx", 0, 0, tiled=True)
    copies = pl.pallas_call(
        mix_kernel,
        out_shape=jax.ShapeDtypeStruct((8, ROWS, CH), BF16),
        compiler_params=params(56),
        name="mix",
    )(conv_rows, feat, skip_gain[None, :])

    mixed = lax.all_to_all(
        copies, "tp", 0, 0, axis_index_groups=PLANE_GROUPS, tiled=True
    )
    mixed_oth = shift(mixed, k=1)
    core_arr = core.astype(jnp.int32)[None]
    half = out_proj(0, core_arr, mixed, w_out, residual, F32)
    stream = out_proj(1, core_arr, mixed_oth, w_out, half, BF16)

    first = lax.ppermute(stream, AXES, pairs_of(to_row_owner_first))
    second = lax.ppermute(stream, AXES, pairs_of(to_row_owner_second))
    here = x_lo == core
    held = jnp.stack([jnp.where(here, stream, first), jnp.where(here, first, second)])
    below, above = [held], [held]
    for step in (2, 1):
        below.insert(1, shift(held, z=step))
        above.insert(1, shift(held, z=-step))
    below.append(shift(below[2], z=1))
    above.append(shift(above[2], z=-1))
    z = ctx // 2
    onward = jnp.where(z % 2 == 0, below[2], above[2])
    opposite = lax.ppermute(onward, AXES, pairs_of(to_opposite))
    gains = (gain, gain_oth)
    near, near_tail = scale([held, above[1], above[2], below[2], below[1]], gains)
    far, far_tail = scale([above[3], opposite, below[3]], gains)
    rows = (near, far, near_tail, far_tail)

    order = []
    for b in range(4):
        for a in range(2):
            d = (4 * ((x_hi + a) % 2) + (y + b) % 4 - z) % 8
            order.append(jnp.where(d <= 2, d, jnp.where(d >= 6, d - 3, d + 2)))
    idx = jnp.stack(order).astype(jnp.int32)
    gate_w, up_w = (wg, wg_oth), (wu, wu_oth)

    def gate_part(order, *groups):
        *outs, token = mlp_part(groups, False, order, rows, gate_w)
        return outs + [token]

    def up_part(order, *groups):
        *outs, token = mlp_part(groups, True, order, rows, up_w)
        return outs + [token]

    def add(*terms):
        total = terms[0].astype(F32)
        for term in terms[1:]:
            total = total + term.astype(F32)
        return total

    u_two, _ = up_part(idx, (4, 5))
    g_send_a, _ = gate_part(idx, (5, 1))
    u_one, _ = up_part(idx, (2, 3))
    u_three, _ = up_part(idx, (6, 7))
    g_send_b, then = gate_part(idx, (3, 7))
    u_two = shift(u_two, y=2)
    g_recv_a = shift(g_send_a, x=2)
    u_one = shift(u_one, y=1)
    u_three = shift(u_three, y=-1)
    g_recv_b = shift(g_send_b, x=2)
    g_keep_a, _ = gate_part(then, (4, 0))
    g_keep_b, _ = gate_part(then, (2, 6))
    u_keep, _ = up_part(then, (0, 1))
    g_last_2 = shift(add(g_keep_a[0], g_recv_a[0]).astype(BF16), y=2)
    g_last_1 = shift(add(g_keep_b[0], g_recv_b[0]).astype(BF16), y=1)
    g_last_3 = shift(add(g_keep_b[1], g_recv_b[1]).astype(BF16), y=-1)
    u_last = shift(add(u_keep[1], u_one[1], u_two[1], u_three[1]).astype(BF16), x=2)
    up = add(u_keep[0], u_one[0], u_two[0], u_three[0], u_last)
    gate = add(g_keep_a[1], g_recv_a[1], g_last_1, g_last_2, g_last_3)
    sums = up[FF_LOC : FF_LOC + 1] + up[FF_LOC + 1 : FF_LOC + 2]
    row_scale = lax.rsqrt(sums * (1.0 / (N_TP * CH)) + EPS)
    gate_vals = gate[:FF_LOC] * row_scale
    up_vals = up[:FF_LOC] * row_scale
    hidden_t = (jax.nn.silu(gate_vals) * up_vals).astype(BF16)
    return stream, hidden_t.T


def solution(mesh):
    placed = (
        P("ctx", "tp"),
        P("ctx", None, "tp"),
        P("ctx", "tp"),
        P("tp"),
        P(None, "tp"),
        P("tp"),
        P("tp", "ctx"),
        P("tp", "ctx"),
    )
    return jax.shard_map(
        shards,
        mesh=mesh,
        in_specs=placed,
        out_specs=(P("ctx", "tp"), P("tp", "ctx")),
        check_vma=False,
    )
```

```python
import functools
import math

import jax
import jax.numpy as jnp
import numpy as np
from jax import lax
from jax.experimental import pallas as pl
from jax.experimental.pallas import tpu as pltpu
from jax.sharding import PartitionSpec as P

F32 = jnp.float32
BF16 = jnp.bfloat16
AXES = ("ctx", "tp")
N_CTX = 16
N_TP = 16
ROWS = 128
CH = 512
SUB = 32
FF_LOC = 1368
FF_PAD = 1376
EPS = 1e-06
NEAR = 5
PLANE_GROUPS = [[xh * 8 + y * 2 + k for xh in range(2) for y in range(4)] for k in range(2)]


def split_index(i):
    c, t = divmod(i, N_TP)
    z, x_lo = divmod(c, 2)
    x_hi, r = divmod(t, 8)
    y, k = divmod(r, 2)
    return z, x_hi * 2 + x_lo, y, k


def join_index(z, x, y, k):
    x = x % 4
    return ((z % 8) * 2 + x % 2) * N_TP + (x // 2) * 8 + (y % 4) * 2 + k % 2


def shift(arr, z=0, x=0, y=0, k=0):
    pairs = []
    for i in range(N_CTX * N_TP):
        az, ax, ay, ak = split_index(i)
        pairs.append((i, join_index(az + z, ax + x, ay + y, ak + k)))
    return lax.ppermute(arr, AXES, pairs)


def split_bf16(table):
    high = np.asarray(table, np.float32).astype(jnp.bfloat16)
    low = (np.asarray(table, np.float32) - high.astype(np.float32)).astype(jnp.bfloat16)
    return high, low


def dft_tables():
    size = 2 * ROWS
    pos = np.arange(ROWS)
    freq = np.arange(ROWS)
    phase = (pos[:, None] * freq[None, :]) % size
    angle = 2.0 * math.pi / size * phase
    cos, sin = np.cos(angle), np.sin(angle)
    sign = np.where(pos % 2 == 0, 1.0, -1.0)
    fwd_im = -sin
    fwd_im[:, 0] = sign
    forward = np.concatenate([cos, fwd_im], axis=1)
    weight = np.where(freq == 0, 1.0, 2.0)[:, None] / size
    inv_re = cos.T * weight
    inv_im = -sin.T * weight
    inv_im[0, :] = sign / size
    inverse = np.concatenate([inv_re, inv_im], axis=0)
    return np.concatenate(split_bf16(forward) + split_bf16(inverse.T), axis=1)


def dot(a, b):
    return jnp.dot(a, b, preferred_element_type=F32)


def dot_nt(a, b):
    return lax.dot_general(a, b, (((1,), (1,)), ((), ())), preferred_element_type=F32)


def prep_kernel(feat_ref, filt_ref, out_ref):
    prod = feat_ref[1].astype(F32) * feat_ref[2].astype(F32)
    filt = filt_ref[...]
    for j in range(CH // 128):
        cols = slice(128 * j, 128 * j + 128)
        out_ref[4 * j : 4 * j + 4, 0:SUB, :] = prod[:, cols].T.astype(BF16).reshape(4, SUB, 128)
        out_ref[4 * j : 4 * j + 4, SUB : 2 * SUB, :] = (
            filt[:, cols].T.astype(BF16).reshape(4, SUB, 128)
        )


def conv_kernel(x_ref, tab_ref, out_ref, spec, filt, outs):
    x = x_ref[...].reshape(N_CTX * 2 * SUB, ROWS)
    spec[...] = (dot(x, tab_ref[:, 0:256]) + dot(x, tab_ref[:, 256:512])).reshape(N_CTX, 2 * SUB, 256)
    lane = lax.broadcasted_iota(jnp.int32, (SUB, 128), 1)
    sign = jnp.where(lane % 2 == 0, 1.0, -1.0).astype(F32)
    first = lane == 0
    for d in range(N_CTX):
        re = spec[d, SUB:, 0:128]
        im = spec[d, SUB:, 128:256]
        if d > 0:
            re = re + sign * spec[d - 1, SUB:, 0:128]
            im = im + sign * spec[d - 1, SUB:, 128:256]
        filt[d, 0] = re
        filt[d, 1] = jnp.where(first, 0.0, im)
        filt[d, 2] = jnp.where(first, im, re)
    for m in range(N_CTX):
        acc_re = jnp.zeros((SUB, 128), F32)
        acc_im = jnp.zeros((SUB, 128), F32)
        for n in range(m + 1):
            pr = spec[n, 0:SUB, 0:128]
            pi = spec[n, 0:SUB, 128:256]
            hr, hz, hq = filt[m - n, 0], filt[m - n, 1], filt[m - n, 2]
            acc_re = acc_re + (pr * hr - pi * hz)
            acc_im = acc_im + (pr * hz + pi * hq)
        outs[m, :, 0:128] = acc_re
        outs[m, :, 128:256] = acc_im
    total = outs[...].reshape(N_CTX * SUB, 256)
    high = total.astype(BF16)
    low = (total - high.astype(F32)).astype(BF16)
    inv_high, inv_low = tab_ref[:, 512:768], tab_ref[:, 768:1024]
    y = dot_nt(high, inv_high) + dot_nt(high, inv_low) + dot_nt(low, inv_high)
    out_ref[...] = y.astype(BF16).reshape(N_CTX, SUB, ROWS)


def mix_kernel(conv_ref, feat_ref, skip_ref, out_ref):
    conv = conv_ref[...].reshape(CH, ROWS).astype(F32)
    for j in range(CH // 128):
        cols = slice(128 * j, 128 * j + 128)
        prod = feat_ref[1, :, cols].astype(F32) * feat_ref[2, :, cols].astype(F32)
        long = conv[cols, :].T
        gate = feat_ref[0, :, cols].astype(F32)
        mixed = (gate * (long + skip_ref[:, cols] * prod)).astype(BF16)
        for copy in range(8):
            out_ref[copy, :, cols] = mixed


def out_proj_kernel(offset, core_ref, mixed_hbm, w_hbm, start_ref, out_ref, mixed, w_buf, sem):
    first = jnp.bitwise_xor(core_ref[0], offset)
    copies = []
    for j in range(N_TP // 2):
        rows = pl.ds(pl.multiple_of((2 * j + first) * CH, CH), CH)
        copies.append(
            (
                pltpu.make_async_copy(mixed_hbm.at[j], mixed.at[j], sem.at[0, j]),
                pltpu.make_async_copy(w_hbm.at[rows], w_buf.at[j], sem.at[1, j]),
            )
        )
    for pair in copies:
        for copy in pair:
            copy.start()
    acc = start_ref[...].astype(F32)
    for j, pair in enumerate(copies):
        for copy in pair:
            copy.wait()
        acc = acc + dot(mixed[j], w_buf[j])
    out_ref[...] = acc.astype(out_ref.dtype)


def square_sums(values):
    ones = jnp.ones((8, CH), BF16)
    sq = values * values
    high = sq.astype(BF16)
    return dot_nt(ones, high) + dot_nt(ones, (sq - high.astype(F32)).astype(BF16))


def two_rows(total):
    high = total.astype(BF16).astype(F32)
    row = lax.broadcasted_iota(jnp.int32, total.shape, 0)
    return jnp.where(row == 0, high, jnp.where(row == 1, total - high, 0.0))


def with_tail(rows, tail):
    return jnp.concatenate([rows, tail], axis=0).astype(BF16)


def load_kernel(wg_ref, wgx_ref, wu_ref, wux_ref, mark_ref, gate_ref, up_ref, out_mark_ref, sem):
    copies = []
    pieces = ((wg_ref, gate_ref, 0), (wgx_ref, gate_ref, CH), (wu_ref, up_ref, 0), (wux_ref, up_ref, CH))
    for i, (src, dst, at) in enumerate(pieces):
        copies.append(pltpu.make_async_copy(src, dst.at[:, pl.ds(at, CH)], sem.at[i]))
        copies[-1].start()
    for copy in copies:
        copy.wait()
    out_mark_ref[...] = mark_ref[...]


def scale_kernel(*refs):
    blocks, (gain_ref, gain_oth_ref, out_ref, tail_ref) = refs[:-4], refs[-4:]
    for i, block in enumerate(blocks):
        own = block[0].astype(F32)
        oth = block[1].astype(F32)
        out_ref[i, :, 0:CH] = (own * gain_ref[...]).astype(BF16)
        out_ref[i, :, CH:] = (oth * gain_oth_ref[...]).astype(BF16)
        tail_ref[i] = two_rows(square_sums(own) + square_sums(oth))


def mlp_kernel(slots, idx_ref, *refs):
    rows, (gate_ref, up_ref) = refs[:8], refs[8:10]
    out_refs, order_ref = refs[10:-3], refs[-3]
    scaled, tail = refs[-2:]
    for slot in range(8):
        order_ref[slot] = idx_ref[slot]
    for at, slot in enumerate(slots):
        which = idx_ref[slot]
        span = slice(at * ROWS, at * ROWS + ROWS)

        @pl.when(which < NEAR)
        def _():
            scaled[span, :] = rows[0][which]
            tail[at] = rows[1][which]

        for i in range(3):

            @pl.when(which == NEAR + i)
            def _():
                scaled[span, :] = rows[2 + 2 * i][0]
                tail[at] = rows[3 + 2 * i][0]

    zeros = jnp.zeros((FF_PAD - FF_LOC, ROWS), F32)
    gate = dot_nt(gate_ref[...], scaled[...])
    for at, out_ref in enumerate(out_refs):
        out_ref[0] = with_tail(gate[:, at * ROWS : at * ROWS + ROWS], zeros)
    up = dot_nt(up_ref[...], scaled[...])
    for at, out_ref in enumerate(out_refs):
        out_ref[1] = with_tail(up[:, at * ROWS : at * ROWS + ROWS], tail[at])


def sum_kernel(*refs):
    total = refs[0][...].astype(F32)
    for ref in refs[1:-1]:
        total = total + ref[...].astype(F32)
    refs[-1][...] = total.astype(BF16)


def finish_kernel(*refs):
    gate = refs[0][0].astype(F32)
    up = refs[0][1].astype(F32)
    for ref in refs[1:-1]:
        gate = gate + ref[0].astype(F32)
        up = up + ref[1].astype(F32)
    sums = up[FF_LOC : FF_LOC + 1] + up[FF_LOC + 1 : FF_LOC + 2]
    scale = lax.rsqrt(sums * (1.0 / (N_TP * CH)) + EPS)
    gate = gate[:FF_LOC] * scale
    refs[-1][...] = (gate / (1.0 + jnp.exp(-gate)) * (up[:FF_LOC] * scale)).astype(BF16)


def params(mib):
    return pltpu.CompilerParams(vmem_limit_bytes=mib * 1024 * 1024)


def pairs_of(rule):
    pairs = []
    for i in range(N_CTX * N_TP):
        target = rule(*split_index(i))
        if target is not None:
            pairs.append((i, join_index(*target)))
    return pairs


def to_row_owner_first(z, x, y, k):
    return (z, x ^ 1, y, k) if k == x % 2 else (z, x, y, k ^ 1)


def to_row_owner_second(z, x, y, k):
    return None if k == x % 2 else (z, x ^ 1, y, k ^ 1)


def in_smem():
    return pl.BlockSpec(memory_space=pltpu.SMEM)


def anywhere():
    return pl.BlockSpec(memory_space=pl.ANY)


def to_opposite(z, x, y, k):
    return (z + 2, x, y, k) if z % 2 == 0 else (z - 2, x, y, k)


def out_proj(offset, core, mixed, w_out, start, dtype):
    return pl.pallas_call(
        functools.partial(out_proj_kernel, offset),
        out_shape=jax.ShapeDtypeStruct((ROWS, CH), dtype),
        in_specs=[
            in_smem(),
            anywhere(),
            pl.BlockSpec(memory_space=pltpu.HBM),
            pl.BlockSpec(memory_space=pltpu.VMEM),
        ],
        scratch_shapes=[
            pltpu.VMEM((N_TP // 2, ROWS, CH), BF16),
            pltpu.VMEM((N_TP // 2, CH, CH), BF16),
            pltpu.SemaphoreType.DMA((2, N_TP // 2)),
        ],
        compiler_params=params(51),
        cost_estimate=pl.CostEstimate(
            flops=2 * ROWS * CH * N_TP // 2 * CH, bytes_accessed=5 << 20, transcendentals=0
        ),
        name="out_proj",
    )(core, mixed, w_out, start)


def load_weights(weights, mark):
    vmem = pl.BlockSpec(memory_space=pltpu.VMEM)
    return pl.pallas_call(
        load_kernel,
        out_shape=[jax.ShapeDtypeStruct((FF_LOC, 2 * CH), BF16)] * 2
        + [jax.ShapeDtypeStruct(mark.shape, mark.dtype)],
        in_specs=[anywhere()] * 4 + [vmem],
        out_specs=[vmem] * 3,
        scratch_shapes=[pltpu.SemaphoreType.DMA((4,))],
        compiler_params=params(16),
        cost_estimate=pl.CostEstimate(flops=1, bytes_accessed=12 << 20, transcendentals=0),
        name="load",
    )(*weights, mark)


def scale(blocks, gains):
    n = len(blocks)
    return pl.pallas_call(
        scale_kernel,
        out_shape=[
            jax.ShapeDtypeStruct((n, ROWS, 2 * CH), BF16),
            jax.ShapeDtypeStruct((n, 8, ROWS), F32),
        ],
        compiler_params=params(14),
        cost_estimate=pl.CostEstimate(
            flops=8 * n * ROWS * CH * 8, bytes_accessed=n << 19, transcendentals=0
        ),
        name="scale",
    )(*blocks, *gains)


def mlp_part(slots, idx, rows, weights):
    n = len(slots)
    vmem = pl.BlockSpec(memory_space=pltpu.VMEM)
    *outs, token = pl.pallas_call(
        functools.partial(mlp_kernel, slots),
        out_shape=[jax.ShapeDtypeStruct((2, FF_PAD, ROWS), BF16)] * n
        + [jax.ShapeDtypeStruct((8,), jnp.int32)],
        in_specs=[in_smem()] + [vmem] * 10,
        out_specs=[vmem] * n + [in_smem()],
        scratch_shapes=[
            pltpu.VMEM((n * ROWS, 2 * CH), BF16),
            pltpu.VMEM((n, 8, ROWS), F32),
        ],
        compiler_params=params(18),
        cost_estimate=pl.CostEstimate(
            flops=10**8, bytes_accessed=1 << 19, transcendentals=0
        ),
        name="mlp",
    )(idx, *rows, *weights)
    return outs, token


def in_vmem_call(kernel, shape, name, parts):
    vmem = pl.BlockSpec(memory_space=pltpu.VMEM)
    return pl.pallas_call(
        kernel,
        out_shape=jax.ShapeDtypeStruct(shape, BF16),
        in_specs=[vmem] * len(parts),
        out_specs=vmem,
        compiler_params=params(16),
        cost_estimate=pl.CostEstimate(flops=1, bytes_accessed=1 << 19, transcendentals=0),
        name=name,
    )(*parts)


def shards(residual, features, filters, skip_gain, w_out, norm_gain, w_gate, w_up):
    ctx = lax.axis_index("ctx")
    tp = lax.axis_index("tp")
    core, x_lo = tp % 2, ctx % 2
    x_hi, y = tp // 8, (tp // 2) % 4
    feat = features.transpose(1, 0, 2)
    wg, wu = w_gate.T, w_up.T
    gain = norm_gain[None, :]
    wg_oth, wu_oth, gain_oth = shift(wg, k=1), shift(wu, k=1), shift(gain, k=1)

    sent = pl.pallas_call(
        prep_kernel,
        out_shape=jax.ShapeDtypeStruct((N_CTX, 2 * SUB, ROWS), BF16),
        compiler_params=params(56),
        name="prep",
    )(feat, filters)
    recv = lax.all_to_all(sent, "ctx", 0, 0, tiled=True)
    recv, wg_oth, wu_oth, gain_oth = lax.optimization_barrier((recv, wg_oth, wu_oth, gain_oth))
    conv = pl.pallas_call(
        conv_kernel,
        out_shape=jax.ShapeDtypeStruct((N_CTX, SUB, ROWS), BF16),
        scratch_shapes=[
            pltpu.VMEM((N_CTX, 2 * SUB, 256), F32),
            pltpu.VMEM((N_CTX, 3, SUB, 128), F32),
            pltpu.VMEM((N_CTX, SUB, 256), F32),
        ],
        compiler_params=params(14),
        name="conv",
    )(recv, jnp.asarray(dft_tables()))
    conv_rows = lax.all_to_all(conv, "ctx", 0, 0, tiled=True)
    copies = pl.pallas_call(
        mix_kernel,
        out_shape=jax.ShapeDtypeStruct((8, ROWS, CH), BF16),
        compiler_params=params(56),
        name="mix",
    )(conv_rows, feat, skip_gain[None, :])

    mixed = lax.all_to_all(
        copies, "tp", 0, 0, axis_index_groups=PLANE_GROUPS, tiled=True
    )
    mixed_oth = shift(mixed, k=1)
    core_arr = core.astype(jnp.int32)[None]
    half = out_proj(0, core_arr, mixed, w_out, residual, F32)
    stream = out_proj(1, core_arr, mixed_oth, w_out, half, BF16)

    first = lax.ppermute(stream, AXES, pairs_of(to_row_owner_first))
    second = lax.ppermute(stream, AXES, pairs_of(to_row_owner_second))
    here = x_lo == core
    held = jnp.stack([jnp.where(here, stream, first), jnp.where(here, first, second)])
    gate_w, up_w, mark = load_weights((wg, wg_oth, wu, wu_oth), held[0, :16])
    gain, _ = lax.optimization_barrier((gain, mark))
    below, above = [held], [held]
    for step in (2, 1):
        below.insert(1, shift(held, z=step))
        above.insert(1, shift(held, z=-step))
    below.append(shift(below[2], z=1))
    above.append(shift(above[2], z=-1))
    z = ctx // 2
    onward = jnp.where(z % 2 == 0, below[2], above[2])
    opposite = lax.ppermute(onward, AXES, pairs_of(to_opposite))
    gains = (gain, gain_oth)
    rows = scale([held, above[1], above[2], below[2], below[1]], gains)
    for block in (above[3], opposite, below[3]):
        rows = rows + scale([block], gains)

    order = []
    for b in range(4):
        for a in range(2):
            d = (4 * ((x_hi + a) % 2) + (y + b) % 4 - z) % 8
            order.append(jnp.where(d <= 2, d, jnp.where(d >= 6, d - 3, d + 2)))
    idx = jnp.stack(order).astype(jnp.int32)

    weights = (gate_w, up_w)
    shape = (2, FF_PAD, ROWS)
    (one_far, three_far), then = mlp_part((3, 7), idx, rows, weights)
    (two_far,), then = mlp_part((5,), then, rows, weights)
    (one_near, three_near), then = mlp_part((2, 6), then, rows, weights)
    (two_near, own_far), then = mlp_part((4, 1), then, rows, weights)
    (own_near,), _ = mlp_part((0,), then, rows, weights)
    one_far = shift(one_far, y=1)
    three_far = shift(three_far, y=-1)
    two_far = shift(two_far, x=2)
    one_near = shift(one_near, y=1)
    three_near = shift(three_near, y=-1)
    across = in_vmem_call(sum_kernel, shape, "sum", (own_far, one_far, three_far))
    two_near = in_vmem_call(sum_kernel, shape, "sum", (two_near, two_far))
    across = shift(across, x=2)
    two_near = shift(two_near, y=2)
    hidden_t = in_vmem_call(
        finish_kernel,
        (FF_LOC, ROWS),
        "finish",
        (own_near, one_near, three_near, across, two_near),
    )
    return stream, hidden_t.T


def solution(mesh):
    placed = (
        P("ctx", "tp"),
        P("ctx", None, "tp"),
        P("ctx", "tp"),
        P("tp"),
        P(None, "tp"),
        P("tp"),
        P("tp", "ctx"),
        P("tp", "ctx"),
    )
    return jax.shard_map(
        shards,
        mesh=mesh,
        in_specs=placed,
        out_specs=(P("ctx", "tp"), P("tp", "ctx")),
        check_vma=False,
    )
```

```python
import functools
import math

import jax
import jax.numpy as jnp
import numpy as np
from jax import lax
from jax.experimental import pallas as pl
from jax.experimental.pallas import tpu as pltpu
from jax.sharding import PartitionSpec as P

F32 = jnp.float32
BF16 = jnp.bfloat16
AXES = ("ctx", "tp")
N_CTX = 16
N_TP = 16
ROWS = 128
CH = 512
SUB = 32
FF_LOC = 1368
FF_PAD = 1376
EPS = 1e-06
NEAR = 5
ROW_OF = (0, 2, 3, 6, 7, 5, 4, 1)
PLANE_GROUPS = [[xh * 8 + y * 2 + k for xh in range(2) for y in range(4)] for k in range(2)]


def split_index(i):
    c, t = divmod(i, N_TP)
    z, x_lo = divmod(c, 2)
    x_hi, r = divmod(t, 8)
    y, k = divmod(r, 2)
    return z, x_hi * 2 + x_lo, y, k


def join_index(z, x, y, k):
    x = x % 4
    return ((z % 8) * 2 + x % 2) * N_TP + (x // 2) * 8 + (y % 4) * 2 + k % 2


def shift(arr, z=0, x=0, y=0, k=0):
    pairs = []
    for i in range(N_CTX * N_TP):
        az, ax, ay, ak = split_index(i)
        pairs.append((i, join_index(az + z, ax + x, ay + y, ak + k)))
    return lax.ppermute(arr, AXES, pairs)


def split_bf16(table):
    high = np.asarray(table, np.float32).astype(jnp.bfloat16)
    low = (np.asarray(table, np.float32) - high.astype(np.float32)).astype(jnp.bfloat16)
    return high, low


def dft_tables():
    size = 2 * ROWS
    pos = np.arange(ROWS)
    freq = np.arange(ROWS)
    phase = (pos[:, None] * freq[None, :]) % size
    angle = 2.0 * math.pi / size * phase
    cos, sin = np.cos(angle), np.sin(angle)
    sign = np.where(pos % 2 == 0, 1.0, -1.0)
    fwd_im = -sin
    fwd_im[:, 0] = sign
    forward = np.concatenate([cos, fwd_im], axis=1)
    weight = np.where(freq == 0, 1.0, 2.0)[:, None] / size
    inv_re = cos.T * weight
    inv_im = -sin.T * weight
    inv_im[0, :] = sign / size
    inverse = np.concatenate([inv_re, inv_im], axis=0)
    return np.concatenate(split_bf16(forward) + split_bf16(inverse.T), axis=1)


def dot(a, b):
    return jnp.dot(a, b, preferred_element_type=F32)


def dot_nt(a, b):
    return lax.dot_general(a, b, (((1,), (1,)), ((), ())), preferred_element_type=F32)


def prep_kernel(feat_ref, filt_ref, out_ref):
    prod = feat_ref[1].astype(F32) * feat_ref[2].astype(F32)
    filt = filt_ref[...]
    for j in range(CH // 128):
        cols = slice(128 * j, 128 * j + 128)
        out_ref[4 * j : 4 * j + 4, 0:SUB, :] = prod[:, cols].T.astype(BF16).reshape(4, SUB, 128)
        out_ref[4 * j : 4 * j + 4, SUB : 2 * SUB, :] = (
            filt[:, cols].T.astype(BF16).reshape(4, SUB, 128)
        )


def conv_kernel(x_ref, tab_ref, out_ref, spec, filt, outs):
    x = x_ref[...].reshape(N_CTX * 2 * SUB, ROWS)
    spec[...] = (dot(x, tab_ref[:, 0:256]) + dot(x, tab_ref[:, 256:512])).reshape(N_CTX, 2 * SUB, 256)
    lane = lax.broadcasted_iota(jnp.int32, (SUB, 128), 1)
    sign = jnp.where(lane % 2 == 0, 1.0, -1.0).astype(F32)
    first = lane == 0
    for d in range(N_CTX):
        re = spec[d, SUB:, 0:128]
        im = spec[d, SUB:, 128:256]
        if d > 0:
            re = re + sign * spec[d - 1, SUB:, 0:128]
            im = im + sign * spec[d - 1, SUB:, 128:256]
        filt[d, 0] = re
        filt[d, 1] = jnp.where(first, 0.0, im)
        filt[d, 2] = jnp.where(first, im, re)
    for m in range(N_CTX):
        acc_re = jnp.zeros((SUB, 128), F32)
        acc_im = jnp.zeros((SUB, 128), F32)
        for n in range(m + 1):
            pr = spec[n, 0:SUB, 0:128]
            pi = spec[n, 0:SUB, 128:256]
            hr, hz, hq = filt[m - n, 0], filt[m - n, 1], filt[m - n, 2]
            acc_re = acc_re + (pr * hr - pi * hz)
            acc_im = acc_im + (pr * hz + pi * hq)
        outs[m, :, 0:128] = acc_re
        outs[m, :, 128:256] = acc_im
    total = outs[...].reshape(N_CTX * SUB, 256)
    high = total.astype(BF16)
    low = (total - high.astype(F32)).astype(BF16)
    inv_high, inv_low = tab_ref[:, 512:768], tab_ref[:, 768:1024]
    y = dot_nt(high, inv_high) + dot_nt(high, inv_low) + dot_nt(low, inv_high)
    out_ref[...] = y.astype(BF16).reshape(N_CTX, SUB, ROWS)


def mix_kernel(conv_ref, feat_ref, skip_ref, out_ref):
    conv = conv_ref[...].reshape(CH, ROWS).astype(F32)
    for j in range(CH // 128):
        cols = slice(128 * j, 128 * j + 128)
        prod = feat_ref[1, :, cols].astype(F32) * feat_ref[2, :, cols].astype(F32)
        long = conv[cols, :].T
        gate = feat_ref[0, :, cols].astype(F32)
        mixed = (gate * (long + skip_ref[:, cols] * prod)).astype(BF16)
        for copy in range(8):
            out_ref[copy, :, cols] = mixed


def out_proj_kernel(offset, core_ref, mixed_hbm, w_hbm, start_ref, out_ref, mixed, w_buf, sem):
    first = jnp.bitwise_xor(core_ref[0], offset)
    copies = []
    for j in range(N_TP // 2):
        rows = pl.ds(pl.multiple_of((2 * j + first) * CH, CH), CH)
        copies.append(
            (
                pltpu.make_async_copy(mixed_hbm.at[j], mixed.at[j], sem.at[0, j]),
                pltpu.make_async_copy(w_hbm.at[rows], w_buf.at[j], sem.at[1, j]),
            )
        )
    for pair in copies:
        for copy in pair:
            copy.start()
    acc = start_ref[...].astype(F32)
    for j, pair in enumerate(copies):
        for copy in pair:
            copy.wait()
        acc = acc + dot(mixed[j], w_buf[j])
    out_ref[...] = acc.astype(out_ref.dtype)


def square_sums(values):
    ones = jnp.ones((8, CH), BF16)
    sq = values * values
    high = sq.astype(BF16)
    return dot_nt(ones, high) + dot_nt(ones, (sq - high.astype(F32)).astype(BF16))


def two_rows(total):
    high = total.astype(BF16).astype(F32)
    row = lax.broadcasted_iota(jnp.int32, total.shape, 0)
    return jnp.where(row == 0, high, jnp.where(row == 1, total - high, 0.0))


def with_tail(rows, tail):
    return jnp.concatenate([rows, tail], axis=0).astype(BF16)


def load_kernel(wg_ref, wgx_ref, wu_ref, wux_ref, mark_ref, gate_ref, up_ref, out_mark_ref, sem):
    copies = []
    pieces = ((wg_ref, gate_ref, 0), (wgx_ref, gate_ref, CH), (wu_ref, up_ref, 0), (wux_ref, up_ref, CH))
    for i, (src, dst, at) in enumerate(pieces):
        copies.append(pltpu.make_async_copy(src, dst.at[:, pl.ds(at, CH)], sem.at[i]))
        copies[-1].start()
    for copy in copies:
        copy.wait()
    out_mark_ref[...] = mark_ref[...]


def scale_kernel(*refs):
    blocks, (gain_ref, gain_oth_ref, out_ref, tail_ref) = refs[:-4], refs[-4:]
    for i, block in enumerate(blocks):
        own = block[0].astype(F32)
        oth = block[1].astype(F32)
        out_ref[i, :, 0:CH] = (own * gain_ref[...]).astype(BF16)
        out_ref[i, :, CH:] = (oth * gain_oth_ref[...]).astype(BF16)
        tail_ref[i] = two_rows(square_sums(own) + square_sums(oth))


def mlp_kernel(slots, split, idx_ref, *refs):
    rows, (gate_ref, up_ref) = refs[:4], refs[4:6]
    out_refs, order_ref = refs[6:-3], refs[-3]
    scaled, tail = refs[-2:]
    for slot in range(8):
        order_ref[slot] = idx_ref[slot]
    for at, slot in enumerate(slots):
        which = idx_ref[slot]
        span = slice(at * ROWS, at * ROWS + ROWS)

        @pl.when(which < NEAR)
        def _():
            scaled[span, :] = rows[0][which]
            tail[at] = rows[1][which]

        @pl.when(which >= NEAR)
        def _():
            scaled[span, :] = rows[2][which - NEAR]
            tail[at] = rows[3][which - NEAR]

    zeros = jnp.zeros((FF_PAD - FF_LOC, ROWS), F32)
    gate = dot_nt(gate_ref[...], scaled[...])
    for at in range(len(slots)):
        target = out_refs[2 * at] if split else out_refs[at].at[0]
        target[...] = with_tail(gate[:, at * ROWS : at * ROWS + ROWS], zeros)
    up = dot_nt(up_ref[...], scaled[...])
    for at in range(len(slots)):
        target = out_refs[2 * at + 1] if split else out_refs[at].at[1]
        target[...] = with_tail(up[:, at * ROWS : at * ROWS + ROWS], tail[at])


def sum_kernel(*refs):
    total = refs[0][...].astype(F32)
    for ref in refs[1:-1]:
        total = total + ref[...].astype(F32)
    refs[-1][...] = total.astype(BF16)


def sum_apart_kernel(left_ref, right_ref, gate_ref, up_ref):
    for i, out_ref in enumerate((gate_ref, up_ref)):
        out_ref[...] = (left_ref[i].astype(F32) + right_ref[i].astype(F32)).astype(BF16)


def finish_kernel(own_ref, across_ref, gate_1_ref, gate_3_ref, up_1_ref, up_3_ref, out_ref):
    gate = own_ref[0].astype(F32) + across_ref[0].astype(F32)
    gate = gate + (gate_1_ref[...].astype(F32) + gate_3_ref[...].astype(F32))
    up = own_ref[1].astype(F32) + across_ref[1].astype(F32)
    up = up + (up_1_ref[...].astype(F32) + up_3_ref[...].astype(F32))
    sums = up[FF_LOC : FF_LOC + 1] + up[FF_LOC + 1 : FF_LOC + 2]
    scale = lax.rsqrt(sums * (1.0 / (N_TP * CH)) + EPS)
    gate = gate[:FF_LOC] * scale
    out_ref[...] = (gate / (1.0 + jnp.exp(-gate)) * (up[:FF_LOC] * scale)).astype(BF16)


def params(mib):
    return pltpu.CompilerParams(vmem_limit_bytes=mib * 1024 * 1024)


def pairs_of(rule):
    pairs = []
    for i in range(N_CTX * N_TP):
        target = rule(*split_index(i))
        if target is not None:
            pairs.append((i, join_index(*target)))
    return pairs


def to_row_owner_first(z, x, y, k):
    return (z, x ^ 1, y, k) if k == x % 2 else (z, x, y, k ^ 1)


def to_row_owner_second(z, x, y, k):
    return None if k == x % 2 else (z, x ^ 1, y, k ^ 1)


def in_smem():
    return pl.BlockSpec(memory_space=pltpu.SMEM)


def anywhere():
    return pl.BlockSpec(memory_space=pl.ANY)


def along(steps, z, x, y, k):
    return (z + steps, x, y, k) if z % 2 == 0 else (z - steps, x, y, k)


def out_proj(offset, core, mixed, w_out, start, dtype):
    return pl.pallas_call(
        functools.partial(out_proj_kernel, offset),
        out_shape=jax.ShapeDtypeStruct((ROWS, CH), dtype),
        in_specs=[
            in_smem(),
            anywhere(),
            pl.BlockSpec(memory_space=pltpu.HBM),
            pl.BlockSpec(memory_space=pltpu.VMEM),
        ],
        scratch_shapes=[
            pltpu.VMEM((N_TP // 2, ROWS, CH), BF16),
            pltpu.VMEM((N_TP // 2, CH, CH), BF16),
            pltpu.SemaphoreType.DMA((2, N_TP // 2)),
        ],
        compiler_params=params(51),
        cost_estimate=pl.CostEstimate(
            flops=2 * ROWS * CH * N_TP // 2 * CH, bytes_accessed=5 << 20, transcendentals=0
        ),
        name="out_proj",
    )(core, mixed, w_out, start)


def load_weights(weights, mark):
    vmem = pl.BlockSpec(memory_space=pltpu.VMEM)
    return pl.pallas_call(
        load_kernel,
        out_shape=[jax.ShapeDtypeStruct((FF_LOC, 2 * CH), BF16)] * 2
        + [jax.ShapeDtypeStruct(mark.shape, mark.dtype)],
        in_specs=[anywhere()] * 4 + [vmem],
        out_specs=[vmem] * 3,
        scratch_shapes=[pltpu.SemaphoreType.DMA((4,))],
        compiler_params=params(16),
        cost_estimate=pl.CostEstimate(flops=1, bytes_accessed=12 << 20, transcendentals=0),
        name="load",
    )(*weights, mark)


def scale(blocks, gains):
    n = len(blocks)
    return pl.pallas_call(
        scale_kernel,
        out_shape=[
            jax.ShapeDtypeStruct((n, ROWS, 2 * CH), BF16),
            jax.ShapeDtypeStruct((n, 8, ROWS), F32),
        ],
        compiler_params=params(14),
        cost_estimate=pl.CostEstimate(
            flops=8 * n * ROWS * CH * 8, bytes_accessed=n << 19, transcendentals=0
        ),
        name="scale",
    )(*blocks, *gains)


def mlp_part(slots, idx, rows, weights, split=False):
    n = len(slots)
    shapes = [(FF_PAD, ROWS)] * (2 * n) if split else [(2, FF_PAD, ROWS)] * n
    vmem = pl.BlockSpec(memory_space=pltpu.VMEM)
    *outs, token = pl.pallas_call(
        functools.partial(mlp_kernel, slots, split),
        out_shape=[jax.ShapeDtypeStruct(shape, BF16) for shape in shapes]
        + [jax.ShapeDtypeStruct((8,), jnp.int32)],
        in_specs=[in_smem()] + [vmem] * 6,
        out_specs=[vmem] * len(shapes) + [in_smem()],
        scratch_shapes=[
            pltpu.VMEM((n * ROWS, 2 * CH), BF16),
            pltpu.VMEM((n, 8, ROWS), F32),
        ],
        compiler_params=params(18),
        cost_estimate=pl.CostEstimate(
            flops=10**8, bytes_accessed=1 << 19, transcendentals=0
        ),
        name="mlp",
    )(idx, *rows, *weights)
    return outs, token


def in_vmem_call(kernel, shapes, name, parts):
    vmem = pl.BlockSpec(memory_space=pltpu.VMEM)
    return pl.pallas_call(
        kernel,
        out_shape=[jax.ShapeDtypeStruct(shape, BF16) for shape in shapes],
        in_specs=[vmem] * len(parts),
        out_specs=[vmem] * len(shapes),
        compiler_params=params(16),
        cost_estimate=pl.CostEstimate(flops=1, bytes_accessed=1 << 19, transcendentals=0),
        name=name,
    )(*parts)


def shards(residual, features, filters, skip_gain, w_out, norm_gain, w_gate, w_up):
    ctx = lax.axis_index("ctx")
    tp = lax.axis_index("tp")
    core, x_lo = tp % 2, ctx % 2
    x_hi, y = tp // 8, (tp // 2) % 4
    feat = features.transpose(1, 0, 2)
    wg, wu = w_gate.T, w_up.T
    gain = norm_gain[None, :]
    wg_oth, wu_oth, gain_oth = shift(wg, k=1), shift(wu, k=1), shift(gain, k=1)

    sent = pl.pallas_call(
        prep_kernel,
        out_shape=jax.ShapeDtypeStruct((N_CTX, 2 * SUB, ROWS), BF16),
        compiler_params=params(56),
        name="prep",
    )(feat, filters)
    recv = lax.all_to_all(sent, "ctx", 0, 0, tiled=True)
    recv, wg_oth, wu_oth, gain_oth = lax.optimization_barrier((recv, wg_oth, wu_oth, gain_oth))
    conv = pl.pallas_call(
        conv_kernel,
        out_shape=jax.ShapeDtypeStruct((N_CTX, SUB, ROWS), BF16),
        scratch_shapes=[
            pltpu.VMEM((N_CTX, 2 * SUB, 256), F32),
            pltpu.VMEM((N_CTX, 3, SUB, 128), F32),
            pltpu.VMEM((N_CTX, SUB, 256), F32),
        ],
        compiler_params=params(14),
        name="conv",
    )(recv, jnp.asarray(dft_tables()))
    conv_rows = lax.all_to_all(conv, "ctx", 0, 0, tiled=True)
    copies = pl.pallas_call(
        mix_kernel,
        out_shape=jax.ShapeDtypeStruct((8, ROWS, CH), BF16),
        compiler_params=params(56),
        name="mix",
    )(conv_rows, feat, skip_gain[None, :])

    mixed = lax.all_to_all(
        copies, "tp", 0, 0, axis_index_groups=PLANE_GROUPS, tiled=True
    )
    mixed_oth = shift(mixed, k=1)
    core_arr = core.astype(jnp.int32)[None]
    half = out_proj(0, core_arr, mixed, w_out, residual, F32)
    stream = out_proj(1, core_arr, mixed_oth, w_out, half, BF16)

    first = lax.ppermute(stream, AXES, pairs_of(to_row_owner_first))
    second = lax.ppermute(stream, AXES, pairs_of(to_row_owner_second))
    here = x_lo == core
    held = jnp.stack([jnp.where(here, stream, first), jnp.where(here, first, second)])
    gate_w, up_w, mark = load_weights((wg, wg_oth, wu, wu_oth), held[0, :16])
    gain, _ = lax.optimization_barrier((gain, mark))
    z = ctx // 2
    side = jnp.where(z % 2 == 0, -1, 1)
    two_first = lax.ppermute(held, AXES, pairs_of(functools.partial(along, 2)))
    two_second = lax.ppermute(held, AXES, pairs_of(functools.partial(along, -2)))
    one_first = lax.ppermute(held, AXES, pairs_of(functools.partial(along, 1)))
    one_second = lax.ppermute(held, AXES, pairs_of(functools.partial(along, -1)))
    three_first = lax.ppermute(two_first, AXES, pairs_of(functools.partial(along, 1)))
    three_second = lax.ppermute(two_second, AXES, pairs_of(functools.partial(along, -1)))
    opposite = lax.ppermute(two_first, AXES, pairs_of(functools.partial(along, 2)))
    gains = (gain, gain_oth)
    rows = scale([held, one_first, one_second, two_first, two_second], gains)
    rows = rows + scale([three_first, three_second, opposite], gains)

    order = []
    for b in range(4):
        for a in range(2):
            d = (side * (4 * ((x_hi + a) % 2) + (y + b) % 4 - z)) % 8
            order.append(d)
    seen = jnp.stack(order)
    idx = sum(jnp.where(seen == d, at, 0) for d, at in enumerate(ROW_OF)).astype(jnp.int32)

    weights = (gate_w, up_w)
    both, half = (2, FF_PAD, ROWS), (FF_PAD, ROWS)
    (two_far,), then = mlp_part((5,), idx, rows, weights)
    (one_far, three_far), then = mlp_part((3, 7), then, rows, weights)
    near, then = mlp_part((2, 6), then, rows, weights, split=True)
    (two_near, own_far), then = mlp_part((4, 1), then, rows, weights)
    (own_near,), _ = mlp_part((0,), then, rows, weights)
    two_far = shift(two_far, x=2)
    one_far = shift(one_far, y=1)
    three_far = shift(three_far, y=-1)
    up_1 = shift(near[1], y=1)
    gate_3 = shift(near[2], y=-1)
    gate_by, up_by = in_vmem_call(sum_apart_kernel, (half, half), "sum", (two_near, two_far))
    (across,) = in_vmem_call(sum_kernel, (both,), "sum", (own_far, one_far, three_far))
    gate_by = shift(gate_by, y=1)
    up_by = shift(up_by, y=-1)
    across = shift(across, x=2)
    (gate_1,) = in_vmem_call(sum_kernel, (half,), "sum", (near[0], gate_by))
    (up_3,) = in_vmem_call(sum_kernel, (half,), "sum", (near[3], up_by))
    gate_1 = shift(gate_1, y=1)
    up_3 = shift(up_3, y=-1)
    (hidden_t,) = in_vmem_call(
        finish_kernel,
        ((FF_LOC, ROWS),),
        "finish",
        (own_near, across, gate_1, gate_3, up_1, up_3),
    )
    return stream, hidden_t.T


def solution(mesh):
    placed = (
        P("ctx", "tp"),
        P("ctx", None, "tp"),
        P("ctx", "tp"),
        P("tp"),
        P(None, "tp"),
        P("tp"),
        P("tp", "ctx"),
        P("tp", "ctx"),
    )
    return jax.shard_map(
        shards,
        mesh=mesh,
        in_specs=placed,
        out_specs=(P("ctx", "tp"), P("tp", "ctx")),
        check_vma=False,
    )
```

```python
import functools
import math

import jax
import jax.numpy as jnp
import numpy as np
from jax import lax
from jax.experimental import pallas as pl
from jax.experimental.pallas import tpu as pltpu
from jax.sharding import PartitionSpec as P

F32 = jnp.float32
BF16 = jnp.bfloat16
AXES = ("ctx", "tp")
N_CTX = 16
N_TP = 16
ROWS = 128
CH = 512
SUB = 32
FF_LOC = 1368
FF_PAD = 1376
EPS = 1e-06
NEAR = 5
ROW_OF = (0, 2, 3, 6, 7, 5, 4, 1)
PLANE_GROUPS = [[xh * 8 + y * 2 + k for xh in range(2) for y in range(4)] for k in range(2)]


def split_index(i):
    c, t = divmod(i, N_TP)
    z, x_lo = divmod(c, 2)
    x_hi, r = divmod(t, 8)
    y, k = divmod(r, 2)
    return z, x_hi * 2 + x_lo, y, k


def join_index(z, x, y, k):
    x = x % 4
    return ((z % 8) * 2 + x % 2) * N_TP + (x // 2) * 8 + (y % 4) * 2 + k % 2


def shift(arr, z=0, x=0, y=0, k=0):
    pairs = []
    for i in range(N_CTX * N_TP):
        az, ax, ay, ak = split_index(i)
        pairs.append((i, join_index(az + z, ax + x, ay + y, ak + k)))
    return lax.ppermute(arr, AXES, pairs)


def split_bf16(table):
    high = np.asarray(table, np.float32).astype(jnp.bfloat16)
    low = (np.asarray(table, np.float32) - high.astype(np.float32)).astype(jnp.bfloat16)
    return high, low


def dft_tables():
    size = 2 * ROWS
    pos = np.arange(ROWS)
    freq = np.arange(ROWS)
    phase = (pos[:, None] * freq[None, :]) % size
    angle = 2.0 * math.pi / size * phase
    cos, sin = np.cos(angle), np.sin(angle)
    sign = np.where(pos % 2 == 0, 1.0, -1.0)
    fwd_im = -sin
    fwd_im[:, 0] = sign
    forward = np.concatenate([cos, fwd_im], axis=1)
    weight = np.where(freq == 0, 1.0, 2.0)[:, None] / size
    inv_re = cos.T * weight
    inv_im = -sin.T * weight
    inv_im[0, :] = sign / size
    inverse = np.concatenate([inv_re, inv_im], axis=0)
    return np.concatenate(split_bf16(forward) + split_bf16(inverse.T), axis=1)


def dot(a, b):
    return jnp.dot(a, b, preferred_element_type=F32)


def dot_nt(a, b):
    return lax.dot_general(a, b, (((1,), (1,)), ((), ())), preferred_element_type=F32)


def prep_kernel(feat_ref, filt_ref, out_ref):
    prod = feat_ref[1].astype(F32) * feat_ref[2].astype(F32)
    filt = filt_ref[...]
    for j in range(CH // 128):
        cols = slice(128 * j, 128 * j + 128)
        out_ref[4 * j : 4 * j + 4, 0:SUB, :] = prod[:, cols].T.astype(BF16).reshape(4, SUB, 128)
        out_ref[4 * j : 4 * j + 4, SUB : 2 * SUB, :] = (
            filt[:, cols].T.astype(BF16).reshape(4, SUB, 128)
        )


def conv_kernel(x_ref, tab_ref, out_ref, spec, filt, outs):
    x = x_ref[...].reshape(N_CTX * 2 * SUB, ROWS)
    spec[...] = (dot(x, tab_ref[:, 0:256]) + dot(x, tab_ref[:, 256:512])).reshape(N_CTX, 2 * SUB, 256)
    lane = lax.broadcasted_iota(jnp.int32, (SUB, 128), 1)
    sign = jnp.where(lane % 2 == 0, 1.0, -1.0).astype(F32)
    first = lane == 0
    for d in range(N_CTX):
        re = spec[d, SUB:, 0:128]
        im = spec[d, SUB:, 128:256]
        if d > 0:
            re = re + sign * spec[d - 1, SUB:, 0:128]
            im = im + sign * spec[d - 1, SUB:, 128:256]
        filt[d, 0] = re
        filt[d, 1] = jnp.where(first, 0.0, im)
        filt[d, 2] = jnp.where(first, im, re)
    for m in range(N_CTX):
        acc_re = jnp.zeros((SUB, 128), F32)
        acc_im = jnp.zeros((SUB, 128), F32)
        for n in range(m + 1):
            pr = spec[n, 0:SUB, 0:128]
            pi = spec[n, 0:SUB, 128:256]
            hr, hz, hq = filt[m - n, 0], filt[m - n, 1], filt[m - n, 2]
            acc_re = acc_re + (pr * hr - pi * hz)
            acc_im = acc_im + (pr * hz + pi * hq)
        outs[m, :, 0:128] = acc_re
        outs[m, :, 128:256] = acc_im
    total = outs[...].reshape(N_CTX * SUB, 256)
    high = total.astype(BF16)
    low = (total - high.astype(F32)).astype(BF16)
    inv_high, inv_low = tab_ref[:, 512:768], tab_ref[:, 768:1024]
    y = dot_nt(high, inv_high) + dot_nt(high, inv_low) + dot_nt(low, inv_high)
    out_ref[...] = y.astype(BF16).reshape(N_CTX, SUB, ROWS)


def mix_kernel(conv_ref, feat_ref, skip_ref, out_ref):
    conv = conv_ref[...].reshape(CH, ROWS).astype(F32)
    for j in range(CH // 128):
        cols = slice(128 * j, 128 * j + 128)
        prod = feat_ref[1, :, cols].astype(F32) * feat_ref[2, :, cols].astype(F32)
        long = conv[cols, :].T
        gate = feat_ref[0, :, cols].astype(F32)
        mixed = (gate * (long + skip_ref[:, cols] * prod)).astype(BF16)
        for copy in range(8):
            out_ref[copy, :, cols] = mixed


def out_proj_kernel(offset, core_ref, mixed_hbm, w_hbm, start_ref, out_ref, mixed, w_buf, sem):
    first = jnp.bitwise_xor(core_ref[0], offset)
    copies = []
    for j in range(N_TP // 2):
        rows = pl.ds(pl.multiple_of((2 * j + first) * CH, CH), CH)
        copies.append(
            (
                pltpu.make_async_copy(mixed_hbm.at[j], mixed.at[j], sem.at[0, j]),
                pltpu.make_async_copy(w_hbm.at[rows], w_buf.at[j], sem.at[1, j]),
            )
        )
    for pair in copies:
        for copy in pair:
            copy.start()
    acc = start_ref[...].astype(F32)
    for j, pair in enumerate(copies):
        for copy in pair:
            copy.wait()
        acc = acc + dot(mixed[j], w_buf[j])
    out_ref[...] = acc.astype(out_ref.dtype)


def square_sums(values):
    ones = jnp.ones((8, CH), BF16)
    sq = values * values
    high = sq.astype(BF16)
    return dot_nt(ones, high) + dot_nt(ones, (sq - high.astype(F32)).astype(BF16))


def two_rows(total):
    high = total.astype(BF16).astype(F32)
    row = lax.broadcasted_iota(jnp.int32, total.shape, 0)
    return jnp.where(row == 0, high, jnp.where(row == 1, total - high, 0.0))


def with_tail(rows, tail):
    return jnp.concatenate([rows, tail], axis=0).astype(BF16)


def load_kernel(wg_ref, wgx_ref, wu_ref, wux_ref, mark_ref, gate_ref, up_ref, out_mark_ref, sem):
    copies = []
    pieces = ((wg_ref, gate_ref, 0), (wgx_ref, gate_ref, CH), (wu_ref, up_ref, 0), (wux_ref, up_ref, CH))
    for i, (src, dst, at) in enumerate(pieces):
        copies.append(pltpu.make_async_copy(src, dst.at[:, pl.ds(at, CH)], sem.at[i]))
        copies[-1].start()
    for copy in copies:
        copy.wait()
    out_mark_ref[...] = mark_ref[...]


def hold_kernel(here_ref, stream_ref, second_ref, first_ref, out_ref):
    @pl.when(here_ref[0] == 1)
    def _():
        out_ref[0] = stream_ref[...]
        out_ref[1] = first_ref[...]

    @pl.when(here_ref[0] == 0)
    def _():
        out_ref[0] = first_ref[...]
        out_ref[1] = second_ref[...]


def scale_kernel(*refs):
    blocks, (gain_ref, gain_oth_ref, out_ref, tail_ref) = refs[:-4], refs[-4:]
    for i, block in enumerate(blocks):
        own = block[0].astype(F32)
        oth = block[1].astype(F32)
        out_ref[i, :, 0:CH] = (own * gain_ref[...]).astype(BF16)
        out_ref[i, :, CH:] = (oth * gain_oth_ref[...]).astype(BF16)
        tail_ref[i] = two_rows(square_sums(own) + square_sums(oth))


def mlp_kernel(slots, split, idx_ref, *refs):
    rows, (gate_ref, up_ref) = refs[:4], refs[4:6]
    out_refs, order_ref = refs[6:-3], refs[-3]
    scaled, tail = refs[-2:]
    for slot in range(8):
        order_ref[slot] = idx_ref[slot]
    for at, slot in enumerate(slots):
        which = idx_ref[slot]
        span = slice(at * ROWS, at * ROWS + ROWS)

        @pl.when(which < NEAR)
        def _():
            scaled[span, :] = rows[0][which]
            tail[at] = rows[1][which]

        @pl.when(which >= NEAR)
        def _():
            scaled[span, :] = rows[2][which - NEAR]
            tail[at] = rows[3][which - NEAR]

    zeros = jnp.zeros((FF_PAD - FF_LOC, ROWS), F32)
    gate = dot_nt(gate_ref[...], scaled[...])
    for at in range(len(slots)):
        target = out_refs[2 * at] if split else out_refs[at].at[0]
        target[...] = with_tail(gate[:, at * ROWS : at * ROWS + ROWS], zeros)
    up = dot_nt(up_ref[...], scaled[...])
    for at in range(len(slots)):
        target = out_refs[2 * at + 1] if split else out_refs[at].at[1]
        target[...] = with_tail(up[:, at * ROWS : at * ROWS + ROWS], tail[at])


def sum_kernel(*refs):
    total = refs[0][...].astype(F32)
    for ref in refs[1:-1]:
        total = total + ref[...].astype(F32)
    refs[-1][...] = total.astype(BF16)


def sum_apart_kernel(left_ref, right_ref, gate_ref, up_ref):
    for i, out_ref in enumerate((gate_ref, up_ref)):
        out_ref[...] = (left_ref[i].astype(F32) + right_ref[i].astype(F32)).astype(BF16)


def finish_kernel(own_ref, across_ref, gate_1_ref, gate_3_ref, up_1_ref, up_3_ref, out_ref):
    gate = own_ref[0].astype(F32) + across_ref[0].astype(F32)
    gate = gate + (gate_1_ref[...].astype(F32) + gate_3_ref[...].astype(F32))
    up = own_ref[1].astype(F32) + across_ref[1].astype(F32)
    up = up + (up_1_ref[...].astype(F32) + up_3_ref[...].astype(F32))
    sums = up[FF_LOC : FF_LOC + 1] + up[FF_LOC + 1 : FF_LOC + 2]
    scale = lax.rsqrt(sums * (1.0 / (N_TP * CH)) + EPS)
    gate = gate[:FF_LOC] * scale
    out_ref[...] = (gate / (1.0 + jnp.exp(-gate)) * (up[:FF_LOC] * scale)).astype(BF16)


def params(mib):
    return pltpu.CompilerParams(vmem_limit_bytes=mib * 1024 * 1024)


def pairs_of(rule):
    pairs = []
    for i in range(N_CTX * N_TP):
        target = rule(*split_index(i))
        if target is not None:
            pairs.append((i, join_index(*target)))
    return pairs


def to_row_owner_first(z, x, y, k):
    return (z, x ^ 1, y, k) if k == x % 2 else (z, x, y, k ^ 1)


def to_row_owner_second(z, x, y, k):
    return None if k == x % 2 else (z, x ^ 1, y, k ^ 1)


def in_smem():
    return pl.BlockSpec(memory_space=pltpu.SMEM)


def anywhere():
    return pl.BlockSpec(memory_space=pl.ANY)


def along(steps, z, x, y, k):
    return (z + steps, x, y, k) if z % 2 == 0 else (z - steps, x, y, k)


def out_proj(offset, core, mixed, w_out, start, dtype):
    return pl.pallas_call(
        functools.partial(out_proj_kernel, offset),
        out_shape=jax.ShapeDtypeStruct((ROWS, CH), dtype),
        in_specs=[
            in_smem(),
            anywhere(),
            pl.BlockSpec(memory_space=pltpu.HBM),
            pl.BlockSpec(memory_space=pltpu.VMEM),
        ],
        scratch_shapes=[
            pltpu.VMEM((N_TP // 2, ROWS, CH), BF16),
            pltpu.VMEM((N_TP // 2, CH, CH), BF16),
            pltpu.SemaphoreType.DMA((2, N_TP // 2)),
        ],
        compiler_params=params(51),
        cost_estimate=pl.CostEstimate(
            flops=2 * ROWS * CH * N_TP // 2 * CH, bytes_accessed=5 << 20, transcendentals=0
        ),
        name="out_proj",
    )(core, mixed, w_out, start)


def hold(here, *parts):
    vmem = pl.BlockSpec(memory_space=pltpu.VMEM)
    return pl.pallas_call(
        hold_kernel,
        out_shape=jax.ShapeDtypeStruct((2, ROWS, CH), BF16),
        in_specs=[in_smem()] + [vmem] * 3,
        out_specs=vmem,
        compiler_params=params(14),
        cost_estimate=pl.CostEstimate(flops=1, bytes_accessed=1 << 19, transcendentals=0),
        name="hold",
    )(here, *parts)


def load_weights(weights, mark):
    vmem = pl.BlockSpec(memory_space=pltpu.VMEM)
    return pl.pallas_call(
        load_kernel,
        out_shape=[jax.ShapeDtypeStruct((FF_LOC, 2 * CH), BF16)] * 2
        + [jax.ShapeDtypeStruct(mark.shape, mark.dtype)],
        in_specs=[anywhere()] * 4 + [vmem],
        out_specs=[vmem] * 3,
        scratch_shapes=[pltpu.SemaphoreType.DMA((4,))],
        compiler_params=params(16),
        cost_estimate=pl.CostEstimate(flops=1, bytes_accessed=12 << 20, transcendentals=0),
        name="load",
    )(*weights, mark)


def scale(blocks, gains):
    n = len(blocks)
    return pl.pallas_call(
        scale_kernel,
        out_shape=[
            jax.ShapeDtypeStruct((n, ROWS, 2 * CH), BF16),
            jax.ShapeDtypeStruct((n, 8, ROWS), F32),
        ],
        compiler_params=params(14),
        cost_estimate=pl.CostEstimate(
            flops=8 * n * ROWS * CH * 8, bytes_accessed=n << 19, transcendentals=0
        ),
        name="scale",
    )(*blocks, *gains)


def mlp_part(slots, idx, rows, weights, split=False):
    n = len(slots)
    shapes = [(FF_PAD, ROWS)] * (2 * n) if split else [(2, FF_PAD, ROWS)] * n
    vmem = pl.BlockSpec(memory_space=pltpu.VMEM)
    *outs, token = pl.pallas_call(
        functools.partial(mlp_kernel, slots, split),
        out_shape=[jax.ShapeDtypeStruct(shape, BF16) for shape in shapes]
        + [jax.ShapeDtypeStruct((8,), jnp.int32)],
        in_specs=[in_smem()] + [vmem] * 6,
        out_specs=[vmem] * len(shapes) + [in_smem()],
        scratch_shapes=[
            pltpu.VMEM((n * ROWS, 2 * CH), BF16),
            pltpu.VMEM((n, 8, ROWS), F32),
        ],
        compiler_params=params(18),
        cost_estimate=pl.CostEstimate(
            flops=10**8, bytes_accessed=1 << 19, transcendentals=0
        ),
        name="mlp",
    )(idx, *rows, *weights)
    return outs, token


def in_vmem_call(kernel, shapes, name, parts):
    vmem = pl.BlockSpec(memory_space=pltpu.VMEM)
    return pl.pallas_call(
        kernel,
        out_shape=[jax.ShapeDtypeStruct(shape, BF16) for shape in shapes],
        in_specs=[vmem] * len(parts),
        out_specs=[vmem] * len(shapes),
        compiler_params=params(16),
        cost_estimate=pl.CostEstimate(flops=1, bytes_accessed=1 << 19, transcendentals=0),
        name=name,
    )(*parts)


def shards(residual, features, filters, skip_gain, w_out, norm_gain, w_gate, w_up):
    ctx = lax.axis_index("ctx")
    tp = lax.axis_index("tp")
    core, x_lo = tp % 2, ctx % 2
    x_hi, y = tp // 8, (tp // 2) % 4
    feat = features.transpose(1, 0, 2)
    wg, wu = w_gate.T, w_up.T
    gain = norm_gain[None, :]
    wg_oth, wu_oth, gain_oth = shift(wg, k=1), shift(wu, k=1), shift(gain, k=1)

    sent = pl.pallas_call(
        prep_kernel,
        out_shape=jax.ShapeDtypeStruct((N_CTX, 2 * SUB, ROWS), BF16),
        compiler_params=params(56),
        name="prep",
    )(feat, filters)
    recv = lax.all_to_all(sent, "ctx", 0, 0, tiled=True)
    recv, wg_oth, wu_oth, gain_oth = lax.optimization_barrier((recv, wg_oth, wu_oth, gain_oth))
    conv = pl.pallas_call(
        conv_kernel,
        out_shape=jax.ShapeDtypeStruct((N_CTX, SUB, ROWS), BF16),
        scratch_shapes=[
            pltpu.VMEM((N_CTX, 2 * SUB, 256), F32),
            pltpu.VMEM((N_CTX, 3, SUB, 128), F32),
            pltpu.VMEM((N_CTX, SUB, 256), F32),
        ],
        compiler_params=params(14),
        name="conv",
    )(recv, jnp.asarray(dft_tables()))
    conv_rows = lax.all_to_all(conv, "ctx", 0, 0, tiled=True)
    copies = pl.pallas_call(
        mix_kernel,
        out_shape=jax.ShapeDtypeStruct((8, ROWS, CH), BF16),
        compiler_params=params(56),
        name="mix",
    )(conv_rows, feat, skip_gain[None, :])

    mixed = lax.all_to_all(
        copies, "tp", 0, 0, axis_index_groups=PLANE_GROUPS, tiled=True
    )
    mixed_oth = shift(mixed, k=1)
    core_arr = core.astype(jnp.int32)[None]
    half = out_proj(0, core_arr, mixed, w_out, residual, F32)
    stream = out_proj(1, core_arr, mixed_oth, w_out, half, BF16)

    first = lax.ppermute(stream, AXES, pairs_of(to_row_owner_first))
    second = lax.ppermute(stream, AXES, pairs_of(to_row_owner_second))
    here = (x_lo == core).astype(jnp.int32)[None]
    held = hold(here, stream, second, first)
    gate_w, up_w, mark = load_weights((wg, wg_oth, wu, wu_oth), held[0, :16])
    gain, _ = lax.optimization_barrier((gain, mark))
    z = ctx // 2
    side = jnp.where(z % 2 == 0, -1, 1)
    two_first = lax.ppermute(held, AXES, pairs_of(functools.partial(along, 2)))
    two_second = lax.ppermute(held, AXES, pairs_of(functools.partial(along, -2)))
    one_first = lax.ppermute(held, AXES, pairs_of(functools.partial(along, 1)))
    one_second = lax.ppermute(held, AXES, pairs_of(functools.partial(along, -1)))
    three_first = lax.ppermute(two_first, AXES, pairs_of(functools.partial(along, 1)))
    three_second = lax.ppermute(two_second, AXES, pairs_of(functools.partial(along, -1)))
    opposite = lax.ppermute(two_first, AXES, pairs_of(functools.partial(along, 2)))
    gains = (gain, gain_oth)
    rows = scale([held, one_first, one_second, two_first, two_second], gains)
    rows = rows + scale([three_first, three_second, opposite], gains)

    order = []
    for b in range(4):
        for a in range(2):
            d = (side * (4 * ((x_hi + a) % 2) + (y + b) % 4 - z)) % 8
            order.append(d)
    seen = jnp.stack(order)
    idx = sum(jnp.where(seen == d, at, 0) for d, at in enumerate(ROW_OF)).astype(jnp.int32)

    weights = (gate_w, up_w)
    both, half = (2, FF_PAD, ROWS), (FF_PAD, ROWS)
    (two_far,), then = mlp_part((5,), idx, rows, weights)
    (one_far, three_far), then = mlp_part((3, 7), then, rows, weights)
    near, then = mlp_part((2, 6), then, rows, weights, split=True)
    (two_near, own_far), then = mlp_part((4, 1), then, rows, weights)
    (own_near,), _ = mlp_part((0,), then, rows, weights)
    two_far = shift(two_far, x=2)
    one_far = shift(one_far, y=1)
    three_far = shift(three_far, y=-1)
    up_1 = shift(near[1], y=1)
    gate_3 = shift(near[2], y=-1)
    gate_by, up_by = in_vmem_call(sum_apart_kernel, (half, half), "sum", (two_near, two_far))
    (across,) = in_vmem_call(sum_kernel, (both,), "sum", (own_far, one_far, three_far))
    gate_by = shift(gate_by, y=1)
    up_by = shift(up_by, y=-1)
    across = shift(across, x=2)
    (gate_1,) = in_vmem_call(sum_kernel, (half,), "sum", (near[0], gate_by))
    (up_3,) = in_vmem_call(sum_kernel, (half,), "sum", (near[3], up_by))
    gate_1 = shift(gate_1, y=1)
    up_3 = shift(up_3, y=-1)
    (hidden_t,) = in_vmem_call(
        finish_kernel,
        ((FF_LOC, ROWS),),
        "finish",
        (own_near, across, gate_1, gate_3, up_1, up_3),
    )
    return stream, hidden_t.T


def solution(mesh):
    placed = (
        P("ctx", "tp"),
        P("ctx", None, "tp"),
        P("ctx", "tp"),
        P("tp"),
        P(None, "tp"),
        P("tp"),
        P("tp", "ctx"),
        P("tp", "ctx"),
    )
    return jax.shard_map(
        shards,
        mesh=mesh,
        in_specs=placed,
        out_specs=(P("ctx", "tp"), P("tp", "ctx")),
        check_vma=False,
    )
```

```python
import functools
import math

import jax
import jax.numpy as jnp
import numpy as np
from jax import lax
from jax.experimental import pallas as pl
from jax.experimental.pallas import tpu as pltpu
from jax.sharding import PartitionSpec as P

F32 = jnp.float32
BF16 = jnp.bfloat16
AXES = ("ctx", "tp")
N_CTX = 16
N_TP = 16
ROWS = 128
CH = 512
SUB = 32
FF_LOC = 1368
FF_PAD = 1376
EPS = 1e-06
NEAR = 5
ROW_OF = (0, 2, 3, 6, 7, 5, 4, 1)
PLANE_GROUPS = [[xh * 8 + y * 2 + k for xh in range(2) for y in range(4)] for k in range(2)]


def split_index(i):
    c, t = divmod(i, N_TP)
    z, x_lo = divmod(c, 2)
    x_hi, r = divmod(t, 8)
    y, k = divmod(r, 2)
    return z, x_hi * 2 + x_lo, y, k


def join_index(z, x, y, k):
    x = x % 4
    return ((z % 8) * 2 + x % 2) * N_TP + (x // 2) * 8 + (y % 4) * 2 + k % 2


def shift(arr, z=0, x=0, y=0, k=0):
    pairs = []
    for i in range(N_CTX * N_TP):
        az, ax, ay, ak = split_index(i)
        pairs.append((i, join_index(az + z, ax + x, ay + y, ak + k)))
    return lax.ppermute(arr, AXES, pairs)


def split_bf16(table):
    high = np.asarray(table, np.float32).astype(jnp.bfloat16)
    low = (np.asarray(table, np.float32) - high.astype(np.float32)).astype(jnp.bfloat16)
    return high, low


def dft_tables():
    size = 2 * ROWS
    pos = np.arange(ROWS)
    freq = np.arange(ROWS)
    phase = (pos[:, None] * freq[None, :]) % size
    angle = 2.0 * math.pi / size * phase
    cos, sin = np.cos(angle), np.sin(angle)
    sign = np.where(pos % 2 == 0, 1.0, -1.0)
    fwd_im = -sin
    fwd_im[:, 0] = sign
    forward = np.concatenate([cos, fwd_im], axis=1)
    weight = np.where(freq == 0, 1.0, 2.0)[:, None] / size
    inv_re = cos.T * weight
    inv_im = -sin.T * weight
    inv_im[0, :] = sign / size
    inverse = np.concatenate([inv_re, inv_im], axis=0)
    return np.concatenate(split_bf16(forward) + split_bf16(inverse.T), axis=1)


def dot(a, b):
    return jnp.dot(a, b, preferred_element_type=F32)


def dot_nt(a, b):
    return lax.dot_general(a, b, (((1,), (1,)), ((), ())), preferred_element_type=F32)


def prep_kernel(feat_ref, filt_ref, out_ref):
    prod = feat_ref[1].astype(F32) * feat_ref[2].astype(F32)
    filt = filt_ref[...]
    for j in range(CH // 128):
        cols = slice(128 * j, 128 * j + 128)
        out_ref[4 * j : 4 * j + 4, 0:SUB, :] = prod[:, cols].T.astype(BF16).reshape(4, SUB, 128)
        out_ref[4 * j : 4 * j + 4, SUB : 2 * SUB, :] = (
            filt[:, cols].T.astype(BF16).reshape(4, SUB, 128)
        )


def conv_kernel(x_ref, tab_ref, out_ref, spec, filt, outs):
    x = x_ref[...].reshape(N_CTX * 2 * SUB, ROWS)
    spec[...] = (dot(x, tab_ref[:, 0:256]) + dot(x, tab_ref[:, 256:512])).reshape(N_CTX, 2 * SUB, 256)
    lane = lax.broadcasted_iota(jnp.int32, (SUB, 128), 1)
    sign = jnp.where(lane % 2 == 0, 1.0, -1.0).astype(F32)
    first = lane == 0
    for d in range(N_CTX):
        re = spec[d, SUB:, 0:128]
        im = spec[d, SUB:, 128:256]
        if d > 0:
            re = re + sign * spec[d - 1, SUB:, 0:128]
            im = im + sign * spec[d - 1, SUB:, 128:256]
        filt[d, 0] = re
        filt[d, 1] = jnp.where(first, 0.0, im)
        filt[d, 2] = jnp.where(first, im, re)
    for m in range(N_CTX):
        acc_re = jnp.zeros((SUB, 128), F32)
        acc_im = jnp.zeros((SUB, 128), F32)
        for n in range(m + 1):
            pr = spec[n, 0:SUB, 0:128]
            pi = spec[n, 0:SUB, 128:256]
            hr, hz, hq = filt[m - n, 0], filt[m - n, 1], filt[m - n, 2]
            acc_re = acc_re + (pr * hr - pi * hz)
            acc_im = acc_im + (pr * hz + pi * hq)
        outs[m, :, 0:128] = acc_re
        outs[m, :, 128:256] = acc_im
    total = outs[...].reshape(N_CTX * SUB, 256)
    high = total.astype(BF16)
    low = (total - high.astype(F32)).astype(BF16)
    inv_high, inv_low = tab_ref[:, 512:768], tab_ref[:, 768:1024]
    y = dot_nt(high, inv_high) + dot_nt(high, inv_low) + dot_nt(low, inv_high)
    out_ref[...] = y.astype(BF16).reshape(N_CTX, SUB, ROWS)


def mix_kernel(conv_ref, feat_ref, skip_ref, out_ref):
    conv = conv_ref[...].reshape(CH, ROWS).astype(F32)
    for j in range(CH // 128):
        cols = slice(128 * j, 128 * j + 128)
        prod = feat_ref[1, :, cols].astype(F32) * feat_ref[2, :, cols].astype(F32)
        long = conv[cols, :].T
        gate = feat_ref[0, :, cols].astype(F32)
        mixed = (gate * (long + skip_ref[:, cols] * prod)).astype(BF16)
        for copy in range(8):
            out_ref[copy, :, cols] = mixed


def out_proj_kernel(offset, core_ref, mixed_hbm, w_hbm, start_ref, *refs):
    *out_refs, mixed, w_buf, sem = refs
    first = jnp.bitwise_xor(core_ref[0], offset)
    copies = []
    for j in range(N_TP // 2):
        rows = pl.ds(pl.multiple_of((2 * j + first) * CH, CH), CH)
        copies.append(
            (
                pltpu.make_async_copy(mixed_hbm.at[j], mixed.at[j], sem.at[0, j]),
                pltpu.make_async_copy(w_hbm.at[rows], w_buf.at[j], sem.at[1, j]),
            )
        )
    for pair in copies:
        for copy in pair:
            copy.start()
    acc = start_ref[...].astype(F32)
    for j, pair in enumerate(copies):
        for copy in pair:
            copy.wait()
        acc = acc + dot(mixed[j], w_buf[j])
    for out_ref in out_refs:
        out_ref[...] = acc.astype(out_ref.dtype)


def square_sums(values):
    ones = jnp.ones((8, CH), BF16)
    sq = values * values
    high = sq.astype(BF16)
    return dot_nt(ones, high) + dot_nt(ones, (sq - high.astype(F32)).astype(BF16))


def two_rows(total):
    high = total.astype(BF16).astype(F32)
    row = lax.broadcasted_iota(jnp.int32, total.shape, 0)
    return jnp.where(row == 0, high, jnp.where(row == 1, total - high, 0.0))


def with_tail(rows, tail):
    return jnp.concatenate([rows, tail], axis=0).astype(BF16)


def load_kernel(wg_ref, wgx_ref, wu_ref, wux_ref, mark_ref, gate_ref, up_ref, out_mark_ref, sem):
    copies = []
    pieces = ((wg_ref, gate_ref, 0), (wgx_ref, gate_ref, CH), (wu_ref, up_ref, 0), (wux_ref, up_ref, CH))
    for i, (src, dst, at) in enumerate(pieces):
        copies.append(pltpu.make_async_copy(src, dst.at[:, pl.ds(at, CH)], sem.at[i]))
        copies[-1].start()
    for copy in copies:
        copy.wait()
    out_mark_ref[...] = mark_ref[...]


def hold_kernel(here_ref, stream_ref, second_ref, first_ref, out_ref):
    @pl.when(here_ref[0] == 1)
    def _():
        out_ref[0] = stream_ref[...]
        out_ref[1] = first_ref[...]

    @pl.when(here_ref[0] == 0)
    def _():
        out_ref[0] = first_ref[...]
        out_ref[1] = second_ref[...]


def scale_kernel(*refs):
    blocks, (gain_ref, gain_oth_ref, out_ref, tail_ref) = refs[:-4], refs[-4:]
    for i, block in enumerate(blocks):
        own = block[0].astype(F32)
        oth = block[1].astype(F32)
        out_ref[i, :, 0:CH] = (own * gain_ref[...]).astype(BF16)
        out_ref[i, :, CH:] = (oth * gain_oth_ref[...]).astype(BF16)
        tail_ref[i] = two_rows(square_sums(own) + square_sums(oth))


def mlp_kernel(slots, split, idx_ref, *refs):
    rows, (gate_ref, up_ref) = refs[:4], refs[4:6]
    out_refs, order_ref = refs[6:-3], refs[-3]
    scaled, tail = refs[-2:]
    for slot in range(8):
        order_ref[slot] = idx_ref[slot]
    for at, slot in enumerate(slots):
        which = idx_ref[slot]
        span = slice(at * ROWS, at * ROWS + ROWS)

        @pl.when(which < NEAR)
        def _():
            scaled[span, :] = rows[0][which]
            tail[at] = rows[1][which]

        @pl.when(which >= NEAR)
        def _():
            scaled[span, :] = rows[2][which - NEAR]
            tail[at] = rows[3][which - NEAR]

    zeros = jnp.zeros((FF_PAD - FF_LOC, ROWS), F32)
    gate = dot_nt(gate_ref[...], scaled[...])
    for at in range(len(slots)):
        target = out_refs[2 * at] if split else out_refs[at].at[0]
        target[...] = with_tail(gate[:, at * ROWS : at * ROWS + ROWS], zeros)
    up = dot_nt(up_ref[...], scaled[...])
    for at in range(len(slots)):
        target = out_refs[2 * at + 1] if split else out_refs[at].at[1]
        target[...] = with_tail(up[:, at * ROWS : at * ROWS + ROWS], tail[at])


def sum_kernel(*refs):
    total = refs[0][...].astype(F32)
    for ref in refs[1:-1]:
        total = total + ref[...].astype(F32)
    refs[-1][...] = total.astype(BF16)


def sum_apart_kernel(left_ref, right_ref, gate_ref, up_ref):
    for i, out_ref in enumerate((gate_ref, up_ref)):
        out_ref[...] = (left_ref[i].astype(F32) + right_ref[i].astype(F32)).astype(BF16)


def finish_kernel(own_ref, across_ref, gate_1_ref, gate_3_ref, up_1_ref, up_3_ref, out_ref):
    gate = own_ref[0].astype(F32) + across_ref[0].astype(F32)
    gate = gate + (gate_1_ref[...].astype(F32) + gate_3_ref[...].astype(F32))
    up = own_ref[1].astype(F32) + across_ref[1].astype(F32)
    up = up + (up_1_ref[...].astype(F32) + up_3_ref[...].astype(F32))
    sums = up[FF_LOC : FF_LOC + 1] + up[FF_LOC + 1 : FF_LOC + 2]
    scale = lax.rsqrt(sums * (1.0 / (N_TP * CH)) + EPS)
    gate = gate[:FF_LOC] * scale
    out_ref[...] = (gate / (1.0 + jnp.exp(-gate)) * (up[:FF_LOC] * scale)).astype(BF16)


def params(mib):
    return pltpu.CompilerParams(vmem_limit_bytes=mib * 1024 * 1024)


def pairs_of(rule):
    pairs = []
    for i in range(N_CTX * N_TP):
        target = rule(*split_index(i))
        if target is not None:
            pairs.append((i, join_index(*target)))
    return pairs


def to_row_owner_first(z, x, y, k):
    return (z, x ^ 1, y, k) if k == x % 2 else (z, x, y, k ^ 1)


def to_row_owner_second(z, x, y, k):
    return None if k == x % 2 else (z, x ^ 1, y, k ^ 1)


def in_smem():
    return pl.BlockSpec(memory_space=pltpu.SMEM)


def anywhere():
    return pl.BlockSpec(memory_space=pl.ANY)


def along(steps, z, x, y, k):
    return (z + steps, x, y, k) if z % 2 == 0 else (z - steps, x, y, k)


def out_proj(offset, core, mixed, w_out, start, dtype, copies):
    return pl.pallas_call(
        functools.partial(out_proj_kernel, offset),
        out_shape=[jax.ShapeDtypeStruct((ROWS, CH), dtype)] * copies,
        in_specs=[
            in_smem(),
            anywhere(),
            pl.BlockSpec(memory_space=pltpu.HBM),
            pl.BlockSpec(memory_space=pltpu.VMEM),
        ],
        scratch_shapes=[
            pltpu.VMEM((N_TP // 2, ROWS, CH), BF16),
            pltpu.VMEM((N_TP // 2, CH, CH), BF16),
            pltpu.SemaphoreType.DMA((2, N_TP // 2)),
        ],
        compiler_params=params(51),
        cost_estimate=pl.CostEstimate(
            flops=2 * ROWS * CH * N_TP // 2 * CH, bytes_accessed=5 << 20, transcendentals=0
        ),
        name="out_proj",
    )(core, mixed, w_out, start)


def hold(here, *parts):
    vmem = pl.BlockSpec(memory_space=pltpu.VMEM)
    return pl.pallas_call(
        hold_kernel,
        out_shape=jax.ShapeDtypeStruct((2, ROWS, CH), BF16),
        in_specs=[in_smem()] + [vmem] * 3,
        out_specs=vmem,
        compiler_params=params(14),
        cost_estimate=pl.CostEstimate(flops=1, bytes_accessed=1 << 19, transcendentals=0),
        name="hold",
    )(here, *parts)


def load_weights(weights, mark):
    vmem = pl.BlockSpec(memory_space=pltpu.VMEM)
    return pl.pallas_call(
        load_kernel,
        out_shape=[jax.ShapeDtypeStruct((FF_LOC, 2 * CH), BF16)] * 2
        + [jax.ShapeDtypeStruct(mark.shape, mark.dtype)],
        in_specs=[anywhere()] * 4 + [vmem],
        out_specs=[vmem] * 3,
        scratch_shapes=[pltpu.SemaphoreType.DMA((4,))],
        compiler_params=params(16),
        cost_estimate=pl.CostEstimate(flops=1, bytes_accessed=12 << 20, transcendentals=0),
        name="load",
    )(*weights, mark)


def scale(blocks, gains):
    n = len(blocks)
    return pl.pallas_call(
        scale_kernel,
        out_shape=[
            jax.ShapeDtypeStruct((n, ROWS, 2 * CH), BF16),
            jax.ShapeDtypeStruct((n, 8, ROWS), F32),
        ],
        compiler_params=params(14),
        cost_estimate=pl.CostEstimate(
            flops=8 * n * ROWS * CH * 8, bytes_accessed=n << 19, transcendentals=0
        ),
        name="scale",
    )(*blocks, *gains)


def mlp_part(slots, idx, rows, weights, split=False):
    n = len(slots)
    shapes = [(FF_PAD, ROWS)] * (2 * n) if split else [(2, FF_PAD, ROWS)] * n
    vmem = pl.BlockSpec(memory_space=pltpu.VMEM)
    *outs, token = pl.pallas_call(
        functools.partial(mlp_kernel, slots, split),
        out_shape=[jax.ShapeDtypeStruct(shape, BF16) for shape in shapes]
        + [jax.ShapeDtypeStruct((8,), jnp.int32)],
        in_specs=[in_smem()] + [vmem] * 6,
        out_specs=[vmem] * len(shapes) + [in_smem()],
        scratch_shapes=[
            pltpu.VMEM((n * ROWS, 2 * CH), BF16),
            pltpu.VMEM((n, 8, ROWS), F32),
        ],
        compiler_params=params(18),
        cost_estimate=pl.CostEstimate(
            flops=10**8, bytes_accessed=1 << 19, transcendentals=0
        ),
        name="mlp",
    )(idx, *rows, *weights)
    return outs, token


def in_vmem_call(kernel, shapes, name, parts):
    vmem = pl.BlockSpec(memory_space=pltpu.VMEM)
    return pl.pallas_call(
        kernel,
        out_shape=[jax.ShapeDtypeStruct(shape, BF16) for shape in shapes],
        in_specs=[vmem] * len(parts),
        out_specs=[vmem] * len(shapes),
        compiler_params=params(16),
        cost_estimate=pl.CostEstimate(flops=1, bytes_accessed=1 << 19, transcendentals=0),
        name=name,
    )(*parts)


def shards(residual, features, filters, skip_gain, w_out, norm_gain, w_gate, w_up):
    ctx = lax.axis_index("ctx")
    tp = lax.axis_index("tp")
    core, x_lo = tp % 2, ctx % 2
    x_hi, y = tp // 8, (tp // 2) % 4
    feat = features.transpose(1, 0, 2)
    wg, wu = w_gate.T, w_up.T
    gain = norm_gain[None, :]
    wg_oth, wu_oth, gain_oth = shift(wg, k=1), shift(wu, k=1), shift(gain, k=1)

    sent = pl.pallas_call(
        prep_kernel,
        out_shape=jax.ShapeDtypeStruct((N_CTX, 2 * SUB, ROWS), BF16),
        compiler_params=params(56),
        name="prep",
    )(feat, filters)
    recv = lax.all_to_all(sent, "ctx", 0, 0, tiled=True)
    recv, wg_oth, wu_oth, gain_oth = lax.optimization_barrier((recv, wg_oth, wu_oth, gain_oth))
    conv = pl.pallas_call(
        conv_kernel,
        out_shape=jax.ShapeDtypeStruct((N_CTX, SUB, ROWS), BF16),
        scratch_shapes=[
            pltpu.VMEM((N_CTX, 2 * SUB, 256), F32),
            pltpu.VMEM((N_CTX, 3, SUB, 128), F32),
            pltpu.VMEM((N_CTX, SUB, 256), F32),
        ],
        compiler_params=params(14),
        name="conv",
    )(recv, jnp.asarray(dft_tables()))
    conv_rows = lax.all_to_all(conv, "ctx", 0, 0, tiled=True)
    copies = pl.pallas_call(
        mix_kernel,
        out_shape=jax.ShapeDtypeStruct((8, ROWS, CH), BF16),
        compiler_params=params(56),
        name="mix",
    )(conv_rows, feat, skip_gain[None, :])

    mixed = lax.all_to_all(
        copies, "tp", 0, 0, axis_index_groups=PLANE_GROUPS, tiled=True
    )
    mixed_oth = shift(mixed, k=1)
    core_arr = core.astype(jnp.int32)[None]
    (half,) = out_proj(0, core_arr, mixed, w_out, residual, F32, 1)
    stream_out, stream = out_proj(1, core_arr, mixed_oth, w_out, half, BF16, 2)

    first = lax.ppermute(stream, AXES, pairs_of(to_row_owner_first))
    second = lax.ppermute(stream, AXES, pairs_of(to_row_owner_second))
    here = (x_lo == core).astype(jnp.int32)[None]
    held = hold(here, stream, second, first)
    gate_w, up_w, mark = load_weights((wg, wg_oth, wu, wu_oth), held[0, :16])
    gain, _ = lax.optimization_barrier((gain, mark))
    z = ctx // 2
    side = jnp.where(z % 2 == 0, -1, 1)
    two_first = lax.ppermute(held, AXES, pairs_of(functools.partial(along, 2)))
    two_second = lax.ppermute(held, AXES, pairs_of(functools.partial(along, -2)))
    one_first = lax.ppermute(held, AXES, pairs_of(functools.partial(along, 1)))
    one_second = lax.ppermute(held, AXES, pairs_of(functools.partial(along, -1)))
    three_first = lax.ppermute(two_first, AXES, pairs_of(functools.partial(along, 1)))
    three_second = lax.ppermute(two_second, AXES, pairs_of(functools.partial(along, -1)))
    opposite = lax.ppermute(two_first, AXES, pairs_of(functools.partial(along, 2)))
    gains = (gain, gain_oth)
    rows = scale([held, one_first, one_second, two_first, two_second], gains)
    rows = rows + scale([three_first, three_second, opposite], gains)

    order = []
    for b in range(4):
        for a in range(2):
            d = (side * (4 * ((x_hi + a) % 2) + (y + b) % 4 - z)) % 8
            order.append(d)
    seen = jnp.stack(order)
    idx = sum(jnp.where(seen == d, at, 0) for d, at in enumerate(ROW_OF)).astype(jnp.int32)

    weights = (gate_w, up_w)
    both, half = (2, FF_PAD, ROWS), (FF_PAD, ROWS)
    (two_far,), then = mlp_part((5,), idx, rows, weights)
    (one_far, three_far), then = mlp_part((3, 7), then, rows, weights)
    near, then = mlp_part((2, 6), then, rows, weights, split=True)
    (two_near, own_far), then = mlp_part((4, 1), then, rows, weights)
    (own_near,), _ = mlp_part((0,), then, rows, weights)
    two_far = shift(two_far, x=2)
    one_far = shift(one_far, y=1)
    three_far = shift(three_far, y=-1)
    up_1 = shift(near[1], y=1)
    gate_3 = shift(near[2], y=-1)
    gate_by, up_by = in_vmem_call(sum_apart_kernel, (half, half), "sum", (two_near, two_far))
    (across,) = in_vmem_call(sum_kernel, (both,), "sum", (own_far, one_far, three_far))
    gate_by = shift(gate_by, y=1)
    up_by = shift(up_by, y=-1)
    across = shift(across, x=2)
    (gate_1,) = in_vmem_call(sum_kernel, (half,), "sum", (near[0], gate_by))
    (up_3,) = in_vmem_call(sum_kernel, (half,), "sum", (near[3], up_by))
    gate_1 = shift(gate_1, y=1)
    up_3 = shift(up_3, y=-1)
    (hidden_t,) = in_vmem_call(
        finish_kernel,
        ((FF_LOC, ROWS),),
        "finish",
        (own_near, across, gate_1, gate_3, up_1, up_3),
    )
    return stream_out, hidden_t.T


def solution(mesh):
    placed = (
        P("ctx", "tp"),
        P("ctx", None, "tp"),
        P("ctx", "tp"),
        P("tp"),
        P(None, "tp"),
        P("tp"),
        P("tp", "ctx"),
        P("tp", "ctx"),
    )
    return jax.shard_map(
        shards,
        mesh=mesh,
        in_specs=placed,
        out_specs=(P("ctx", "tp"), P("tp", "ctx")),
        check_vma=False,
    )
```

```python
import functools
import math

import jax
import jax.numpy as jnp
import numpy as np
from jax import lax
from jax.experimental import pallas as pl
from jax.experimental.pallas import tpu as pltpu
from jax.sharding import PartitionSpec as P

F32 = jnp.float32
BF16 = jnp.bfloat16
AXES = ("ctx", "tp")
N_CTX = 16
N_TP = 16
ROWS = 128
CH = 512
SUB = 32
FF_LOC = 1368
FF_PAD = 1376
EPS = 1e-06
NEAR = 5
ROW_OF = (0, 2, 3, 6, 7, 5, 4, 1)
PLANE_GROUPS = [[xh * 8 + y * 2 + k for xh in range(2) for y in range(4)] for k in range(2)]


def split_index(i):
    c, t = divmod(i, N_TP)
    z, x_lo = divmod(c, 2)
    x_hi, r = divmod(t, 8)
    y, k = divmod(r, 2)
    return z, x_hi * 2 + x_lo, y, k


def join_index(z, x, y, k):
    x = x % 4
    return ((z % 8) * 2 + x % 2) * N_TP + (x // 2) * 8 + (y % 4) * 2 + k % 2


def shift(arr, z=0, x=0, y=0, k=0):
    pairs = []
    for i in range(N_CTX * N_TP):
        az, ax, ay, ak = split_index(i)
        pairs.append((i, join_index(az + z, ax + x, ay + y, ak + k)))
    return lax.ppermute(arr, AXES, pairs)


def split_bf16(table):
    high = np.asarray(table, np.float32).astype(jnp.bfloat16)
    low = (np.asarray(table, np.float32) - high.astype(np.float32)).astype(jnp.bfloat16)
    return high, low


def dft_tables():
    size = 2 * ROWS
    pos = np.arange(ROWS)
    freq = np.arange(ROWS)
    phase = (pos[:, None] * freq[None, :]) % size
    angle = 2.0 * math.pi / size * phase
    cos, sin = np.cos(angle), np.sin(angle)
    sign = np.where(pos % 2 == 0, 1.0, -1.0)
    fwd_im = -sin
    fwd_im[:, 0] = sign
    forward = np.concatenate([cos, fwd_im], axis=1)
    weight = np.where(freq == 0, 1.0, 2.0)[:, None] / size
    inv_re = cos.T * weight
    inv_im = -sin.T * weight
    inv_im[0, :] = sign / size
    inverse = np.concatenate([inv_re, inv_im], axis=0)
    return np.concatenate(split_bf16(forward) + split_bf16(inverse.T), axis=1)


def dot(a, b):
    return jnp.dot(a, b, preferred_element_type=F32)


def dot_nt(a, b):
    return lax.dot_general(a, b, (((1,), (1,)), ((), ())), preferred_element_type=F32)


def prep_kernel(feat_ref, filt_ref, out_ref):
    prod = feat_ref[1].astype(F32) * feat_ref[2].astype(F32)
    filt = filt_ref[...]
    for j in range(CH // 128):
        cols = slice(128 * j, 128 * j + 128)
        out_ref[4 * j : 4 * j + 4, 0:SUB, :] = prod[:, cols].T.astype(BF16).reshape(4, SUB, 128)
        out_ref[4 * j : 4 * j + 4, SUB : 2 * SUB, :] = (
            filt[:, cols].T.astype(BF16).reshape(4, SUB, 128)
        )


def conv_kernel(x_ref, tab_ref, out_ref, spec, filt, outs):
    x = x_ref[...].reshape(N_CTX * 2 * SUB, ROWS)
    spec[...] = (dot(x, tab_ref[:, 0:256]) + dot(x, tab_ref[:, 256:512])).reshape(N_CTX, 2 * SUB, 256)
    lane = lax.broadcasted_iota(jnp.int32, (SUB, 128), 1)
    sign = jnp.where(lane % 2 == 0, 1.0, -1.0).astype(F32)
    first = lane == 0
    for d in range(N_CTX):
        re = spec[d, SUB:, 0:128]
        im = spec[d, SUB:, 128:256]
        if d > 0:
            re = re + sign * spec[d - 1, SUB:, 0:128]
            im = im + sign * spec[d - 1, SUB:, 128:256]
        filt[d, 0] = re
        filt[d, 1] = jnp.where(first, 0.0, im)
        filt[d, 2] = jnp.where(first, im, re)
    for m in range(N_CTX):
        acc_re = jnp.zeros((SUB, 128), F32)
        acc_im = jnp.zeros((SUB, 128), F32)
        for n in range(m + 1):
            pr = spec[n, 0:SUB, 0:128]
            pi = spec[n, 0:SUB, 128:256]
            hr, hz, hq = filt[m - n, 0], filt[m - n, 1], filt[m - n, 2]
            acc_re = acc_re + (pr * hr - pi * hz)
            acc_im = acc_im + (pr * hz + pi * hq)
        outs[m, :, 0:128] = acc_re
        outs[m, :, 128:256] = acc_im
    total = outs[...].reshape(N_CTX * SUB, 256)
    high = total.astype(BF16)
    low = (total - high.astype(F32)).astype(BF16)
    inv_high, inv_low = tab_ref[:, 512:768], tab_ref[:, 768:1024]
    y = dot_nt(high, inv_high) + dot_nt(high, inv_low) + dot_nt(low, inv_high)
    out_ref[...] = y.astype(BF16).reshape(N_CTX, SUB, ROWS)


def mix_kernel(conv_ref, feat_ref, skip_ref, out_ref):
    conv = conv_ref[...].reshape(CH, ROWS).astype(F32)
    for j in range(CH // 128):
        cols = slice(128 * j, 128 * j + 128)
        prod = feat_ref[1, :, cols].astype(F32) * feat_ref[2, :, cols].astype(F32)
        long = conv[cols, :].T
        gate = feat_ref[0, :, cols].astype(F32)
        mixed = (gate * (long + skip_ref[:, cols] * prod)).astype(BF16)
        for copy in range(8):
            out_ref[copy, :, cols] = mixed


def out_proj_first_kernel(
    core_ref, mixed_hbm, w_hbm, start_ref, out_ref, w_next, mixed, w_buf, sem
):
    core = core_ref[0]
    copies = []
    for j in range(N_TP // 2):
        rows = pl.ds(pl.multiple_of((2 * j + core) * CH, CH), CH)
        copies.append(pltpu.make_async_copy(mixed_hbm.at[j], mixed.at[j], sem.at[0, j]))
        copies.append(pltpu.make_async_copy(w_hbm.at[rows], w_buf.at[j], sem.at[1, j]))
    later = []
    for j in range(N_TP // 2):
        rows = pl.ds(pl.multiple_of((2 * j + 1 - core) * CH, CH), CH)
        later.append(pltpu.make_async_copy(w_hbm.at[rows], w_next.at[j], sem.at[2, j]))
    for copy in copies + later:
        copy.start()
    acc = start_ref[...].astype(F32)
    for j in range(N_TP // 2):
        copies[2 * j].wait()
        copies[2 * j + 1].wait()
        acc = acc + dot(mixed[j], w_buf[j])
    out_ref[...] = acc
    for copy in later:
        copy.wait()


def out_proj_second_kernel(mixed_ref, w_ref, start_ref, out_ref, keep_ref):
    acc = start_ref[...]
    for j in range(N_TP // 2):
        acc = acc + dot(mixed_ref[j], w_ref[j])
    out_ref[...] = acc.astype(BF16)
    keep_ref[...] = acc.astype(BF16)


def square_sums(values):
    ones = jnp.ones((8, CH), BF16)
    sq = values * values
    high = sq.astype(BF16)
    return dot_nt(ones, high) + dot_nt(ones, (sq - high.astype(F32)).astype(BF16))


def two_rows(total):
    high = total.astype(BF16).astype(F32)
    row = lax.broadcasted_iota(jnp.int32, total.shape, 0)
    return jnp.where(row == 0, high, jnp.where(row == 1, total - high, 0.0))


def with_tail(rows, tail):
    return jnp.concatenate([rows, tail], axis=0).astype(BF16)


def load_kernel(wg_ref, wgx_ref, wu_ref, wux_ref, mark_ref, gate_ref, up_ref, out_mark_ref, sem):
    copies = []
    pieces = ((wg_ref, gate_ref, 0), (wgx_ref, gate_ref, CH), (wu_ref, up_ref, 0), (wux_ref, up_ref, CH))
    for i, (src, dst, at) in enumerate(pieces):
        copies.append(pltpu.make_async_copy(src, dst.at[:, pl.ds(at, CH)], sem.at[i]))
        copies[-1].start()
    for copy in copies:
        copy.wait()
    out_mark_ref[...] = mark_ref[...]


def hold_kernel(here_ref, stream_ref, second_ref, first_ref, out_ref):
    @pl.when(here_ref[0] == 1)
    def _():
        out_ref[0] = stream_ref[...]
        out_ref[1] = first_ref[...]

    @pl.when(here_ref[0] == 0)
    def _():
        out_ref[0] = first_ref[...]
        out_ref[1] = second_ref[...]


def scale_kernel(*refs):
    blocks, (gain_ref, gain_oth_ref, out_ref, tail_ref) = refs[:-4], refs[-4:]
    for i, block in enumerate(blocks):
        own = block[0].astype(F32)
        oth = block[1].astype(F32)
        out_ref[i, :, 0:CH] = (own * gain_ref[...]).astype(BF16)
        out_ref[i, :, CH:] = (oth * gain_oth_ref[...]).astype(BF16)
        tail_ref[i] = two_rows(square_sums(own) + square_sums(oth))


def mlp_kernel(slots, split, idx_ref, *refs):
    rows, (gate_ref, up_ref) = refs[:4], refs[4:6]
    out_refs, order_ref = refs[6:-3], refs[-3]
    scaled, tail = refs[-2:]
    for slot in range(8):
        order_ref[slot] = idx_ref[slot]
    for at, slot in enumerate(slots):
        which = idx_ref[slot]
        span = slice(at * ROWS, at * ROWS + ROWS)

        @pl.when(which < NEAR)
        def _():
            scaled[span, :] = rows[0][which]
            tail[at] = rows[1][which]

        @pl.when(which >= NEAR)
        def _():
            scaled[span, :] = rows[2][which - NEAR]
            tail[at] = rows[3][which - NEAR]

    zeros = jnp.zeros((FF_PAD - FF_LOC, ROWS), F32)
    gate = dot_nt(gate_ref[...], scaled[...])
    for at in range(len(slots)):
        target = out_refs[2 * at] if split else out_refs[at].at[0]
        target[...] = with_tail(gate[:, at * ROWS : at * ROWS + ROWS], zeros)
    up = dot_nt(up_ref[...], scaled[...])
    for at in range(len(slots)):
        target = out_refs[2 * at + 1] if split else out_refs[at].at[1]
        target[...] = with_tail(up[:, at * ROWS : at * ROWS + ROWS], tail[at])


def sum_kernel(*refs):
    total = refs[0][...].astype(F32)
    for ref in refs[1:-1]:
        total = total + ref[...].astype(F32)
    refs[-1][...] = total.astype(BF16)


def sum_apart_kernel(left_ref, right_ref, gate_ref, up_ref):
    for i, out_ref in enumerate((gate_ref, up_ref)):
        out_ref[...] = (left_ref[i].astype(F32) + right_ref[i].astype(F32)).astype(BF16)


def finish_kernel(own_ref, across_ref, gate_1_ref, gate_3_ref, up_1_ref, up_3_ref, out_ref):
    gate = own_ref[0].astype(F32) + across_ref[0].astype(F32)
    gate = gate + (gate_1_ref[...].astype(F32) + gate_3_ref[...].astype(F32))
    up = own_ref[1].astype(F32) + across_ref[1].astype(F32)
    up = up + (up_1_ref[...].astype(F32) + up_3_ref[...].astype(F32))
    sums = up[FF_LOC : FF_LOC + 1] + up[FF_LOC + 1 : FF_LOC + 2]
    scale = lax.rsqrt(sums * (1.0 / (N_TP * CH)) + EPS)
    gate = gate[:FF_LOC] * scale
    out_ref[...] = (gate / (1.0 + jnp.exp(-gate)) * (up[:FF_LOC] * scale)).astype(BF16)


def params(mib):
    return pltpu.CompilerParams(vmem_limit_bytes=mib * 1024 * 1024)


def pairs_of(rule):
    pairs = []
    for i in range(N_CTX * N_TP):
        target = rule(*split_index(i))
        if target is not None:
            pairs.append((i, join_index(*target)))
    return pairs


def to_row_owner_first(z, x, y, k):
    return (z, x ^ 1, y, k) if k == x % 2 else (z, x, y, k ^ 1)


def to_row_owner_second(z, x, y, k):
    return None if k == x % 2 else (z, x ^ 1, y, k ^ 1)


def in_smem():
    return pl.BlockSpec(memory_space=pltpu.SMEM)


def anywhere():
    return pl.BlockSpec(memory_space=pl.ANY)


def along(steps, z, x, y, k):
    return (z + steps, x, y, k) if z % 2 == 0 else (z - steps, x, y, k)


def out_proj_first(core, mixed, w_out, start):
    vmem = pl.BlockSpec(memory_space=pltpu.VMEM)
    return pl.pallas_call(
        out_proj_first_kernel,
        out_shape=[
            jax.ShapeDtypeStruct((ROWS, CH), F32),
            jax.ShapeDtypeStruct((N_TP // 2, CH, CH), BF16),
        ],
        in_specs=[in_smem(), anywhere(), anywhere(), vmem],
        out_specs=[vmem] * 2,
        scratch_shapes=[
            pltpu.VMEM((N_TP // 2, ROWS, CH), BF16),
            pltpu.VMEM((N_TP // 2, CH, CH), BF16),
            pltpu.SemaphoreType.DMA((3, N_TP // 2)),
        ],
        compiler_params=params(45),
        cost_estimate=pl.CostEstimate(
            flops=2 * ROWS * CH * N_TP // 2 * CH, bytes_accessed=9 << 20, transcendentals=0
        ),
        name="out_proj_first",
    )(core, mixed, w_out, start)


def out_proj_second(mixed, weights, start):
    vmem = pl.BlockSpec(memory_space=pltpu.VMEM)
    return pl.pallas_call(
        out_proj_second_kernel,
        out_shape=[jax.ShapeDtypeStruct((ROWS, CH), BF16)] * 2,
        in_specs=[vmem] * 3,
        out_specs=[vmem] * 2,
        compiler_params=params(16),
        cost_estimate=pl.CostEstimate(
            flops=2 * ROWS * CH * N_TP // 2 * CH, bytes_accessed=1 << 20, transcendentals=0
        ),
        name="out_proj_second",
    )(mixed, weights, start)


def hold(here, *parts):
    vmem = pl.BlockSpec(memory_space=pltpu.VMEM)
    return pl.pallas_call(
        hold_kernel,
        out_shape=jax.ShapeDtypeStruct((2, ROWS, CH), BF16),
        in_specs=[in_smem()] + [vmem] * 3,
        out_specs=vmem,
        compiler_params=params(14),
        cost_estimate=pl.CostEstimate(flops=1, bytes_accessed=1 << 19, transcendentals=0),
        name="hold",
    )(here, *parts)


def load_weights(weights, mark):
    vmem = pl.BlockSpec(memory_space=pltpu.VMEM)
    return pl.pallas_call(
        load_kernel,
        out_shape=[jax.ShapeDtypeStruct((FF_LOC, 2 * CH), BF16)] * 2
        + [jax.ShapeDtypeStruct(mark.shape, mark.dtype)],
        in_specs=[anywhere()] * 4 + [vmem],
        out_specs=[vmem] * 3,
        scratch_shapes=[pltpu.SemaphoreType.DMA((4,))],
        compiler_params=params(16),
        cost_estimate=pl.CostEstimate(flops=1, bytes_accessed=12 << 20, transcendentals=0),
        name="load",
    )(*weights, mark)


def scale(blocks, gains):
    n = len(blocks)
    return pl.pallas_call(
        scale_kernel,
        out_shape=[
            jax.ShapeDtypeStruct((n, ROWS, 2 * CH), BF16),
            jax.ShapeDtypeStruct((n, 8, ROWS), F32),
        ],
        compiler_params=params(14),
        cost_estimate=pl.CostEstimate(
            flops=8 * n * ROWS * CH * 8, bytes_accessed=n << 19, transcendentals=0
        ),
        name="scale",
    )(*blocks, *gains)


def mlp_part(slots, idx, rows, weights, split=False):
    n = len(slots)
    shapes = [(FF_PAD, ROWS)] * (2 * n) if split else [(2, FF_PAD, ROWS)] * n
    vmem = pl.BlockSpec(memory_space=pltpu.VMEM)
    *outs, token = pl.pallas_call(
        functools.partial(mlp_kernel, slots, split),
        out_shape=[jax.ShapeDtypeStruct(shape, BF16) for shape in shapes]
        + [jax.ShapeDtypeStruct((8,), jnp.int32)],
        in_specs=[in_smem()] + [vmem] * 6,
        out_specs=[vmem] * len(shapes) + [in_smem()],
        scratch_shapes=[
            pltpu.VMEM((n * ROWS, 2 * CH), BF16),
            pltpu.VMEM((n, 8, ROWS), F32),
        ],
        compiler_params=params(18),
        cost_estimate=pl.CostEstimate(
            flops=10**8, bytes_accessed=1 << 19, transcendentals=0
        ),
        name="mlp",
    )(idx, *rows, *weights)
    return outs, token


def in_vmem_call(kernel, shapes, name, parts):
    vmem = pl.BlockSpec(memory_space=pltpu.VMEM)
    return pl.pallas_call(
        kernel,
        out_shape=[jax.ShapeDtypeStruct(shape, BF16) for shape in shapes],
        in_specs=[vmem] * len(parts),
        out_specs=[vmem] * len(shapes),
        compiler_params=params(16),
        cost_estimate=pl.CostEstimate(flops=1, bytes_accessed=1 << 19, transcendentals=0),
        name=name,
    )(*parts)


def shards(residual, features, filters, skip_gain, w_out, norm_gain, w_gate, w_up):
    ctx = lax.axis_index("ctx")
    tp = lax.axis_index("tp")
    core, x_lo = tp % 2, ctx % 2
    x_hi, y = tp // 8, (tp // 2) % 4
    feat = features.transpose(1, 0, 2)
    wg, wu = w_gate.T, w_up.T
    gain = norm_gain[None, :]
    wg_oth, wu_oth, gain_oth = shift(wg, k=1), shift(wu, k=1), shift(gain, k=1)

    sent = pl.pallas_call(
        prep_kernel,
        out_shape=jax.ShapeDtypeStruct((N_CTX, 2 * SUB, ROWS), BF16),
        compiler_params=params(56),
        name="prep",
    )(feat, filters)
    recv = lax.all_to_all(sent, "ctx", 0, 0, tiled=True)
    recv, gain_oth = lax.optimization_barrier((recv, gain_oth))
    conv = pl.pallas_call(
        conv_kernel,
        out_shape=jax.ShapeDtypeStruct((N_CTX, SUB, ROWS), BF16),
        scratch_shapes=[
            pltpu.VMEM((N_CTX, 2 * SUB, 256), F32),
            pltpu.VMEM((N_CTX, 3, SUB, 128), F32),
            pltpu.VMEM((N_CTX, SUB, 256), F32),
        ],
        compiler_params=params(14),
        name="conv",
    )(recv, jnp.asarray(dft_tables()))
    conv_rows = lax.all_to_all(conv, "ctx", 0, 0, tiled=True)
    copies = pl.pallas_call(
        mix_kernel,
        out_shape=jax.ShapeDtypeStruct((8, ROWS, CH), BF16),
        compiler_params=params(56),
        name="mix",
    )(conv_rows, feat, skip_gain[None, :])

    mixed = lax.all_to_all(
        copies, "tp", 0, 0, axis_index_groups=PLANE_GROUPS, tiled=True
    )
    mixed_oth = shift(mixed, k=1)
    core_arr = core.astype(jnp.int32)[None]
    half, w_next = out_proj_first(core_arr, mixed, w_out, residual)
    stream_out, stream = out_proj_second(mixed_oth, w_next, half)

    stream, wg_oth, wu_oth = lax.optimization_barrier((stream, wg_oth, wu_oth))
    first = lax.ppermute(stream, AXES, pairs_of(to_row_owner_first))
    second = lax.ppermute(stream, AXES, pairs_of(to_row_owner_second))
    here = (x_lo == core).astype(jnp.int32)[None]
    held = hold(here, stream, second, first)
    gate_w, up_w, mark = load_weights((wg, wg_oth, wu, wu_oth), held[0, :16])
    gain, _ = lax.optimization_barrier((gain, mark))
    z = ctx // 2
    side = jnp.where(z % 2 == 0, -1, 1)
    two_first = lax.ppermute(held, AXES, pairs_of(functools.partial(along, 2)))
    two_second = lax.ppermute(held, AXES, pairs_of(functools.partial(along, -2)))
    one_first = lax.ppermute(held, AXES, pairs_of(functools.partial(along, 1)))
    one_second = lax.ppermute(held, AXES, pairs_of(functools.partial(along, -1)))
    three_first = lax.ppermute(two_first, AXES, pairs_of(functools.partial(along, 1)))
    three_second = lax.ppermute(two_second, AXES, pairs_of(functools.partial(along, -1)))
    opposite = lax.ppermute(two_first, AXES, pairs_of(functools.partial(along, 2)))
    gains = (gain, gain_oth)
    rows = scale([held, one_first, one_second, two_first, two_second], gains)
    rows = rows + scale([three_first, three_second, opposite], gains)

    order = []
    for b in range(4):
        for a in range(2):
            d = (side * (4 * ((x_hi + a) % 2) + (y + b) % 4 - z)) % 8
            order.append(d)
    seen = jnp.stack(order)
    idx = sum(jnp.where(seen == d, at, 0) for d, at in enumerate(ROW_OF)).astype(jnp.int32)

    weights = (gate_w, up_w)
    both, half = (2, FF_PAD, ROWS), (FF_PAD, ROWS)
    (two_far,), then = mlp_part((5,), idx, rows, weights)
    (one_far, three_far), then = mlp_part((3, 7), then, rows, weights)
    near, then = mlp_part((2, 6), then, rows, weights, split=True)
    (two_near, own_far), then = mlp_part((4, 1), then, rows, weights)
    (own_near,), _ = mlp_part((0,), then, rows, weights)
    two_far = shift(two_far, x=2)
    one_far = shift(one_far, y=1)
    three_far = shift(three_far, y=-1)
    up_1 = shift(near[1], y=1)
    gate_3 = shift(near[2], y=-1)
    gate_by, up_by = in_vmem_call(sum_apart_kernel, (half, half), "sum", (two_near, two_far))
    (across,) = in_vmem_call(sum_kernel, (both,), "sum", (own_far, one_far, three_far))
    gate_by = shift(gate_by, y=1)
    up_by = shift(up_by, y=-1)
    across = shift(across, x=2)
    (gate_1,) = in_vmem_call(sum_kernel, (half,), "sum", (near[0], gate_by))
    (up_3,) = in_vmem_call(sum_kernel, (half,), "sum", (near[3], up_by))
    gate_1 = shift(gate_1, y=1)
    up_3 = shift(up_3, y=-1)
    (hidden_t,) = in_vmem_call(
        finish_kernel,
        ((FF_LOC, ROWS),),
        "finish",
        (own_near, across, gate_1, gate_3, up_1, up_3),
    )
    return stream_out, hidden_t.T


def solution(mesh):
    placed = (
        P("ctx", "tp"),
        P("ctx", None, "tp"),
        P("ctx", "tp"),
        P("tp"),
        P(None, "tp"),
        P("tp"),
        P("tp", "ctx"),
        P("tp", "ctx"),
    )
    return jax.shard_map(
        shards,
        mesh=mesh,
        in_specs=placed,
        out_specs=(P("ctx", "tp"), P("tp", "ctx")),
        check_vma=False,
    )
```

```python
import functools
import math

import jax
import jax.numpy as jnp
import numpy as np
from jax import lax
from jax.experimental import pallas as pl
from jax.experimental.pallas import tpu as pltpu
from jax.sharding import PartitionSpec as P

F32 = jnp.float32
BF16 = jnp.bfloat16
AXES = ("ctx", "tp")
N_CTX = 16
N_TP = 16
ROWS = 128
CH = 512
SUB = 32
FF_LOC = 1368
FF_PAD = 1376
EPS = 1e-06
NEAR = 5
ROW_OF = (0, 2, 3, 6, 7, 5, 4, 1)
PLANE_GROUPS = [[xh * 8 + y * 2 + k for xh in range(2) for y in range(4)] for k in range(2)]


def split_index(i):
    c, t = divmod(i, N_TP)
    z, x_lo = divmod(c, 2)
    x_hi, r = divmod(t, 8)
    y, k = divmod(r, 2)
    return z, x_hi * 2 + x_lo, y, k


def join_index(z, x, y, k):
    x = x % 4
    return ((z % 8) * 2 + x % 2) * N_TP + (x // 2) * 8 + (y % 4) * 2 + k % 2


def shift(arr, z=0, x=0, y=0, k=0):
    pairs = []
    for i in range(N_CTX * N_TP):
        az, ax, ay, ak = split_index(i)
        pairs.append((i, join_index(az + z, ax + x, ay + y, ak + k)))
    return lax.ppermute(arr, AXES, pairs)


def split_bf16(table):
    high = np.asarray(table, np.float32).astype(jnp.bfloat16)
    low = (np.asarray(table, np.float32) - high.astype(np.float32)).astype(jnp.bfloat16)
    return high, low


def dft_tables():
    size = 2 * ROWS
    pos = np.arange(ROWS)
    freq = np.arange(ROWS)
    phase = (pos[:, None] * freq[None, :]) % size
    angle = 2.0 * math.pi / size * phase
    cos, sin = np.cos(angle), np.sin(angle)
    sign = np.where(pos % 2 == 0, 1.0, -1.0)
    fwd_im = -sin
    fwd_im[:, 0] = sign
    forward = np.concatenate([cos, fwd_im], axis=1)
    weight = np.where(freq == 0, 1.0, 2.0)[:, None] / size
    inv_re = cos.T * weight
    inv_im = -sin.T * weight
    inv_im[0, :] = sign / size
    inverse = np.concatenate([inv_re, inv_im], axis=0)
    return np.concatenate(split_bf16(forward) + split_bf16(inverse.T), axis=1)


def dot(a, b):
    return jnp.dot(a, b, preferred_element_type=F32)


def dot_nt(a, b):
    return lax.dot_general(a, b, (((1,), (1,)), ((), ())), preferred_element_type=F32)


def prep_kernel(feat_ref, filt_ref, out_ref):
    prod = feat_ref[1].astype(F32) * feat_ref[2].astype(F32)
    filt = filt_ref[...]
    for j in range(CH // 128):
        cols = slice(128 * j, 128 * j + 128)
        out_ref[4 * j : 4 * j + 4, 0:SUB, :] = prod[:, cols].T.astype(BF16).reshape(4, SUB, 128)
        out_ref[4 * j : 4 * j + 4, SUB : 2 * SUB, :] = (
            filt[:, cols].T.astype(BF16).reshape(4, SUB, 128)
        )


def conv_kernel(x_ref, tab_ref, out_ref, spec, filt, outs):
    x = x_ref[...].reshape(N_CTX * 2 * SUB, ROWS)
    spec[...] = (dot(x, tab_ref[:, 0:256]) + dot(x, tab_ref[:, 256:512])).reshape(N_CTX, 2 * SUB, 256)
    lane = lax.broadcasted_iota(jnp.int32, (SUB, 128), 1)
    sign = jnp.where(lane % 2 == 0, 1.0, -1.0).astype(F32)
    first = lane == 0
    for d in range(N_CTX):
        re = spec[d, SUB:, 0:128]
        im = spec[d, SUB:, 128:256]
        if d > 0:
            re = re + sign * spec[d - 1, SUB:, 0:128]
            im = im + sign * spec[d - 1, SUB:, 128:256]
        filt[d, 0] = re
        filt[d, 1] = jnp.where(first, 0.0, im)
        filt[d, 2] = jnp.where(first, im, re)
    for m in range(N_CTX):
        acc_re = jnp.zeros((SUB, 128), F32)
        acc_im = jnp.zeros((SUB, 128), F32)
        for n in range(m + 1):
            pr = spec[n, 0:SUB, 0:128]
            pi = spec[n, 0:SUB, 128:256]
            hr, hz, hq = filt[m - n, 0], filt[m - n, 1], filt[m - n, 2]
            acc_re = acc_re + (pr * hr - pi * hz)
            acc_im = acc_im + (pr * hz + pi * hq)
        outs[m, :, 0:128] = acc_re
        outs[m, :, 128:256] = acc_im
    total = outs[...].reshape(N_CTX * SUB, 256)
    high = total.astype(BF16)
    low = (total - high.astype(F32)).astype(BF16)
    inv_high, inv_low = tab_ref[:, 512:768], tab_ref[:, 768:1024]
    y = dot_nt(high, inv_high) + dot_nt(high, inv_low) + dot_nt(low, inv_high)
    out_ref[...] = y.astype(BF16).reshape(N_CTX, SUB, ROWS)


def mix_kernel(conv_ref, feat_ref, skip_ref, out_ref):
    conv = conv_ref[...].reshape(CH, ROWS).astype(F32)
    for j in range(CH // 128):
        cols = slice(128 * j, 128 * j + 128)
        prod = feat_ref[1, :, cols].astype(F32) * feat_ref[2, :, cols].astype(F32)
        long = conv[cols, :].T
        gate = feat_ref[0, :, cols].astype(F32)
        mixed = (gate * (long + skip_ref[:, cols] * prod)).astype(BF16)
        for copy in range(8):
            out_ref[copy, :, cols] = mixed


def out_proj_first_kernel(
    core_ref, mixed_hbm, w_hbm, start_hbm, out_ref, w_next, mixed, w_buf, start, sem, start_sem
):
    core = core_ref[0]
    copies = []
    for j in range(N_TP // 2):
        rows = pl.ds(pl.multiple_of((2 * j + core) * CH, CH), CH)
        copies.append(pltpu.make_async_copy(mixed_hbm.at[j], mixed.at[j], sem.at[0, j]))
        copies.append(pltpu.make_async_copy(w_hbm.at[rows], w_buf.at[j], sem.at[1, j]))
    later = []
    for j in range(N_TP // 2):
        rows = pl.ds(pl.multiple_of((2 * j + 1 - core) * CH, CH), CH)
        later.append(pltpu.make_async_copy(w_hbm.at[rows], w_next.at[j], sem.at[2, j]))
    start_copy = pltpu.make_async_copy(start_hbm, start, start_sem)
    for copy in [start_copy] + copies + later:
        copy.start()
    start_copy.wait()
    acc = start[...].astype(F32)
    for j in range(N_TP // 2):
        copies[2 * j].wait()
        copies[2 * j + 1].wait()
        acc = acc + dot(mixed[j], w_buf[j])
    out_ref[...] = acc
    for copy in later:
        copy.wait()


def out_proj_second_kernel(mixed_hbm, w_ref, start_ref, out_ref, keep_ref, mixed, sem):
    copies = []
    for j in range(N_TP // 2):
        copies.append(pltpu.make_async_copy(mixed_hbm.at[j], mixed.at[j], sem.at[j]))
        copies[-1].start()
    acc = start_ref[...]
    for j, copy in enumerate(copies):
        copy.wait()
        acc = acc + dot(mixed[j], w_ref[j])
    out_ref[...] = acc.astype(BF16)
    keep_ref[...] = acc.astype(BF16)


def square_sums(values):
    ones = jnp.ones((8, CH), BF16)
    sq = values * values
    high = sq.astype(BF16)
    return dot_nt(ones, high) + dot_nt(ones, (sq - high.astype(F32)).astype(BF16))


def two_rows(total):
    high = total.astype(BF16).astype(F32)
    row = lax.broadcasted_iota(jnp.int32, total.shape, 0)
    return jnp.where(row == 0, high, jnp.where(row == 1, total - high, 0.0))


def with_tail(rows, tail):
    return jnp.concatenate([rows, tail], axis=0).astype(BF16)


def load_kernel(wg_ref, wgx_ref, wu_ref, wux_ref, mark_ref, gate_ref, up_ref, out_mark_ref, sem):
    copies = []
    pieces = ((wg_ref, gate_ref, 0), (wgx_ref, gate_ref, CH), (wu_ref, up_ref, 0), (wux_ref, up_ref, CH))
    for i, (src, dst, at) in enumerate(pieces):
        copies.append(pltpu.make_async_copy(src, dst.at[:, pl.ds(at, CH)], sem.at[i]))
        copies[-1].start()
    for copy in copies:
        copy.wait()
    out_mark_ref[...] = mark_ref[...]


def hold_kernel(here_ref, stream_ref, second_ref, first_ref, out_ref):
    @pl.when(here_ref[0] == 1)
    def _():
        out_ref[0] = stream_ref[...]
        out_ref[1] = first_ref[...]

    @pl.when(here_ref[0] == 0)
    def _():
        out_ref[0] = first_ref[...]
        out_ref[1] = second_ref[...]


def scale_kernel(*refs):
    blocks, (gain_ref, gain_oth_ref, out_ref, tail_ref) = refs[:-4], refs[-4:]
    for i, block in enumerate(blocks):
        own = block[0].astype(F32)
        oth = block[1].astype(F32)
        out_ref[i, :, 0:CH] = (own * gain_ref[...]).astype(BF16)
        out_ref[i, :, CH:] = (oth * gain_oth_ref[...]).astype(BF16)
        tail_ref[i] = two_rows(square_sums(own) + square_sums(oth))


def mlp_kernel(slots, split, idx_ref, *refs):
    rows, (gate_ref, up_ref) = refs[:4], refs[4:6]
    out_refs, order_ref = refs[6:-3], refs[-3]
    scaled, tail = refs[-2:]
    for slot in range(8):
        order_ref[slot] = idx_ref[slot]
    for at, slot in enumerate(slots):
        which = idx_ref[slot]
        span = slice(at * ROWS, at * ROWS + ROWS)

        @pl.when(which < NEAR)
        def _():
            scaled[span, :] = rows[0][which]
            tail[at] = rows[1][which]

        @pl.when(which >= NEAR)
        def _():
            scaled[span, :] = rows[2][which - NEAR]
            tail[at] = rows[3][which - NEAR]

    zeros = jnp.zeros((FF_PAD - FF_LOC, ROWS), F32)
    gate = dot_nt(gate_ref[...], scaled[...])
    for at in range(len(slots)):
        target = out_refs[2 * at] if split else out_refs[at].at[0]
        target[...] = with_tail(gate[:, at * ROWS : at * ROWS + ROWS], zeros)
    up = dot_nt(up_ref[...], scaled[...])
    for at in range(len(slots)):
        target = out_refs[2 * at + 1] if split else out_refs[at].at[1]
        target[...] = with_tail(up[:, at * ROWS : at * ROWS + ROWS], tail[at])


def sum_kernel(*refs):
    total = refs[0][...].astype(F32)
    for ref in refs[1:-1]:
        total = total + ref[...].astype(F32)
    refs[-1][...] = total.astype(BF16)


def sum_apart_kernel(left_ref, right_ref, gate_ref, up_ref):
    for i, out_ref in enumerate((gate_ref, up_ref)):
        out_ref[...] = (left_ref[i].astype(F32) + right_ref[i].astype(F32)).astype(BF16)


def finish_kernel(own_ref, across_ref, gate_1_ref, gate_3_ref, up_1_ref, up_3_ref, out_ref):
    gate = own_ref[0].astype(F32) + across_ref[0].astype(F32)
    gate = gate + (gate_1_ref[...].astype(F32) + gate_3_ref[...].astype(F32))
    up = own_ref[1].astype(F32) + across_ref[1].astype(F32)
    up = up + (up_1_ref[...].astype(F32) + up_3_ref[...].astype(F32))
    sums = up[FF_LOC : FF_LOC + 1] + up[FF_LOC + 1 : FF_LOC + 2]
    scale = lax.rsqrt(sums * (1.0 / (N_TP * CH)) + EPS)
    gate = gate[:FF_LOC] * scale
    out_ref[...] = (gate / (1.0 + jnp.exp(-gate)) * (up[:FF_LOC] * scale)).astype(BF16)


def params(mib):
    return pltpu.CompilerParams(vmem_limit_bytes=mib * 1024 * 1024)


def pairs_of(rule):
    pairs = []
    for i in range(N_CTX * N_TP):
        target = rule(*split_index(i))
        if target is not None:
            pairs.append((i, join_index(*target)))
    return pairs


def to_row_owner_first(z, x, y, k):
    return (z, x ^ 1, y, k) if k == x % 2 else (z, x, y, k ^ 1)


def to_row_owner_second(z, x, y, k):
    return None if k == x % 2 else (z, x ^ 1, y, k ^ 1)


def in_smem():
    return pl.BlockSpec(memory_space=pltpu.SMEM)


def anywhere():
    return pl.BlockSpec(memory_space=pl.ANY)


def along(steps, z, x, y, k):
    return (z + steps, x, y, k) if z % 2 == 0 else (z - steps, x, y, k)


def out_proj_first(core, mixed, w_out, start):
    vmem = pl.BlockSpec(memory_space=pltpu.VMEM)
    return pl.pallas_call(
        out_proj_first_kernel,
        out_shape=[
            jax.ShapeDtypeStruct((ROWS, CH), F32),
            jax.ShapeDtypeStruct((N_TP // 2, CH, CH), BF16),
        ],
        in_specs=[in_smem(), anywhere(), anywhere(), anywhere()],
        out_specs=[vmem] * 2,
        scratch_shapes=[
            pltpu.VMEM((N_TP // 2, ROWS, CH), BF16),
            pltpu.VMEM((N_TP // 2, CH, CH), BF16),
            pltpu.VMEM((ROWS, CH), BF16),
            pltpu.SemaphoreType.DMA((3, N_TP // 2)),
            pltpu.SemaphoreType.DMA,
        ],
        compiler_params=params(43),
        cost_estimate=pl.CostEstimate(
            flops=2 * ROWS * CH * N_TP // 2 * CH, bytes_accessed=9 << 20, transcendentals=0
        ),
        name="out_proj_first",
    )(core, mixed, w_out, start)


def out_proj_second(mixed, weights, start):
    vmem = pl.BlockSpec(memory_space=pltpu.VMEM)
    return pl.pallas_call(
        out_proj_second_kernel,
        out_shape=[jax.ShapeDtypeStruct((ROWS, CH), BF16)] * 2,
        in_specs=[anywhere(), vmem, vmem],
        out_specs=[vmem] * 2,
        scratch_shapes=[
            pltpu.VMEM((N_TP // 2, ROWS, CH), BF16),
            pltpu.SemaphoreType.DMA((N_TP // 2,)),
        ],
        compiler_params=params(16),
        cost_estimate=pl.CostEstimate(
            flops=2 * ROWS * CH * N_TP // 2 * CH, bytes_accessed=1 << 20, transcendentals=0
        ),
        name="out_proj_second",
    )(mixed, weights, start)


def hold(here, *parts):
    vmem = pl.BlockSpec(memory_space=pltpu.VMEM)
    return pl.pallas_call(
        hold_kernel,
        out_shape=jax.ShapeDtypeStruct((2, ROWS, CH), BF16),
        in_specs=[in_smem()] + [vmem] * 3,
        out_specs=vmem,
        compiler_params=params(14),
        cost_estimate=pl.CostEstimate(flops=1, bytes_accessed=1 << 19, transcendentals=0),
        name="hold",
    )(here, *parts)


def load_weights(weights, mark):
    vmem = pl.BlockSpec(memory_space=pltpu.VMEM)
    return pl.pallas_call(
        load_kernel,
        out_shape=[jax.ShapeDtypeStruct((FF_LOC, 2 * CH), BF16)] * 2
        + [jax.ShapeDtypeStruct(mark.shape, mark.dtype)],
        in_specs=[anywhere()] * 4 + [vmem],
        out_specs=[vmem] * 3,
        scratch_shapes=[pltpu.SemaphoreType.DMA((4,))],
        compiler_params=params(16),
        cost_estimate=pl.CostEstimate(flops=1, bytes_accessed=12 << 20, transcendentals=0),
        name="load",
    )(*weights, mark)


def scale(blocks, gains):
    n = len(blocks)
    return pl.pallas_call(
        scale_kernel,
        out_shape=[
            jax.ShapeDtypeStruct((n, ROWS, 2 * CH), BF16),
            jax.ShapeDtypeStruct((n, 8, ROWS), F32),
        ],
        compiler_params=params(14),
        cost_estimate=pl.CostEstimate(
            flops=8 * n * ROWS * CH * 8, bytes_accessed=n << 19, transcendentals=0
        ),
        name="scale",
    )(*blocks, *gains)


def mlp_part(slots, idx, rows, weights, split=False):
    n = len(slots)
    shapes = [(FF_PAD, ROWS)] * (2 * n) if split else [(2, FF_PAD, ROWS)] * n
    vmem = pl.BlockSpec(memory_space=pltpu.VMEM)
    *outs, token = pl.pallas_call(
        functools.partial(mlp_kernel, slots, split),
        out_shape=[jax.ShapeDtypeStruct(shape, BF16) for shape in shapes]
        + [jax.ShapeDtypeStruct((8,), jnp.int32)],
        in_specs=[in_smem()] + [vmem] * 6,
        out_specs=[vmem] * len(shapes) + [in_smem()],
        scratch_shapes=[
            pltpu.VMEM((n * ROWS, 2 * CH), BF16),
            pltpu.VMEM((n, 8, ROWS), F32),
        ],
        compiler_params=params(18),
        cost_estimate=pl.CostEstimate(
            flops=10**8, bytes_accessed=1 << 19, transcendentals=0
        ),
        name="mlp",
    )(idx, *rows, *weights)
    return outs, token


def in_vmem_call(kernel, shapes, name, parts):
    vmem = pl.BlockSpec(memory_space=pltpu.VMEM)
    return pl.pallas_call(
        kernel,
        out_shape=[jax.ShapeDtypeStruct(shape, BF16) for shape in shapes],
        in_specs=[vmem] * len(parts),
        out_specs=[vmem] * len(shapes),
        compiler_params=params(16),
        cost_estimate=pl.CostEstimate(flops=1, bytes_accessed=1 << 19, transcendentals=0),
        name=name,
    )(*parts)


def shards(residual, features, filters, skip_gain, w_out, norm_gain, w_gate, w_up):
    ctx = lax.axis_index("ctx")
    tp = lax.axis_index("tp")
    core, x_lo = tp % 2, ctx % 2
    x_hi, y = tp // 8, (tp // 2) % 4
    feat = features.transpose(1, 0, 2)
    wg, wu = w_gate.T, w_up.T
    gain = norm_gain[None, :]
    wg_oth, wu_oth, gain_oth = shift(wg, k=1), shift(wu, k=1), shift(gain, k=1)

    sent = pl.pallas_call(
        prep_kernel,
        out_shape=jax.ShapeDtypeStruct((N_CTX, 2 * SUB, ROWS), BF16),
        compiler_params=params(56),
        name="prep",
    )(feat, filters)
    recv = lax.all_to_all(sent, "ctx", 0, 0, tiled=True)
    recv, gain_oth = lax.optimization_barrier((recv, gain_oth))
    conv = pl.pallas_call(
        conv_kernel,
        out_shape=jax.ShapeDtypeStruct((N_CTX, SUB, ROWS), BF16),
        scratch_shapes=[
            pltpu.VMEM((N_CTX, 2 * SUB, 256), F32),
            pltpu.VMEM((N_CTX, 3, SUB, 128), F32),
            pltpu.VMEM((N_CTX, SUB, 256), F32),
        ],
        compiler_params=params(14),
        name="conv",
    )(recv, jnp.asarray(dft_tables()))
    conv_rows = lax.all_to_all(conv, "ctx", 0, 0, tiled=True)
    copies = pl.pallas_call(
        mix_kernel,
        out_shape=jax.ShapeDtypeStruct((8, ROWS, CH), BF16),
        compiler_params=params(56),
        name="mix",
    )(conv_rows, feat, skip_gain[None, :])

    mixed = lax.all_to_all(
        copies, "tp", 0, 0, axis_index_groups=PLANE_GROUPS, tiled=True
    )
    mixed_oth = shift(mixed, k=1)
    core_arr = core.astype(jnp.int32)[None]
    half, w_next = out_proj_first(core_arr, mixed, w_out, residual)
    stream_out, stream = out_proj_second(mixed_oth, w_next, half)

    stream, wg_oth, wu_oth = lax.optimization_barrier((stream, wg_oth, wu_oth))
    first = lax.ppermute(stream, AXES, pairs_of(to_row_owner_first))
    second = lax.ppermute(stream, AXES, pairs_of(to_row_owner_second))
    here = (x_lo == core).astype(jnp.int32)[None]
    held = hold(here, stream, second, first)
    gate_w, up_w, mark = load_weights((wg, wg_oth, wu, wu_oth), held[0, :16])
    gain, _ = lax.optimization_barrier((gain, mark))
    z = ctx // 2
    side = jnp.where(z % 2 == 0, -1, 1)
    two_first = lax.ppermute(held, AXES, pairs_of(functools.partial(along, 2)))
    two_second = lax.ppermute(held, AXES, pairs_of(functools.partial(along, -2)))
    one_first = lax.ppermute(held, AXES, pairs_of(functools.partial(along, 1)))
    one_second = lax.ppermute(held, AXES, pairs_of(functools.partial(along, -1)))
    three_first = lax.ppermute(two_first, AXES, pairs_of(functools.partial(along, 1)))
    three_second = lax.ppermute(two_second, AXES, pairs_of(functools.partial(along, -1)))
    opposite = lax.ppermute(two_first, AXES, pairs_of(functools.partial(along, 2)))
    gains = (gain, gain_oth)
    rows = scale([held, one_first, one_second, two_first, two_second], gains)
    rows = rows + scale([three_first, three_second, opposite], gains)

    order = []
    for b in range(4):
        for a in range(2):
            d = (side * (4 * ((x_hi + a) % 2) + (y + b) % 4 - z)) % 8
            order.append(d)
    seen = jnp.stack(order)
    idx = sum(jnp.where(seen == d, at, 0) for d, at in enumerate(ROW_OF)).astype(jnp.int32)

    weights = (gate_w, up_w)
    both, half = (2, FF_PAD, ROWS), (FF_PAD, ROWS)
    (two_far,), then = mlp_part((5,), idx, rows, weights)
    (one_far, three_far), then = mlp_part((3, 7), then, rows, weights)
    near, then = mlp_part((2, 6), then, rows, weights, split=True)
    (two_near, own_far), then = mlp_part((4, 1), then, rows, weights)
    (own_near,), _ = mlp_part((0,), then, rows, weights)
    two_far = shift(two_far, x=2)
    one_far = shift(one_far, y=1)
    three_far = shift(three_far, y=-1)
    up_1 = shift(near[1], y=1)
    gate_3 = shift(near[2], y=-1)
    gate_by, up_by = in_vmem_call(sum_apart_kernel, (half, half), "sum", (two_near, two_far))
    (across,) = in_vmem_call(sum_kernel, (both,), "sum", (own_far, one_far, three_far))
    gate_by = shift(gate_by, y=1)
    up_by = shift(up_by, y=-1)
    across = shift(across, x=2)
    (gate_1,) = in_vmem_call(sum_kernel, (half,), "sum", (near[0], gate_by))
    (up_3,) = in_vmem_call(sum_kernel, (half,), "sum", (near[3], up_by))
    gate_1 = shift(gate_1, y=1)
    up_3 = shift(up_3, y=-1)
    (hidden_t,) = in_vmem_call(
        finish_kernel,
        ((FF_LOC, ROWS),),
        "finish",
        (own_near, across, gate_1, gate_3, up_1, up_3),
    )
    return stream_out, hidden_t.T


def solution(mesh):
    placed = (
        P("ctx", "tp"),
        P("ctx", None, "tp"),
        P("ctx", "tp"),
        P("tp"),
        P(None, "tp"),
        P("tp"),
        P("tp", "ctx"),
        P("tp", "ctx"),
    )
    return jax.shard_map(
        shards,
        mesh=mesh,
        in_specs=placed,
        out_specs=(P("ctx", "tp"), P("tp", "ctx")),
        check_vma=False,
    )
```

```python
import functools
import math

import jax
import jax.numpy as jnp
import numpy as np
from jax import lax
from jax.experimental import pallas as pl
from jax.experimental.pallas import tpu as pltpu
from jax.sharding import PartitionSpec as P

F32 = jnp.float32
BF16 = jnp.bfloat16
AXES = ("ctx", "tp")
N_CTX = 16
N_TP = 16
ROWS = 128
CH = 512
SUB = 32
FF_LOC = 1368
FF_PAD = 1376
EPS = 1e-06
NEAR = 5
ROW_OF = (0, 2, 3, 6, 7, 5, 4, 1)
PLANE_GROUPS = [[xh * 8 + y * 2 + k for xh in range(2) for y in range(4)] for k in range(2)]


def split_index(i):
    c, t = divmod(i, N_TP)
    z, x_lo = divmod(c, 2)
    x_hi, r = divmod(t, 8)
    y, k = divmod(r, 2)
    return z, x_hi * 2 + x_lo, y, k


def join_index(z, x, y, k):
    x = x % 4
    return ((z % 8) * 2 + x % 2) * N_TP + (x // 2) * 8 + (y % 4) * 2 + k % 2


def shift(arr, z=0, x=0, y=0, k=0):
    pairs = []
    for i in range(N_CTX * N_TP):
        az, ax, ay, ak = split_index(i)
        pairs.append((i, join_index(az + z, ax + x, ay + y, ak + k)))
    return lax.ppermute(arr, AXES, pairs)


def split_bf16(table):
    high = np.asarray(table, np.float32).astype(jnp.bfloat16)
    low = (np.asarray(table, np.float32) - high.astype(np.float32)).astype(jnp.bfloat16)
    return high, low


def dft_tables():
    size = 2 * ROWS
    pos = np.arange(ROWS)
    freq = np.arange(ROWS)
    phase = (pos[:, None] * freq[None, :]) % size
    angle = 2.0 * math.pi / size * phase
    cos, sin = np.cos(angle), np.sin(angle)
    sign = np.where(pos % 2 == 0, 1.0, -1.0)
    fwd_im = -sin
    fwd_im[:, 0] = sign
    forward = np.concatenate([cos, fwd_im], axis=1)
    weight = np.where(freq == 0, 1.0, 2.0)[:, None] / size
    inv_re = cos.T * weight
    inv_im = -sin.T * weight
    inv_im[0, :] = sign / size
    inverse = np.concatenate([inv_re, inv_im], axis=0)
    return np.concatenate(split_bf16(forward) + split_bf16(inverse.T), axis=1)


def dot(a, b):
    return jnp.dot(a, b, preferred_element_type=F32)


def dot_nt(a, b):
    return lax.dot_general(a, b, (((1,), (1,)), ((), ())), preferred_element_type=F32)


def prep_kernel(feat_ref, filt_ref, out_ref):
    prod = feat_ref[1].astype(F32) * feat_ref[2].astype(F32)
    filt = filt_ref[...]
    for j in range(CH // 128):
        cols = slice(128 * j, 128 * j + 128)
        out_ref[4 * j : 4 * j + 4, 0:SUB, :] = prod[:, cols].T.astype(BF16).reshape(4, SUB, 128)
        out_ref[4 * j : 4 * j + 4, SUB : 2 * SUB, :] = (
            filt[:, cols].T.astype(BF16).reshape(4, SUB, 128)
        )


def conv_kernel(x_ref, tab_ref, out_ref, spec, filt, outs):
    x = x_ref[...].reshape(N_CTX * 2 * SUB, ROWS)
    spec[...] = (dot(x, tab_ref[:, 0:256]) + dot(x, tab_ref[:, 256:512])).reshape(N_CTX, 2 * SUB, 256)
    lane = lax.broadcasted_iota(jnp.int32, (SUB, 128), 1)
    sign = jnp.where(lane % 2 == 0, 1.0, -1.0).astype(F32)
    first = lane == 0
    for d in range(N_CTX):
        re = spec[d, SUB:, 0:128]
        im = spec[d, SUB:, 128:256]
        if d > 0:
            re = re + sign * spec[d - 1, SUB:, 0:128]
            im = im + sign * spec[d - 1, SUB:, 128:256]
        filt[d, 0] = re
        filt[d, 1] = jnp.where(first, 0.0, im)
        filt[d, 2] = jnp.where(first, im, re)
    for m in range(N_CTX):
        acc_re = jnp.zeros((SUB, 128), F32)
        acc_im = jnp.zeros((SUB, 128), F32)
        for n in range(m + 1):
            pr = spec[n, 0:SUB, 0:128]
            pi = spec[n, 0:SUB, 128:256]
            hr, hz, hq = filt[m - n, 0], filt[m - n, 1], filt[m - n, 2]
            acc_re = acc_re + (pr * hr - pi * hz)
            acc_im = acc_im + (pr * hz + pi * hq)
        outs[m, :, 0:128] = acc_re
        outs[m, :, 128:256] = acc_im
    total = outs[...].reshape(N_CTX * SUB, 256)
    high = total.astype(BF16)
    low = (total - high.astype(F32)).astype(BF16)
    inv_high, inv_low = tab_ref[:, 512:768], tab_ref[:, 768:1024]
    y = dot_nt(high, inv_high) + dot_nt(high, inv_low) + dot_nt(low, inv_high)
    out_ref[...] = y.astype(BF16).reshape(N_CTX, SUB, ROWS)


def mix_kernel(conv_ref, feat_ref, skip_ref, out_ref):
    conv = conv_ref[...].reshape(CH, ROWS).astype(F32)
    for j in range(CH // 128):
        cols = slice(128 * j, 128 * j + 128)
        prod = feat_ref[1, :, cols].astype(F32) * feat_ref[2, :, cols].astype(F32)
        long = conv[cols, :].T
        gate = feat_ref[0, :, cols].astype(F32)
        mixed = (gate * (long + skip_ref[:, cols] * prod)).astype(BF16)
        for copy in range(8):
            out_ref[copy, :, cols] = mixed


def out_proj_kernel(offset, core_ref, mixed_hbm, w_hbm, start_ref, *refs):
    *out_refs, mixed, w_buf, sem = refs
    first = jnp.bitwise_xor(core_ref[0], offset)
    copies = []
    for j in range(N_TP // 2):
        rows = pl.ds(pl.multiple_of((2 * j + first) * CH, CH), CH)
        copies.append(
            (
                pltpu.make_async_copy(mixed_hbm.at[j], mixed.at[j], sem.at[0, j]),
                pltpu.make_async_copy(w_hbm.at[rows], w_buf.at[j], sem.at[1, j]),
            )
        )
    for pair in copies:
        for copy in pair:
            copy.start()
    acc = start_ref[...].astype(F32)
    for j, pair in enumerate(copies):
        for copy in pair:
            copy.wait()
        acc = acc + dot(mixed[j], w_buf[j])
    for out_ref in out_refs:
        out_ref[...] = acc.astype(out_ref.dtype)


def square_sums(values):
    ones = jnp.ones((8, CH), BF16)
    sq = values * values
    high = sq.astype(BF16)
    return dot_nt(ones, high) + dot_nt(ones, (sq - high.astype(F32)).astype(BF16))


def two_rows(total):
    high = total.astype(BF16).astype(F32)
    row = lax.broadcasted_iota(jnp.int32, total.shape, 0)
    return jnp.where(row == 0, high, jnp.where(row == 1, total - high, 0.0))


def with_tail(rows, tail):
    return jnp.concatenate([rows, tail], axis=0).astype(BF16)


def load_kernel(wg_ref, wgx_ref, wu_ref, wux_ref, mark_ref, gate_ref, up_ref, out_mark_ref, sem):
    copies = []
    pieces = ((wg_ref, gate_ref, 0), (wgx_ref, gate_ref, CH), (wu_ref, up_ref, 0), (wux_ref, up_ref, CH))
    for i, (src, dst, at) in enumerate(pieces):
        copies.append(pltpu.make_async_copy(src, dst.at[:, pl.ds(at, CH)], sem.at[i]))
        copies[-1].start()
    for copy in copies:
        copy.wait()
    out_mark_ref[...] = mark_ref[...]


def hold_kernel(here_ref, stream_ref, second_ref, first_ref, out_ref):
    @pl.when(here_ref[0] == 1)
    def _():
        out_ref[0] = stream_ref[...]
        out_ref[1] = first_ref[...]

    @pl.when(here_ref[0] == 0)
    def _():
        out_ref[0] = first_ref[...]
        out_ref[1] = second_ref[...]


def scale_kernel(*refs):
    blocks, (gain_ref, gain_oth_ref, out_ref, tail_ref) = refs[:-4], refs[-4:]
    for i, block in enumerate(blocks):
        own = block[0].astype(F32)
        oth = block[1].astype(F32)
        out_ref[i, :, 0:CH] = (own * gain_ref[...]).astype(BF16)
        out_ref[i, :, CH:] = (oth * gain_oth_ref[...]).astype(BF16)
        tail_ref[i] = two_rows(square_sums(own) + square_sums(oth))


def mlp_kernel(slots, split, idx_ref, *refs):
    rows, (gate_ref, up_ref) = refs[:4], refs[4:6]
    out_refs, order_ref = refs[6:-3], refs[-3]
    scaled, tail = refs[-2:]
    for slot in range(8):
        order_ref[slot] = idx_ref[slot]
    for at, slot in enumerate(slots):
        which = idx_ref[slot]
        span = slice(at * ROWS, at * ROWS + ROWS)

        @pl.when(which < NEAR)
        def _():
            scaled[span, :] = rows[0][which]
            tail[at] = rows[1][which]

        @pl.when(which >= NEAR)
        def _():
            scaled[span, :] = rows[2][which - NEAR]
            tail[at] = rows[3][which - NEAR]

    zeros = jnp.zeros((FF_PAD - FF_LOC, ROWS), F32)
    gate = dot_nt(gate_ref[...], scaled[...])
    for at in range(len(slots)):
        target = out_refs[2 * at] if split else out_refs[at].at[0]
        target[...] = with_tail(gate[:, at * ROWS : at * ROWS + ROWS], zeros)
    up = dot_nt(up_ref[...], scaled[...])
    for at in range(len(slots)):
        target = out_refs[2 * at + 1] if split else out_refs[at].at[1]
        target[...] = with_tail(up[:, at * ROWS : at * ROWS + ROWS], tail[at])


def sum_kernel(*refs):
    total = refs[0][...].astype(F32)
    for ref in refs[1:-1]:
        total = total + ref[...].astype(F32)
    refs[-1][...] = total.astype(BF16)


def sum_apart_kernel(left_ref, right_ref, gate_ref, up_ref):
    for i, out_ref in enumerate((gate_ref, up_ref)):
        out_ref[...] = (left_ref[i].astype(F32) + right_ref[i].astype(F32)).astype(BF16)


def finish_kernel(own_ref, across_ref, gate_1_ref, gate_3_ref, up_1_ref, up_3_ref, out_ref):
    gate = own_ref[0].astype(F32) + across_ref[0].astype(F32)
    gate = gate + (gate_1_ref[...].astype(F32) + gate_3_ref[...].astype(F32))
    up = own_ref[1].astype(F32) + across_ref[1].astype(F32)
    up = up + (up_1_ref[...].astype(F32) + up_3_ref[...].astype(F32))
    sums = up[FF_LOC : FF_LOC + 1] + up[FF_LOC + 1 : FF_LOC + 2]
    scale = lax.rsqrt(sums * (1.0 / (N_TP * CH)) + EPS)
    gate = gate[:FF_LOC] * scale
    out_ref[...] = (gate / (1.0 + jnp.exp(-gate)) * (up[:FF_LOC] * scale)).astype(BF16)


def params(mib):
    return pltpu.CompilerParams(vmem_limit_bytes=mib * 1024 * 1024)


def pairs_of(rule):
    pairs = []
    for i in range(N_CTX * N_TP):
        target = rule(*split_index(i))
        if target is not None:
            pairs.append((i, join_index(*target)))
    return pairs


def to_row_owner_first(z, x, y, k):
    return (z, x ^ 1, y, k) if k == x % 2 else (z, x, y, k ^ 1)


def to_row_owner_second(z, x, y, k):
    return None if k == x % 2 else (z, x ^ 1, y, k ^ 1)


def in_smem():
    return pl.BlockSpec(memory_space=pltpu.SMEM)


def anywhere():
    return pl.BlockSpec(memory_space=pl.ANY)


def along(steps, z, x, y, k):
    return (z + steps, x, y, k) if z % 2 == 0 else (z - steps, x, y, k)


def out_proj(offset, core, mixed, w_out, start, dtype, copies):
    return pl.pallas_call(
        functools.partial(out_proj_kernel, offset),
        out_shape=[jax.ShapeDtypeStruct((ROWS, CH), dtype)] * copies,
        in_specs=[
            in_smem(),
            anywhere(),
            pl.BlockSpec(memory_space=pltpu.HBM),
            pl.BlockSpec(memory_space=pltpu.VMEM),
        ],
        scratch_shapes=[
            pltpu.VMEM((N_TP // 2, ROWS, CH), BF16),
            pltpu.VMEM((N_TP // 2, CH, CH), BF16),
            pltpu.SemaphoreType.DMA((2, N_TP // 2)),
        ],
        compiler_params=params(51),
        cost_estimate=pl.CostEstimate(
            flops=2 * ROWS * CH * N_TP // 2 * CH, bytes_accessed=5 << 20, transcendentals=0
        ),
        name="out_proj",
    )(core, mixed, w_out, start)


def hold(here, *parts):
    vmem = pl.BlockSpec(memory_space=pltpu.VMEM)
    return pl.pallas_call(
        hold_kernel,
        out_shape=jax.ShapeDtypeStruct((2, ROWS, CH), BF16),
        in_specs=[in_smem()] + [vmem] * 3,
        out_specs=vmem,
        compiler_params=params(14),
        cost_estimate=pl.CostEstimate(flops=1, bytes_accessed=1 << 19, transcendentals=0),
        name="hold",
    )(here, *parts)


def load_weights(weights, mark):
    vmem = pl.BlockSpec(memory_space=pltpu.VMEM)
    return pl.pallas_call(
        load_kernel,
        out_shape=[jax.ShapeDtypeStruct((FF_LOC, 2 * CH), BF16)] * 2
        + [jax.ShapeDtypeStruct(mark.shape, mark.dtype)],
        in_specs=[anywhere()] * 4 + [vmem],
        out_specs=[vmem] * 3,
        scratch_shapes=[pltpu.SemaphoreType.DMA((4,))],
        compiler_params=params(16),
        cost_estimate=pl.CostEstimate(flops=1, bytes_accessed=12 << 20, transcendentals=0),
        name="load",
    )(*weights, mark)


def scale(blocks, gains):
    n = len(blocks)
    return pl.pallas_call(
        scale_kernel,
        out_shape=[
            jax.ShapeDtypeStruct((n, ROWS, 2 * CH), BF16),
            jax.ShapeDtypeStruct((n, 8, ROWS), F32),
        ],
        compiler_params=params(14),
        cost_estimate=pl.CostEstimate(
            flops=8 * n * ROWS * CH * 8, bytes_accessed=n << 19, transcendentals=0
        ),
        name="scale",
    )(*blocks, *gains)


def mlp_part(slots, idx, rows, weights, split=False):
    n = len(slots)
    shapes = [(FF_PAD, ROWS)] * (2 * n) if split else [(2, FF_PAD, ROWS)] * n
    vmem = pl.BlockSpec(memory_space=pltpu.VMEM)
    *outs, token = pl.pallas_call(
        functools.partial(mlp_kernel, slots, split),
        out_shape=[jax.ShapeDtypeStruct(shape, BF16) for shape in shapes]
        + [jax.ShapeDtypeStruct((8,), jnp.int32)],
        in_specs=[in_smem()] + [vmem] * 6,
        out_specs=[vmem] * len(shapes) + [in_smem()],
        scratch_shapes=[
            pltpu.VMEM((n * ROWS, 2 * CH), BF16),
            pltpu.VMEM((n, 8, ROWS), F32),
        ],
        compiler_params=params(18),
        cost_estimate=pl.CostEstimate(
            flops=10**8, bytes_accessed=1 << 19, transcendentals=0
        ),
        name="mlp",
    )(idx, *rows, *weights)
    return outs, token


def in_vmem_call(kernel, shapes, name, parts):
    vmem = pl.BlockSpec(memory_space=pltpu.VMEM)
    return pl.pallas_call(
        kernel,
        out_shape=[jax.ShapeDtypeStruct(shape, BF16) for shape in shapes],
        in_specs=[vmem] * len(parts),
        out_specs=[vmem] * len(shapes),
        compiler_params=params(16),
        cost_estimate=pl.CostEstimate(flops=1, bytes_accessed=1 << 19, transcendentals=0),
        name=name,
    )(*parts)


def shards(residual, features, filters, skip_gain, w_out, norm_gain, w_gate, w_up):
    ctx = lax.axis_index("ctx")
    tp = lax.axis_index("tp")
    core, x_lo = tp % 2, ctx % 2
    x_hi, y = tp // 8, (tp // 2) % 4
    feat = features.transpose(1, 0, 2)
    wg, wu = w_gate.T, w_up.T
    gain = norm_gain[None, :]
    wg_oth, wu_oth, gain_oth = shift(wg, k=1), shift(wu, k=1), shift(gain, k=1)

    sent = pl.pallas_call(
        prep_kernel,
        out_shape=jax.ShapeDtypeStruct((N_CTX, 2 * SUB, ROWS), BF16),
        compiler_params=params(56),
        name="prep",
    )(feat, filters)
    recv = lax.all_to_all(sent, "ctx", 0, 0, tiled=True)
    recv, gain_oth = lax.optimization_barrier((recv, gain_oth))
    conv = pl.pallas_call(
        conv_kernel,
        out_shape=jax.ShapeDtypeStruct((N_CTX, SUB, ROWS), BF16),
        scratch_shapes=[
            pltpu.VMEM((N_CTX, 2 * SUB, 256), F32),
            pltpu.VMEM((N_CTX, 3, SUB, 128), F32),
            pltpu.VMEM((N_CTX, SUB, 256), F32),
        ],
        compiler_params=params(14),
        name="conv",
    )(recv, jnp.asarray(dft_tables()))
    conv_rows = lax.all_to_all(conv, "ctx", 0, 0, tiled=True)
    copies = pl.pallas_call(
        mix_kernel,
        out_shape=jax.ShapeDtypeStruct((8, ROWS, CH), BF16),
        compiler_params=params(56),
        name="mix",
    )(conv_rows, feat, skip_gain[None, :])

    mixed = lax.all_to_all(
        copies, "tp", 0, 0, axis_index_groups=PLANE_GROUPS, tiled=True
    )
    mixed_oth = shift(mixed, k=1)
    core_arr = core.astype(jnp.int32)[None]
    (half,) = out_proj(0, core_arr, mixed, w_out, residual, F32, 1)
    stream_out, stream = out_proj(1, core_arr, mixed_oth, w_out, half, BF16, 2)

    stream, wg_oth, wu_oth = lax.optimization_barrier((stream, wg_oth, wu_oth))
    first = lax.ppermute(stream, AXES, pairs_of(to_row_owner_first))
    second = lax.ppermute(stream, AXES, pairs_of(to_row_owner_second))
    here = (x_lo == core).astype(jnp.int32)[None]
    held = hold(here, stream, second, first)
    gate_w, up_w, mark = load_weights((wg, wg_oth, wu, wu_oth), held[0, :16])
    gain, _ = lax.optimization_barrier((gain, mark))
    z = ctx // 2
    side = jnp.where(z % 2 == 0, -1, 1)
    two_first = lax.ppermute(held, AXES, pairs_of(functools.partial(along, 2)))
    two_second = lax.ppermute(held, AXES, pairs_of(functools.partial(along, -2)))
    one_first = lax.ppermute(held, AXES, pairs_of(functools.partial(along, 1)))
    one_second = lax.ppermute(held, AXES, pairs_of(functools.partial(along, -1)))
    three_first = lax.ppermute(two_first, AXES, pairs_of(functools.partial(along, 1)))
    three_second = lax.ppermute(two_second, AXES, pairs_of(functools.partial(along, -1)))
    opposite = lax.ppermute(two_first, AXES, pairs_of(functools.partial(along, 2)))
    gains = (gain, gain_oth)
    rows = scale([held, one_first, one_second, two_first, two_second], gains)
    rows = rows + scale([three_first, three_second, opposite], gains)

    order = []
    for b in range(4):
        for a in range(2):
            d = (side * (4 * ((x_hi + a) % 2) + (y + b) % 4 - z)) % 8
            order.append(d)
    seen = jnp.stack(order)
    idx = sum(jnp.where(seen == d, at, 0) for d, at in enumerate(ROW_OF)).astype(jnp.int32)

    weights = (gate_w, up_w)
    both, half = (2, FF_PAD, ROWS), (FF_PAD, ROWS)
    (two_far,), then = mlp_part((5,), idx, rows, weights)
    (one_far, three_far), then = mlp_part((3, 7), then, rows, weights)
    near, then = mlp_part((2, 6), then, rows, weights, split=True)
    (two_near, own_far), then = mlp_part((4, 1), then, rows, weights)
    (own_near,), _ = mlp_part((0,), then, rows, weights)
    two_far = shift(two_far, x=2)
    one_far = shift(one_far, y=1)
    three_far = shift(three_far, y=-1)
    up_1 = shift(near[1], y=1)
    gate_3 = shift(near[2], y=-1)
    gate_by, up_by = in_vmem_call(sum_apart_kernel, (half, half), "sum", (two_near, two_far))
    (across,) = in_vmem_call(sum_kernel, (both,), "sum", (own_far, one_far, three_far))
    gate_by = shift(gate_by, y=1)
    up_by = shift(up_by, y=-1)
    across = shift(across, x=2)
    (gate_1,) = in_vmem_call(sum_kernel, (half,), "sum", (near[0], gate_by))
    (up_3,) = in_vmem_call(sum_kernel, (half,), "sum", (near[3], up_by))
    gate_1 = shift(gate_1, y=1)
    up_3 = shift(up_3, y=-1)
    (hidden_t,) = in_vmem_call(
        finish_kernel,
        ((FF_LOC, ROWS),),
        "finish",
        (own_near, across, gate_1, gate_3, up_1, up_3),
    )
    return stream_out, hidden_t.T


def solution(mesh):
    placed = (
        P("ctx", "tp"),
        P("ctx", None, "tp"),
        P("ctx", "tp"),
        P("tp"),
        P(None, "tp"),
        P("tp"),
        P("tp", "ctx"),
        P("tp", "ctx"),
    )
    return jax.shard_map(
        shards,
        mesh=mesh,
        in_specs=placed,
        out_specs=(P("ctx", "tp"), P("tp", "ctx")),
        check_vma=False,
    )
```

```python
import functools
import math

import jax
import jax.numpy as jnp
import numpy as np
from jax import lax
from jax.experimental import pallas as pl
from jax.experimental.pallas import tpu as pltpu
from jax.sharding import PartitionSpec as P

F32 = jnp.float32
BF16 = jnp.bfloat16
AXES = ("ctx", "tp")
N_CTX = 16
N_TP = 16
ROWS = 128
CH = 512
SUB = 32
FF_LOC = 1368
FF_PAD = 1376
EPS = 1e-06
NEAR = 5
ROW_OF = (0, 2, 3, 6, 7, 5, 4, 1)
PLANE_GROUPS = [[xh * 8 + y * 2 + k for xh in range(2) for y in range(4)] for k in range(2)]


def split_index(i):
    c, t = divmod(i, N_TP)
    z, x_lo = divmod(c, 2)
    x_hi, r = divmod(t, 8)
    y, k = divmod(r, 2)
    return z, x_hi * 2 + x_lo, y, k


def join_index(z, x, y, k):
    x = x % 4
    return ((z % 8) * 2 + x % 2) * N_TP + (x // 2) * 8 + (y % 4) * 2 + k % 2


def shift(arr, z=0, x=0, y=0, k=0):
    pairs = []
    for i in range(N_CTX * N_TP):
        az, ax, ay, ak = split_index(i)
        pairs.append((i, join_index(az + z, ax + x, ay + y, ak + k)))
    return lax.ppermute(arr, AXES, pairs)


def split_bf16(table):
    high = np.asarray(table, np.float32).astype(jnp.bfloat16)
    low = (np.asarray(table, np.float32) - high.astype(np.float32)).astype(jnp.bfloat16)
    return high, low


def dft_tables():
    size = 2 * ROWS
    pos = np.arange(ROWS)
    freq = np.arange(ROWS)
    phase = (pos[:, None] * freq[None, :]) % size
    angle = 2.0 * math.pi / size * phase
    cos, sin = np.cos(angle), np.sin(angle)
    sign = np.where(pos % 2 == 0, 1.0, -1.0)
    fwd_im = -sin
    fwd_im[:, 0] = sign
    forward = np.concatenate([cos, fwd_im], axis=1)
    weight = np.where(freq == 0, 1.0, 2.0)[:, None] / size
    inv_re = cos.T * weight
    inv_im = -sin.T * weight
    inv_im[0, :] = sign / size
    inverse = np.concatenate([inv_re, inv_im], axis=0)
    return np.concatenate(split_bf16(forward) + split_bf16(inverse.T), axis=1)


def dot(a, b):
    return jnp.dot(a, b, preferred_element_type=F32)


def dot_nt(a, b):
    return lax.dot_general(a, b, (((1,), (1,)), ((), ())), preferred_element_type=F32)


def prep_kernel(feat_ref, filt_ref, out_ref):
    prod = feat_ref[1].astype(F32) * feat_ref[2].astype(F32)
    filt = filt_ref[...]
    for j in range(CH // 128):
        cols = slice(128 * j, 128 * j + 128)
        out_ref[4 * j : 4 * j + 4, 0:SUB, :] = prod[:, cols].T.astype(BF16).reshape(4, SUB, 128)
        out_ref[4 * j : 4 * j + 4, SUB : 2 * SUB, :] = (
            filt[:, cols].T.astype(BF16).reshape(4, SUB, 128)
        )


def conv_kernel(x_ref, tab_ref, out_ref, spec, filt, outs):
    x = x_ref[...].reshape(N_CTX * 2 * SUB, ROWS)
    spec[...] = (dot(x, tab_ref[:, 0:256]) + dot(x, tab_ref[:, 256:512])).reshape(N_CTX, 2 * SUB, 256)
    lane = lax.broadcasted_iota(jnp.int32, (SUB, 128), 1)
    sign = jnp.where(lane % 2 == 0, 1.0, -1.0).astype(F32)
    first = lane == 0
    for d in range(N_CTX):
        re = spec[d, SUB:, 0:128]
        im = spec[d, SUB:, 128:256]
        if d > 0:
            re = re + sign * spec[d - 1, SUB:, 0:128]
            im = im + sign * spec[d - 1, SUB:, 128:256]
        filt[d, 0] = re
        filt[d, 1] = jnp.where(first, 0.0, im)
        filt[d, 2] = jnp.where(first, im, re)
    for m in range(N_CTX):
        acc_re = jnp.zeros((SUB, 128), F32)
        acc_im = jnp.zeros((SUB, 128), F32)
        for n in range(m + 1):
            pr = spec[n, 0:SUB, 0:128]
            pi = spec[n, 0:SUB, 128:256]
            hr, hz, hq = filt[m - n, 0], filt[m - n, 1], filt[m - n, 2]
            acc_re = acc_re + (pr * hr - pi * hz)
            acc_im = acc_im + (pr * hz + pi * hq)
        outs[m, :, 0:128] = acc_re
        outs[m, :, 128:256] = acc_im
    total = outs[...].reshape(N_CTX * SUB, 256)
    high = total.astype(BF16)
    low = (total - high.astype(F32)).astype(BF16)
    inv_high, inv_low = tab_ref[:, 512:768], tab_ref[:, 768:1024]
    y = dot_nt(high, inv_high) + dot_nt(high, inv_low) + dot_nt(low, inv_high)
    out_ref[...] = y.astype(BF16).reshape(N_CTX, SUB, ROWS)


def mix_kernel(conv_ref, feat_ref, skip_ref, out_ref):
    conv = conv_ref[...].reshape(CH, ROWS).astype(F32)
    for j in range(CH // 128):
        cols = slice(128 * j, 128 * j + 128)
        prod = feat_ref[1, :, cols].astype(F32) * feat_ref[2, :, cols].astype(F32)
        long = conv[cols, :].T
        gate = feat_ref[0, :, cols].astype(F32)
        mixed = (gate * (long + skip_ref[:, cols] * prod)).astype(BF16)
        for copy in range(8):
            out_ref[copy, :, cols] = mixed


def out_proj_kernel(offset, core_ref, mixed_hbm, w_hbm, start_ref, *refs):
    *out_refs, mixed, w_buf, sem = refs
    first = jnp.bitwise_xor(core_ref[0], offset)
    copies = []
    for j in range(N_TP // 2):
        rows = pl.ds(pl.multiple_of((2 * j + first) * CH, CH), CH)
        copies.append(
            (
                pltpu.make_async_copy(mixed_hbm.at[j], mixed.at[j], sem.at[0, j]),
                pltpu.make_async_copy(w_hbm.at[rows], w_buf.at[j], sem.at[1, j]),
            )
        )
    for pair in copies:
        for copy in pair:
            copy.start()
    acc = start_ref[...].astype(F32)
    for j, pair in enumerate(copies):
        for copy in pair:
            copy.wait()
        acc = acc + dot(mixed[j], w_buf[j])
    for out_ref in out_refs:
        out_ref[...] = acc.astype(out_ref.dtype)


def square_sums(values):
    ones = jnp.ones((8, CH), BF16)
    sq = values * values
    high = sq.astype(BF16)
    return dot_nt(ones, high) + dot_nt(ones, (sq - high.astype(F32)).astype(BF16))


def two_rows(total):
    high = total.astype(BF16).astype(F32)
    row = lax.broadcasted_iota(jnp.int32, total.shape, 0)
    return jnp.where(row == 0, high, jnp.where(row == 1, total - high, 0.0))


def with_tail(rows, tail):
    return jnp.concatenate([rows, tail], axis=0).astype(BF16)


def load_kernel(wg_ref, wgx_ref, wu_ref, wux_ref, mark_ref, gate_ref, up_ref, out_mark_ref, sem):
    copies = []
    pieces = ((wg_ref, gate_ref, 0), (wgx_ref, gate_ref, CH), (wu_ref, up_ref, 0), (wux_ref, up_ref, CH))
    for i, (src, dst, at) in enumerate(pieces):
        copies.append(pltpu.make_async_copy(src, dst.at[:, pl.ds(at, CH)], sem.at[i]))
        copies[-1].start()
    for copy in copies:
        copy.wait()
    out_mark_ref[...] = mark_ref[...]


def hold_kernel(here_ref, stream_ref, second_ref, first_ref, out_ref):
    @pl.when(here_ref[0] == 1)
    def _():
        out_ref[0] = stream_ref[...]
        out_ref[1] = first_ref[...]

    @pl.when(here_ref[0] == 0)
    def _():
        out_ref[0] = first_ref[...]
        out_ref[1] = second_ref[...]


def scale_kernel(*refs):
    blocks, (gain_ref, gain_oth_ref, out_ref, tail_ref) = refs[:-4], refs[-4:]
    for i, block in enumerate(blocks):
        own = block[0].astype(F32)
        oth = block[1].astype(F32)
        out_ref[i, :, 0:CH] = (own * gain_ref[...]).astype(BF16)
        out_ref[i, :, CH:] = (oth * gain_oth_ref[...]).astype(BF16)
        tail_ref[i] = two_rows(square_sums(own) + square_sums(oth))


def mlp_kernel(slots, split, idx_ref, *refs):
    rows, (gate_ref, up_ref) = refs[:4], refs[4:6]
    out_refs, order_ref = refs[6:-3], refs[-3]
    scaled, tail = refs[-2:]
    for slot in range(8):
        order_ref[slot] = idx_ref[slot]
    for at, slot in enumerate(slots):
        which = idx_ref[slot]
        span = slice(at * ROWS, at * ROWS + ROWS)

        @pl.when(which < NEAR)
        def _():
            scaled[span, :] = rows[0][which]
            tail[at] = rows[1][which]

        @pl.when(which >= NEAR)
        def _():
            scaled[span, :] = rows[2][which - NEAR]
            tail[at] = rows[3][which - NEAR]

    zeros = jnp.zeros((FF_PAD - FF_LOC, ROWS), F32)
    gate = dot_nt(gate_ref[...], scaled[...])
    for at in range(len(slots)):
        target = out_refs[2 * at] if split else out_refs[at].at[0]
        target[...] = with_tail(gate[:, at * ROWS : at * ROWS + ROWS], zeros)
    up = dot_nt(up_ref[...], scaled[...])
    for at in range(len(slots)):
        target = out_refs[2 * at + 1] if split else out_refs[at].at[1]
        target[...] = with_tail(up[:, at * ROWS : at * ROWS + ROWS], tail[at])


def sum_kernel(*refs):
    total = refs[0][...].astype(F32)
    for ref in refs[1:-1]:
        total = total + ref[...].astype(F32)
    refs[-1][...] = total.astype(BF16)


def sum_apart_kernel(left_ref, right_ref, gate_ref, up_ref):
    for i, out_ref in enumerate((gate_ref, up_ref)):
        out_ref[...] = (left_ref[i].astype(F32) + right_ref[i].astype(F32)).astype(BF16)


def finish_kernel(own_ref, across_ref, gate_1_ref, gate_3_ref, up_1_ref, up_3_ref, out_ref):
    gate = own_ref[0].astype(F32) + across_ref[0].astype(F32)
    gate = gate + (gate_1_ref[...].astype(F32) + gate_3_ref[...].astype(F32))
    up = own_ref[1].astype(F32) + across_ref[1].astype(F32)
    up = up + (up_1_ref[...].astype(F32) + up_3_ref[...].astype(F32))
    sums = up[FF_LOC : FF_LOC + 1] + up[FF_LOC + 1 : FF_LOC + 2]
    scale = lax.rsqrt(sums * (1.0 / (N_TP * CH)) + EPS)
    gate = gate[:FF_LOC] * scale
    out_ref[...] = (gate / (1.0 + jnp.exp(-gate)) * (up[:FF_LOC] * scale)).astype(BF16)


def params(mib):
    return pltpu.CompilerParams(vmem_limit_bytes=mib * 1024 * 1024)


def pairs_of(rule):
    pairs = []
    for i in range(N_CTX * N_TP):
        target = rule(*split_index(i))
        if target is not None:
            pairs.append((i, join_index(*target)))
    return pairs


def to_row_owner_first(z, x, y, k):
    return (z, x ^ 1, y, k) if k == x % 2 else (z, x, y, k ^ 1)


def to_row_owner_second(z, x, y, k):
    return None if k == x % 2 else (z, x ^ 1, y, k ^ 1)


def in_smem():
    return pl.BlockSpec(memory_space=pltpu.SMEM)


def anywhere():
    return pl.BlockSpec(memory_space=pl.ANY)


def along(steps, z, x, y, k):
    return (z + steps, x, y, k) if z % 2 == 0 else (z - steps, x, y, k)


def out_proj(offset, core, mixed, w_out, start, dtype, copies):
    return pl.pallas_call(
        functools.partial(out_proj_kernel, offset),
        out_shape=[jax.ShapeDtypeStruct((ROWS, CH), dtype)] * copies,
        in_specs=[
            in_smem(),
            anywhere(),
            pl.BlockSpec(memory_space=pltpu.HBM),
            pl.BlockSpec(memory_space=pltpu.VMEM),
        ],
        scratch_shapes=[
            pltpu.VMEM((N_TP // 2, ROWS, CH), BF16),
            pltpu.VMEM((N_TP // 2, CH, CH), BF16),
            pltpu.SemaphoreType.DMA((2, N_TP // 2)),
        ],
        compiler_params=params(53),
        cost_estimate=pl.CostEstimate(
            flops=2 * ROWS * CH * N_TP // 2 * CH, bytes_accessed=5 << 20, transcendentals=0
        ),
        name="out_proj",
    )(core, mixed, w_out, start)


def hold(here, *parts):
    vmem = pl.BlockSpec(memory_space=pltpu.VMEM)
    return pl.pallas_call(
        hold_kernel,
        out_shape=jax.ShapeDtypeStruct((2, ROWS, CH), BF16),
        in_specs=[in_smem()] + [vmem] * 3,
        out_specs=vmem,
        compiler_params=params(14),
        cost_estimate=pl.CostEstimate(flops=1, bytes_accessed=1 << 19, transcendentals=0),
        name="hold",
    )(here, *parts)


def load_weights(weights, mark):
    vmem = pl.BlockSpec(memory_space=pltpu.VMEM)
    return pl.pallas_call(
        load_kernel,
        out_shape=[jax.ShapeDtypeStruct((FF_LOC, 2 * CH), BF16)] * 2
        + [jax.ShapeDtypeStruct(mark.shape, mark.dtype)],
        in_specs=[anywhere()] * 4 + [vmem],
        out_specs=[vmem] * 3,
        scratch_shapes=[pltpu.SemaphoreType.DMA((4,))],
        compiler_params=params(16),
        cost_estimate=pl.CostEstimate(flops=1, bytes_accessed=12 << 20, transcendentals=0),
        name="load",
    )(*weights, mark)


def scale(blocks, gains):
    n = len(blocks)
    return pl.pallas_call(
        scale_kernel,
        out_shape=[
            jax.ShapeDtypeStruct((n, ROWS, 2 * CH), BF16),
            jax.ShapeDtypeStruct((n, 8, ROWS), F32),
        ],
        compiler_params=params(14),
        cost_estimate=pl.CostEstimate(
            flops=8 * n * ROWS * CH * 8, bytes_accessed=n << 19, transcendentals=0
        ),
        name="scale",
    )(*blocks, *gains)


def mlp_part(slots, idx, rows, weights, split=False):
    n = len(slots)
    shapes = [(FF_PAD, ROWS)] * (2 * n) if split else [(2, FF_PAD, ROWS)] * n
    vmem = pl.BlockSpec(memory_space=pltpu.VMEM)
    *outs, token = pl.pallas_call(
        functools.partial(mlp_kernel, slots, split),
        out_shape=[jax.ShapeDtypeStruct(shape, BF16) for shape in shapes]
        + [jax.ShapeDtypeStruct((8,), jnp.int32)],
        in_specs=[in_smem()] + [vmem] * 6,
        out_specs=[vmem] * len(shapes) + [in_smem()],
        scratch_shapes=[
            pltpu.VMEM((n * ROWS, 2 * CH), BF16),
            pltpu.VMEM((n, 8, ROWS), F32),
        ],
        compiler_params=params(18),
        cost_estimate=pl.CostEstimate(
            flops=10**8, bytes_accessed=1 << 19, transcendentals=0
        ),
        name="mlp",
    )(idx, *rows, *weights)
    return outs, token


def in_vmem_call(kernel, shapes, name, parts):
    vmem = pl.BlockSpec(memory_space=pltpu.VMEM)
    return pl.pallas_call(
        kernel,
        out_shape=[jax.ShapeDtypeStruct(shape, BF16) for shape in shapes],
        in_specs=[vmem] * len(parts),
        out_specs=[vmem] * len(shapes),
        compiler_params=params(16),
        cost_estimate=pl.CostEstimate(flops=1, bytes_accessed=1 << 19, transcendentals=0),
        name=name,
    )(*parts)


def shards(residual, features, filters, skip_gain, w_out, norm_gain, w_gate, w_up):
    ctx = lax.axis_index("ctx")
    tp = lax.axis_index("tp")
    core, x_lo = tp % 2, ctx % 2
    x_hi, y = tp // 8, (tp // 2) % 4
    feat = features.transpose(1, 0, 2)
    wg, wu = w_gate.T, w_up.T
    gain = norm_gain[None, :]
    wg_oth, wu_oth, gain_oth = shift(wg, k=1), shift(wu, k=1), shift(gain, k=1)

    sent = pl.pallas_call(
        prep_kernel,
        out_shape=jax.ShapeDtypeStruct((N_CTX, 2 * SUB, ROWS), BF16),
        compiler_params=params(56),
        name="prep",
    )(feat, filters)
    recv = lax.all_to_all(sent, "ctx", 0, 0, tiled=True)
    recv, gain_oth = lax.optimization_barrier((recv, gain_oth))
    conv = pl.pallas_call(
        conv_kernel,
        out_shape=jax.ShapeDtypeStruct((N_CTX, SUB, ROWS), BF16),
        scratch_shapes=[
            pltpu.VMEM((N_CTX, 2 * SUB, 256), F32),
            pltpu.VMEM((N_CTX, 3, SUB, 128), F32),
            pltpu.VMEM((N_CTX, SUB, 256), F32),
        ],
        compiler_params=params(14),
        name="conv",
    )(recv, jnp.asarray(dft_tables()))
    conv_rows = lax.all_to_all(conv, "ctx", 0, 0, tiled=True)
    copies = pl.pallas_call(
        mix_kernel,
        out_shape=jax.ShapeDtypeStruct((8, ROWS, CH), BF16),
        compiler_params=params(56),
        name="mix",
    )(conv_rows, feat, skip_gain[None, :])

    mixed = lax.all_to_all(
        copies, "tp", 0, 0, axis_index_groups=PLANE_GROUPS, tiled=True
    )
    mixed_oth = shift(mixed, k=1)
    core_arr = core.astype(jnp.int32)[None]
    (half,) = out_proj(0, core_arr, mixed, w_out, residual, F32, 1)
    stream_out, stream = out_proj(1, core_arr, mixed_oth, w_out, half, BF16, 2)

    stream, wg_oth, wu_oth = lax.optimization_barrier((stream, wg_oth, wu_oth))
    first = lax.ppermute(stream, AXES, pairs_of(to_row_owner_first))
    second = lax.ppermute(stream, AXES, pairs_of(to_row_owner_second))
    here = (x_lo == core).astype(jnp.int32)[None]
    held = hold(here, stream, second, first)
    gate_w, up_w, mark = load_weights((wg, wg_oth, wu, wu_oth), held[0, :16])
    gain, _ = lax.optimization_barrier((gain, mark))
    z = ctx // 2
    side = jnp.where(z % 2 == 0, -1, 1)
    two_first = lax.ppermute(held, AXES, pairs_of(functools.partial(along, 2)))
    two_second = lax.ppermute(held, AXES, pairs_of(functools.partial(along, -2)))
    one_first = lax.ppermute(held, AXES, pairs_of(functools.partial(along, 1)))
    one_second = lax.ppermute(held, AXES, pairs_of(functools.partial(along, -1)))
    three_first = lax.ppermute(two_first, AXES, pairs_of(functools.partial(along, 1)))
    three_second = lax.ppermute(two_second, AXES, pairs_of(functools.partial(along, -1)))
    opposite = lax.ppermute(two_first, AXES, pairs_of(functools.partial(along, 2)))
    gains = (gain, gain_oth)
    rows = scale([held, one_first, one_second, two_first, two_second], gains)
    rows = rows + scale([three_first, three_second, opposite], gains)

    order = []
    for b in range(4):
        for a in range(2):
            d = (side * (4 * ((x_hi + a) % 2) + (y + b) % 4 - z)) % 8
            order.append(d)
    seen = jnp.stack(order)
    idx = sum(jnp.where(seen == d, at, 0) for d, at in enumerate(ROW_OF)).astype(jnp.int32)

    weights = (gate_w, up_w)
    both, half = (2, FF_PAD, ROWS), (FF_PAD, ROWS)
    (two_far,), then = mlp_part((5,), idx, rows, weights)
    (one_far, three_far), then = mlp_part((3, 7), then, rows, weights)
    near, then = mlp_part((2, 6), then, rows, weights, split=True)
    (two_near, own_far), then = mlp_part((4, 1), then, rows, weights)
    (own_near,), _ = mlp_part((0,), then, rows, weights)
    two_far = shift(two_far, x=2)
    one_far = shift(one_far, y=1)
    three_far = shift(three_far, y=-1)
    up_1 = shift(near[1], y=1)
    gate_3 = shift(near[2], y=-1)
    gate_by, up_by = in_vmem_call(sum_apart_kernel, (half, half), "sum", (two_near, two_far))
    (across,) = in_vmem_call(sum_kernel, (both,), "sum", (own_far, one_far, three_far))
    gate_by = shift(gate_by, y=1)
    up_by = shift(up_by, y=-1)
    across = shift(across, x=2)
    (gate_1,) = in_vmem_call(sum_kernel, (half,), "sum", (near[0], gate_by))
    (up_3,) = in_vmem_call(sum_kernel, (half,), "sum", (near[3], up_by))
    gate_1 = shift(gate_1, y=1)
    up_3 = shift(up_3, y=-1)
    (hidden_t,) = in_vmem_call(
        finish_kernel,
        ((FF_LOC, ROWS),),
        "finish",
        (own_near, across, gate_1, gate_3, up_1, up_3),
    )
    return stream_out, hidden_t.T


def solution(mesh):
    placed = (
        P("ctx", "tp"),
        P("ctx", None, "tp"),
        P("ctx", "tp"),
        P("tp"),
        P(None, "tp"),
        P("tp"),
        P("tp", "ctx"),
        P("tp", "ctx"),
    )
    return jax.shard_map(
        shards,
        mesh=mesh,
        in_specs=placed,
        out_specs=(P("ctx", "tp"), P("tp", "ctx")),
        check_vma=False,
    )
```

```python
import functools
import math

import jax
import jax.numpy as jnp
import numpy as np
from jax import lax
from jax.experimental import pallas as pl
from jax.experimental.pallas import tpu as pltpu
from jax.sharding import PartitionSpec as P

F32 = jnp.float32
BF16 = jnp.bfloat16
AXES = ("ctx", "tp")
N_CTX = 16
N_TP = 16
ROWS = 128
CH = 512
SUB = 32
FF_LOC = 1368
FF_PAD = 1376
EPS = 1e-06
NEAR = 5
ROW_OF = (0, 2, 3, 6, 7, 5, 4, 1)
PLANE_GROUPS = [[xh * 8 + y * 2 + k for xh in range(2) for y in range(4)] for k in range(2)]


def split_index(i):
    c, t = divmod(i, N_TP)
    z, x_lo = divmod(c, 2)
    x_hi, r = divmod(t, 8)
    y, k = divmod(r, 2)
    return z, x_hi * 2 + x_lo, y, k


def join_index(z, x, y, k):
    x = x % 4
    return ((z % 8) * 2 + x % 2) * N_TP + (x // 2) * 8 + (y % 4) * 2 + k % 2


def shift(arr, z=0, x=0, y=0, k=0):
    pairs = []
    for i in range(N_CTX * N_TP):
        az, ax, ay, ak = split_index(i)
        pairs.append((i, join_index(az + z, ax + x, ay + y, ak + k)))
    return lax.ppermute(arr, AXES, pairs)


def split_bf16(table):
    high = np.asarray(table, np.float32).astype(jnp.bfloat16)
    low = (np.asarray(table, np.float32) - high.astype(np.float32)).astype(jnp.bfloat16)
    return high, low


def dft_tables():
    size = 2 * ROWS
    pos = np.arange(ROWS)
    freq = np.arange(ROWS)
    phase = (pos[:, None] * freq[None, :]) % size
    angle = 2.0 * math.pi / size * phase
    cos, sin = np.cos(angle), np.sin(angle)
    sign = np.where(pos % 2 == 0, 1.0, -1.0)
    fwd_im = -sin
    fwd_im[:, 0] = sign
    forward = np.concatenate([cos, fwd_im], axis=1)
    weight = np.where(freq == 0, 1.0, 2.0)[:, None] / size
    inv_re = cos.T * weight
    inv_im = -sin.T * weight
    inv_im[0, :] = sign / size
    inverse = np.concatenate([inv_re, inv_im], axis=0)
    return np.concatenate(split_bf16(forward) + split_bf16(inverse.T), axis=1)


def dot(a, b):
    return jnp.dot(a, b, preferred_element_type=F32)


def dot_nt(a, b):
    return lax.dot_general(a, b, (((1,), (1,)), ((), ())), preferred_element_type=F32)


def prep_kernel(feat_ref, filt_ref, out_ref):
    prod = feat_ref[1].astype(F32) * feat_ref[2].astype(F32)
    filt = filt_ref[...]
    for j in range(CH // 128):
        cols = slice(128 * j, 128 * j + 128)
        out_ref[4 * j : 4 * j + 4, 0:SUB, :] = prod[:, cols].T.astype(BF16).reshape(4, SUB, 128)
        out_ref[4 * j : 4 * j + 4, SUB : 2 * SUB, :] = (
            filt[:, cols].T.astype(BF16).reshape(4, SUB, 128)
        )


def conv_kernel(x_ref, tab_ref, out_ref, spec, filt, outs):
    x = x_ref[...].reshape(N_CTX * 2 * SUB, ROWS)
    spec[...] = (dot(x, tab_ref[:, 0:256]) + dot(x, tab_ref[:, 256:512])).reshape(N_CTX, 2 * SUB, 256)
    lane = lax.broadcasted_iota(jnp.int32, (SUB, 128), 1)
    sign = jnp.where(lane % 2 == 0, 1.0, -1.0).astype(F32)
    first = lane == 0
    for d in range(N_CTX):
        re = spec[d, SUB:, 0:128]
        im = spec[d, SUB:, 128:256]
        if d > 0:
            re = re + sign * spec[d - 1, SUB:, 0:128]
            im = im + sign * spec[d - 1, SUB:, 128:256]
        filt[d, 0] = re
        filt[d, 1] = jnp.where(first, 0.0, im)
        filt[d, 2] = jnp.where(first, im, re)
    for m in range(N_CTX):
        acc_re = jnp.zeros((SUB, 128), F32)
        acc_im = jnp.zeros((SUB, 128), F32)
        for n in range(m + 1):
            pr = spec[n, 0:SUB, 0:128]
            pi = spec[n, 0:SUB, 128:256]
            hr, hz, hq = filt[m - n, 0], filt[m - n, 1], filt[m - n, 2]
            acc_re = acc_re + (pr * hr - pi * hz)
            acc_im = acc_im + (pr * hz + pi * hq)
        outs[m, :, 0:128] = acc_re
        outs[m, :, 128:256] = acc_im
    total = outs[...].reshape(N_CTX * SUB, 256)
    high = total.astype(BF16)
    low = (total - high.astype(F32)).astype(BF16)
    inv_high, inv_low = tab_ref[:, 512:768], tab_ref[:, 768:1024]
    y = dot_nt(high, inv_high) + dot_nt(high, inv_low) + dot_nt(low, inv_high)
    out_ref[...] = y.astype(BF16).reshape(N_CTX, SUB, ROWS)


def mix_kernel(conv_ref, feat_ref, skip_ref, out_ref):
    conv = conv_ref[...].reshape(CH, ROWS).astype(F32)
    for j in range(CH // 128):
        cols = slice(128 * j, 128 * j + 128)
        prod = feat_ref[1, :, cols].astype(F32) * feat_ref[2, :, cols].astype(F32)
        long = conv[cols, :].T
        gate = feat_ref[0, :, cols].astype(F32)
        mixed = (gate * (long + skip_ref[:, cols] * prod)).astype(BF16)
        for copy in range(8):
            out_ref[copy, :, cols] = mixed


def out_proj_kernel(offset, core_ref, mixed_hbm, w_hbm, start_ref, *refs):
    *out_refs, mixed, w_buf, sem = refs
    first = jnp.bitwise_xor(core_ref[0], offset)
    copies = []
    for j in range(N_TP // 2):
        rows = pl.ds(pl.multiple_of((2 * j + first) * CH, CH), CH)
        copies.append(
            (
                pltpu.make_async_copy(mixed_hbm.at[j], mixed.at[j], sem.at[0, j]),
                pltpu.make_async_copy(w_hbm.at[rows], w_buf.at[j], sem.at[1, j]),
            )
        )
    for pair in copies:
        for copy in pair:
            copy.start()
    acc = start_ref[...].astype(F32)
    for j, pair in enumerate(copies):
        for copy in pair:
            copy.wait()
        acc = acc + dot(mixed[j], w_buf[j])
    for out_ref in out_refs:
        out_ref[...] = acc.astype(out_ref.dtype)


def square_sums(values):
    ones = jnp.ones((8, CH), BF16)
    sq = values * values
    high = sq.astype(BF16)
    return dot_nt(ones, high) + dot_nt(ones, (sq - high.astype(F32)).astype(BF16))


def two_rows(total):
    high = total.astype(BF16).astype(F32)
    row = lax.broadcasted_iota(jnp.int32, total.shape, 0)
    return jnp.where(row == 0, high, jnp.where(row == 1, total - high, 0.0))


def with_tail(rows, tail):
    return jnp.concatenate([rows, tail], axis=0).astype(BF16)


def load_kernel(wg_ref, wgx_ref, wu_ref, wux_ref, mark_ref, gate_ref, up_ref, out_mark_ref, sem):
    copies = []
    pieces = ((wg_ref, gate_ref, 0), (wgx_ref, gate_ref, CH), (wu_ref, up_ref, 0), (wux_ref, up_ref, CH))
    for i, (src, dst, at) in enumerate(pieces):
        copies.append(pltpu.make_async_copy(src, dst.at[:, pl.ds(at, CH)], sem.at[i]))
        copies[-1].start()
    for copy in copies:
        copy.wait()
    out_mark_ref[...] = mark_ref[...]


def hold_kernel(here_ref, stream_ref, second_ref, first_ref, out_ref):
    @pl.when(here_ref[0] == 1)
    def _():
        out_ref[0] = stream_ref[...]
        out_ref[1] = first_ref[...]

    @pl.when(here_ref[0] == 0)
    def _():
        out_ref[0] = first_ref[...]
        out_ref[1] = second_ref[...]


def scale_kernel(*refs):
    blocks, (gain_ref, gain_oth_ref, out_ref, tail_ref) = refs[:-4], refs[-4:]
    for i, block in enumerate(blocks):
        own = block[0].astype(F32)
        oth = block[1].astype(F32)
        out_ref[i, :, 0:CH] = (own * gain_ref[...]).astype(BF16)
        out_ref[i, :, CH:] = (oth * gain_oth_ref[...]).astype(BF16)
        tail_ref[i] = two_rows(square_sums(own) + square_sums(oth))


def mlp_kernel(slots, split, idx_ref, *refs):
    rows, (gate_ref, up_ref) = refs[:4], refs[4:6]
    out_refs, order_ref = refs[6:-3], refs[-3]
    scaled, tail = refs[-2:]
    for slot in range(8):
        order_ref[slot] = idx_ref[slot]
    for at, slot in enumerate(slots):
        which = idx_ref[slot]
        span = slice(at * ROWS, at * ROWS + ROWS)

        @pl.when(which < NEAR)
        def _():
            scaled[span, :] = rows[0][which]
            tail[at] = rows[1][which]

        @pl.when(which >= NEAR)
        def _():
            scaled[span, :] = rows[2][which - NEAR]
            tail[at] = rows[3][which - NEAR]

    zeros = jnp.zeros((FF_PAD - FF_LOC, ROWS), F32)
    gate = dot_nt(gate_ref[...], scaled[...])
    for at in range(len(slots)):
        target = out_refs[2 * at] if split else out_refs[at].at[0]
        target[...] = with_tail(gate[:, at * ROWS : at * ROWS + ROWS], zeros)
    up = dot_nt(up_ref[...], scaled[...])
    for at in range(len(slots)):
        target = out_refs[2 * at + 1] if split else out_refs[at].at[1]
        target[...] = with_tail(up[:, at * ROWS : at * ROWS + ROWS], tail[at])


def sum_kernel(*refs):
    total = refs[0][...].astype(F32)
    for ref in refs[1:-1]:
        total = total + ref[...].astype(F32)
    refs[-1][...] = total.astype(BF16)


def sum_apart_kernel(left_ref, right_ref, gate_ref, up_ref):
    for i, out_ref in enumerate((gate_ref, up_ref)):
        out_ref[...] = (left_ref[i].astype(F32) + right_ref[i].astype(F32)).astype(BF16)


def finish_kernel(own_ref, across_ref, gate_1_ref, gate_3_ref, up_1_ref, up_3_ref, out_ref):
    gate = own_ref[0].astype(F32) + across_ref[0].astype(F32)
    gate = gate + (gate_1_ref[...].astype(F32) + gate_3_ref[...].astype(F32))
    up = own_ref[1].astype(F32) + across_ref[1].astype(F32)
    up = up + (up_1_ref[...].astype(F32) + up_3_ref[...].astype(F32))
    sums = up[FF_LOC : FF_LOC + 1] + up[FF_LOC + 1 : FF_LOC + 2]
    scale = lax.rsqrt(sums * (1.0 / (N_TP * CH)) + EPS)
    gate = gate[:FF_LOC] * scale
    out_ref[...] = (gate / (1.0 + jnp.exp(-gate)) * (up[:FF_LOC] * scale)).astype(BF16)


def params(mib):
    return pltpu.CompilerParams(vmem_limit_bytes=mib * 1024 * 1024)


def pairs_of(rule):
    pairs = []
    for i in range(N_CTX * N_TP):
        target = rule(*split_index(i))
        if target is not None:
            pairs.append((i, join_index(*target)))
    return pairs


def to_row_owner_first(z, x, y, k):
    return (z, x ^ 1, y, k) if k == x % 2 else (z, x, y, k ^ 1)


def to_row_owner_second(z, x, y, k):
    return None if k == x % 2 else (z, x ^ 1, y, k ^ 1)


def in_smem():
    return pl.BlockSpec(memory_space=pltpu.SMEM)


def anywhere():
    return pl.BlockSpec(memory_space=pl.ANY)


def along(steps, z, x, y, k):
    return (z + steps, x, y, k) if z % 2 == 0 else (z - steps, x, y, k)


def out_proj(offset, core, mixed, w_out, start, dtype, copies):
    return pl.pallas_call(
        functools.partial(out_proj_kernel, offset),
        out_shape=[jax.ShapeDtypeStruct((ROWS, CH), dtype)] * copies,
        in_specs=[
            in_smem(),
            anywhere(),
            pl.BlockSpec(memory_space=pltpu.HBM),
            pl.BlockSpec(memory_space=pltpu.VMEM),
        ],
        scratch_shapes=[
            pltpu.VMEM((N_TP // 2, ROWS, CH), BF16),
            pltpu.VMEM((N_TP // 2, CH, CH), BF16),
            pltpu.SemaphoreType.DMA((2, N_TP // 2)),
        ],
        compiler_params=params(53),
        cost_estimate=pl.CostEstimate(
            flops=2 * ROWS * CH * N_TP // 2 * CH, bytes_accessed=5 << 20, transcendentals=0
        ),
        name="out_proj",
    )(core, mixed, w_out, start)


def hold(here, *parts):
    vmem = pl.BlockSpec(memory_space=pltpu.VMEM)
    return pl.pallas_call(
        hold_kernel,
        out_shape=jax.ShapeDtypeStruct((2, ROWS, CH), BF16),
        in_specs=[in_smem()] + [vmem] * 3,
        out_specs=vmem,
        compiler_params=params(14),
        cost_estimate=pl.CostEstimate(flops=1, bytes_accessed=1 << 19, transcendentals=0),
        name="hold",
    )(here, *parts)


def load_weights(weights, mark):
    vmem = pl.BlockSpec(memory_space=pltpu.VMEM)
    return pl.pallas_call(
        load_kernel,
        out_shape=[jax.ShapeDtypeStruct((FF_LOC, 2 * CH), BF16)] * 2
        + [jax.ShapeDtypeStruct(mark.shape, mark.dtype)],
        in_specs=[anywhere()] * 4 + [vmem],
        out_specs=[vmem] * 3,
        scratch_shapes=[pltpu.SemaphoreType.DMA((4,))],
        compiler_params=params(16),
        cost_estimate=pl.CostEstimate(flops=1, bytes_accessed=12 << 20, transcendentals=0),
        name="load",
    )(*weights, mark)


def scale(blocks, gains):
    n = len(blocks)
    return pl.pallas_call(
        scale_kernel,
        out_shape=[
            jax.ShapeDtypeStruct((n, ROWS, 2 * CH), BF16),
            jax.ShapeDtypeStruct((n, 8, ROWS), F32),
        ],
        compiler_params=params(14),
        cost_estimate=pl.CostEstimate(
            flops=8 * n * ROWS * CH * 8, bytes_accessed=n << 19, transcendentals=0
        ),
        name="scale",
    )(*blocks, *gains)


def mlp_part(slots, idx, rows, weights, split=False):
    n = len(slots)
    shapes = [(FF_PAD, ROWS)] * (2 * n) if split else [(2, FF_PAD, ROWS)] * n
    vmem = pl.BlockSpec(memory_space=pltpu.VMEM)
    *outs, token = pl.pallas_call(
        functools.partial(mlp_kernel, slots, split),
        out_shape=[jax.ShapeDtypeStruct(shape, BF16) for shape in shapes]
        + [jax.ShapeDtypeStruct((8,), jnp.int32)],
        in_specs=[in_smem()] + [vmem] * 6,
        out_specs=[vmem] * len(shapes) + [in_smem()],
        scratch_shapes=[
            pltpu.VMEM((n * ROWS, 2 * CH), BF16),
            pltpu.VMEM((n, 8, ROWS), F32),
        ],
        compiler_params=params(18),
        cost_estimate=pl.CostEstimate(
            flops=10**8, bytes_accessed=1 << 19, transcendentals=0
        ),
        name="mlp",
    )(idx, *rows, *weights)
    return outs, token


def in_vmem_call(kernel, shapes, name, parts):
    vmem = pl.BlockSpec(memory_space=pltpu.VMEM)
    return pl.pallas_call(
        kernel,
        out_shape=[jax.ShapeDtypeStruct(shape, BF16) for shape in shapes],
        in_specs=[vmem] * len(parts),
        out_specs=[vmem] * len(shapes),
        compiler_params=params(16),
        cost_estimate=pl.CostEstimate(flops=1, bytes_accessed=1 << 19, transcendentals=0),
        name=name,
    )(*parts)


def shards(residual, features, filters, skip_gain, w_out, norm_gain, w_gate, w_up):
    ctx = lax.axis_index("ctx")
    tp = lax.axis_index("tp")
    core, x_lo = tp % 2, ctx % 2
    x_hi, y = tp // 8, (tp // 2) % 4
    feat = features.transpose(1, 0, 2)
    wg, wu = w_gate.T, w_up.T
    gain = norm_gain[None, :]
    wg_oth, wu_oth, gain_oth = shift(wg, k=1), shift(wu, k=1), shift(gain, k=1)

    sent = pl.pallas_call(
        prep_kernel,
        out_shape=jax.ShapeDtypeStruct((N_CTX, 2 * SUB, ROWS), BF16),
        compiler_params=params(56),
        name="prep",
    )(feat, filters)
    recv = lax.all_to_all(sent, "ctx", 0, 0, tiled=True)
    recv, gain_oth = lax.optimization_barrier((recv, gain_oth))
    conv = pl.pallas_call(
        conv_kernel,
        out_shape=jax.ShapeDtypeStruct((N_CTX, SUB, ROWS), BF16),
        scratch_shapes=[
            pltpu.VMEM((N_CTX, 2 * SUB, 256), F32),
            pltpu.VMEM((N_CTX, 3, SUB, 128), F32),
            pltpu.VMEM((N_CTX, SUB, 256), F32),
        ],
        compiler_params=params(14),
        name="conv",
    )(recv, jnp.asarray(dft_tables()))
    conv_rows = lax.all_to_all(conv, "ctx", 0, 0, tiled=True)
    copies = pl.pallas_call(
        mix_kernel,
        out_shape=jax.ShapeDtypeStruct((8, ROWS, CH), BF16),
        compiler_params=params(56),
        name="mix",
    )(conv_rows, feat, skip_gain[None, :])

    mixed = lax.all_to_all(
        copies, "tp", 0, 0, axis_index_groups=PLANE_GROUPS, tiled=True
    )
    mixed_oth = shift(mixed, k=1)
    core_arr = core.astype(jnp.int32)[None]
    (half,) = out_proj(0, core_arr, mixed, w_out, residual, F32, 1)
    stream_out, stream = out_proj(1, core_arr, mixed_oth, w_out, half, BF16, 2)

    stream, wg_oth, wu_oth = lax.optimization_barrier((stream, wg_oth, wu_oth))
    first = lax.ppermute(stream, AXES, pairs_of(to_row_owner_first))
    second = lax.ppermute(stream, AXES, pairs_of(to_row_owner_second))
    here = (x_lo == core).astype(jnp.int32)[None]
    held = hold(here, stream, second, first)
    gate_w, up_w, mark = load_weights((wg, wg_oth, wu, wu_oth), held[0, :16])
    gain, _ = lax.optimization_barrier((gain, mark))
    z = ctx // 2
    side = jnp.where(z % 2 == 0, -1, 1)
    two_first = lax.ppermute(held, AXES, pairs_of(functools.partial(along, 2)))
    two_second = lax.ppermute(held, AXES, pairs_of(functools.partial(along, -2)))
    one_first = lax.ppermute(held, AXES, pairs_of(functools.partial(along, 1)))
    one_second = lax.ppermute(held, AXES, pairs_of(functools.partial(along, -1)))
    three_first = lax.ppermute(two_first, AXES, pairs_of(functools.partial(along, 1)))
    three_second = lax.ppermute(two_second, AXES, pairs_of(functools.partial(along, -1)))
    opposite = lax.ppermute(two_first, AXES, pairs_of(functools.partial(along, 2)))
    gains = (gain, gain_oth)
    rows = scale([held, one_first, one_second, two_first, two_second], gains)
    rows = rows + scale([three_first, three_second, opposite], gains)

    order = []
    for b in range(4):
        for a in range(2):
            d = (side * (4 * ((x_hi + a) % 2) + (y + b) % 4 - z)) % 8
            order.append(d)
    seen = jnp.stack(order)
    idx = sum(jnp.where(seen == d, at, 0) for d, at in enumerate(ROW_OF)).astype(jnp.int32)

    weights = (gate_w, up_w)
    both, half = (2, FF_PAD, ROWS), (FF_PAD, ROWS)
    (two_far, one_far, three_far), then = mlp_part((5, 3, 7), idx, rows, weights)
    near, then = mlp_part((2, 6), then, rows, weights, split=True)
    (two_near, own_far), then = mlp_part((4, 1), then, rows, weights)
    (own_near,), _ = mlp_part((0,), then, rows, weights)
    two_far = shift(two_far, x=2)
    one_far = shift(one_far, y=1)
    three_far = shift(three_far, y=-1)
    up_1 = shift(near[1], y=1)
    gate_3 = shift(near[2], y=-1)
    gate_by, up_by = in_vmem_call(sum_apart_kernel, (half, half), "sum", (two_near, two_far))
    (across,) = in_vmem_call(sum_kernel, (both,), "sum", (own_far, one_far, three_far))
    gate_by = shift(gate_by, y=1)
    up_by = shift(up_by, y=-1)
    across = shift(across, x=2)
    (gate_1,) = in_vmem_call(sum_kernel, (half,), "sum", (near[0], gate_by))
    (up_3,) = in_vmem_call(sum_kernel, (half,), "sum", (near[3], up_by))
    gate_1 = shift(gate_1, y=1)
    up_3 = shift(up_3, y=-1)
    (hidden_t,) = in_vmem_call(
        finish_kernel,
        ((FF_LOC, ROWS),),
        "finish",
        (own_near, across, gate_1, gate_3, up_1, up_3),
    )
    return stream_out, hidden_t.T


def solution(mesh):
    placed = (
        P("ctx", "tp"),
        P("ctx", None, "tp"),
        P("ctx", "tp"),
        P("tp"),
        P(None, "tp"),
        P("tp"),
        P("tp", "ctx"),
        P("tp", "ctx"),
    )
    return jax.shard_map(
        shards,
        mesh=mesh,
        in_specs=placed,
        out_specs=(P("ctx", "tp"), P("tp", "ctx")),
        check_vma=False,
    )
```
